32 devices in a mesh: view: 16 (over z, y, core), chord: 2 (over x).
Axes of the slice: x: 2, y: 2, z: 4, core: 2. Of those that a mesh axis runs over, the one named last changes fastest.
Arguments:
- proj: bfloat16 [192, 256, 128], P('view', 'chord'), may hold values from -6 to 6
- tiles: bfloat16 [96, 256, 1024], P('view'), may hold values from -0.0390625 to 0.0390625
- owner: int32 [2, 128], replicated, may hold values from 0 to 127, as said below
- lengths: int32 [2, 128], replicated, may hold values from 1 to 1024, as said below
Outputs:
- recon: float32 [2, 128, 1024], P('chord', 'view')
The draws below stay inside these ranges and needn't reach their ends.
Inputs may be any that keep to these rules, and one draw needn't show every extreme that they name: `owner`: each row is an ordering of the 128 chords of one group. In each group, the lengths of the chords at owner positions k * 8 to k * 8 + 7 sum to at most 4608, exactly 4608 for some k; the largest entry of each row is 1024.
All inputs are finite; a program needn't handle non-finite values.
Results may differ from the reference program's by a relative error of at most 0.0003.
Values sent between devices are 32-bit elements; how exact they have to be, the bound alone decides.
No kernel may reach another device: no remote copies, remote signals or barrier semaphores. Data moves between devices by JAX's collectives and lax.ppermute only.
A program may use at most 64 MiB of HBM per device.

```python
import math
import jax
import jax.numpy as jnp
from jax import lax

S = 1024
DW = 128
VB = 2
CHD = 8
PACK = 4608
VIEWS = 192
CH_GRP = 128
GROUPS = 2
CHORDS = 256


def chord_layout(key):
    base = jax.random.fold_in(key, 11)
    perm_keys = jax.random.split(jax.random.fold_in(base, 1), GROUPS)
    owner = jax.vmap(lambda k: jax.random.permutation(k, CH_GRP))(perm_keys).astype(jnp.int32)
    first = jax.random.randint(jax.random.fold_in(base, 2), (GROUPS, CH_GRP), 0, S, dtype=jnp.int32)
    second = jax.random.randint(jax.random.fold_in(base, 3), (GROUPS, CH_GRP), 0, S, dtype=jnp.int32)
    raw = 1 + first * second // S
    owners = CH_GRP // CHD
    blocks = raw.reshape(GROUPS, owners, CHD)
    total = jnp.sum(blocks, axis=2, keepdims=True)
    room = PACK - CHD
    scaled = 1 + (blocks - 1) * room // jnp.maximum(total - CHD, room)
    pick = jax.random.randint(jax.random.fold_in(base, 4), (GROUPS, 1, 1), 0, owners, dtype=jnp.int32)
    full = jnp.where(jnp.arange(CHD, dtype=jnp.int32) == 0, S, S // 2).astype(jnp.int32)[None, None, :]
    chosen = jnp.arange(owners, dtype=jnp.int32)[None, :, None] == pick
    ordered = jnp.where(chosen, full, scaled).astype(jnp.int32).reshape(GROUPS, CH_GRP)
    rows = jnp.arange(GROUPS, dtype=jnp.int32)[:, None]
    lengths = jnp.zeros((GROUPS, CH_GRP), jnp.int32).at[rows, owner].set(ordered)
    return (owner, lengths)


def draw_owner(key, part):
    return chord_layout(key)[0]


def draw_lengths(key, part):
    return chord_layout(key)[1]


def with_spikes(drawn, key, source, target, shards_of, factor):
    owner, partner = [(jnp.arange(drawn.shape[axis_at]) // (drawn.shape[axis_at] // shards_of)).reshape([-1 if axis == axis_at else 1 for axis in range(drawn.ndim)]) for axis_at in (source, target)]
    chosen = jax.random.permutation(key, shards_of)[partner]
    strong = (owner == chosen) | (owner == (partner + shards_of // 2) % shards_of)
    return jnp.where(strong, factor * drawn, drawn)


def block_levels(key, shape, cuts, low, high):
    def one(dim, shards_of):
        steps = jax.random.uniform(jax.random.fold_in(jax.random.fold_in(key, 6), dim), (shards_of,), jnp.float32, low / len(cuts), high / len(cuts))
        return jnp.repeat(jnp.exp(steps), shape[dim] // shards_of).reshape((-1,) + (1,) * (len(shape) - dim - 1))

    gain = one(*cuts[0])
    for cut in cuts[1:]:
        gain = gain * one(*cut)
    return gain


def gaussian(key, dims, spread, bound, shards=(), kind=jnp.bfloat16):
    level = block_levels(key, dims, shards, -0.22, 0.18) if shards else 1.0
    values = jax.random.normal(key, dims, jnp.float32) * spread * level
    return jnp.minimum(jnp.maximum(values, -bound), bound).astype(kind)


def noise_with(rng, shape, deviation, most, shards, heavy, held_as=jnp.bfloat16):
    result = deviation * jax.random.normal(rng, shape, jnp.float32)
    if shards:
        result = result * block_levels(rng, shape, shards, -0.22, 0.18)
    return jnp.clip(with_spikes(result, jax.random.fold_in(rng, 3), *heavy), -most, most).astype(held_as)


def setup_inputs(seed: int = 0) -> dict:
    splits = jax.random.split(jax.random.key(seed), 5)
    return {
        "proj": noise_with(splits[0], (VIEWS, CHORDS, DW), 1.0, 6.0, ((0, 16), (1, 2)), (0, 1, 16, 2.0)),
        "tiles": gaussian(splits[1], (VIEWS // VB, VB * DW, S), (VIEWS * DW) ** -0.5, 0.0390625, ((0, 16),)),
        "owner": draw_owner(jax.random.fold_in(splits[4], 71), 0),
        "lengths": draw_lengths(jax.random.fold_in(splits[4], 71), 0),
    }


def kernel_table(rows, start, cols):
    row_pos = start + jnp.arange(rows, dtype=jnp.float32)[:, None]
    col_pos = jnp.arange(cols, dtype=jnp.float32)[None, :]
    return 1.0 / (row_pos - col_pos + 0.5)

def weigh(length, count, start):
    position = start + jnp.arange(count, dtype=jnp.float32)[None, :] + 0.5
    inside = position < length
    return (inside, jnp.sqrt(jnp.where(inside, position * (length - position), 1.0)))

def invert_block(sums, length, table, start):
    length = length.astype(jnp.float32)[:, None]
    col_in, col_w = weigh(length, sums.shape[1], 0.0)
    row_in, row_w = weigh(length, table.shape[0], start)
    scaled = jnp.where(col_in, col_w * sums, 0.0)
    image = jnp.dot(scaled, table.T, precision=lax.Precision.HIGHEST, preferred_element_type=jnp.float32)
    return jnp.where(row_in, image / (math.pi * row_w), 0.0)

def reference(proj, tiles, owner, lengths):
    block_data = proj.reshape(VIEWS // VB, VB, CHORDS, DW)
    tile_stack = tiles.reshape(VIEWS // VB, VB, DW, S)

    def step(total, inputs):
        views_now, tile = inputs
        term = jnp.einsum('vkd,vds->ks', views_now.astype(jnp.float32), tile.astype(jnp.float32), precision=lax.Precision.HIGHEST)
        return (total + term, None)
    sums, _ = lax.scan(step, jnp.zeros((CHORDS, S), jnp.float32), (block_data, tile_stack))
    grouped = sums.reshape(GROUPS, CH_GRP, S)
    ordered = jnp.take_along_axis(grouped, owner[:, :, None], axis=1)
    ordered_len = jnp.take_along_axis(lengths, owner, axis=1)
    table = kernel_table(S, 0.0, S)
    recon = invert_block(ordered.reshape(CHORDS, S), ordered_len.reshape(CHORDS), table, 0.0)
    return recon.reshape(GROUPS, CH_GRP, S)
```

```python
import math

import jax
import jax.numpy as jnp
from jax import lax
from jax.experimental import pallas as pl
from jax.experimental.pallas import tpu as pltpu
from jax.sharding import PartitionSpec as P

LANE = 128
OWNED_SAMPLES = 4608
COLS = 256


def exchange_masks(devices):
    steps = devices.bit_length() - 1
    return [1] + [(1 << step) | 1 for step in range(1, steps)]


def slot_mask(slot, devices):
    masks = exchange_masks(devices)
    steps = len(masks)
    distance = 0
    for step, mask in enumerate(masks):
        bit = (slot >> (steps - 1 - step)) & 1
        distance = distance ^ (bit * mask)
    return distance


def slot_of(distance, devices):
    steps = devices.bit_length() - 1
    slot = jnp.zeros_like(distance)
    parity = jnp.zeros_like(distance)
    for step in range(1, steps):
        bit = (distance >> step) & 1
        slot = slot | (bit << (steps - 1 - step))
        parity = parity ^ bit
    first = (distance & 1) ^ parity
    return slot | (first << (steps - 1))


def rows_per_owner(owned):
    rows = (OWNED_SAMPLES + owned * (LANE - 1)) // LANE
    return -(-rows // 4) * 4


def block_counts(owner_ref, lengths_ref, group, place, owned):
    total = jnp.int32(0)
    lengths = []
    for index in range(owned):
        length = lengths_ref[group, owner_ref[group, place * owned + index]]
        lengths.append(length)
        blocks = (length + (LANE - 1)) >> 7
        total = total + lax.shift_right_logical(jnp.int32(0x11111111), 32 - 4 * blocks)
    return total, lengths


def block_offsets(counts, blocks):
    offset = jnp.int32(0)
    offsets = []
    for block in range(blocks):
        offsets.append(offset)
        offset = offset + (lax.shift_right_logical(counts, 4 * block) & 15)
    return offsets


def project_kernel(
    devices, owner_hbm, lengths_hbm, proj_hbm, tiles_hbm, keep_ref, send_ref,
    owner_s, lengths_s, owner_v, lengths_v, proj_buf, tile_buf, left_buf, sums_buf,
    small_sem, proj_sem, tile_sem,
):
    views, rows, footprint = proj_buf.shape
    chunks = tile_buf.shape[0]
    samples = chunks * COLS
    owned = rows // devices
    group = lax.axis_index("chord")
    me = lax.axis_index("view")
    small = [
        pltpu.make_async_copy(source, kept, small_sem.at[index])
        for index, (source, kept) in enumerate(
            [(owner_hbm, owner_v), (lengths_hbm, lengths_v), (owner_hbm, owner_s), (lengths_hbm, lengths_s)]
        )
    ]
    for copy in small:
        copy.start()
    proj_copy = pltpu.make_async_copy(proj_hbm, proj_buf, proj_sem)
    proj_copy.start()
    tile_copies = []
    for chunk in range(chunks):
        copy = pltpu.make_async_copy(
            tiles_hbm.at[:, :, pl.ds(chunk * COLS, COLS)], tile_buf.at[chunk], tile_sem.at[chunk]
        )
        copy.start()
        tile_copies.append(copy)

    keep_ref[...] = jnp.zeros_like(keep_ref)
    send_ref[...] = jnp.zeros_like(send_ref)
    for copy in small:
        copy.wait()
    down = lax.broadcasted_iota(jnp.int32, (rows, rows), 0)
    across = lax.broadcasted_iota(jnp.int32, (rows, rows), 1)
    diagonal = down == across

    def turned(row):
        spread = jnp.broadcast_to(row.astype(jnp.float32), (rows, rows))
        return jnp.sum(jnp.where(diagonal, spread, 0.0), axis=1, keepdims=True)

    order = turned(owner_v[pl.ds(group, 1), :])
    hit = order == across.astype(jnp.float32)
    position = jnp.sum(jnp.where(hit, down.astype(jnp.float32), 0.0), axis=0, keepdims=True)
    position = position.astype(jnp.int32)
    place = position // owned
    slot = slot_of(place ^ me, devices)
    key = (slot * (samples + 1) + (samples - lengths_v[pl.ds(group, 1), :])) * owned + (
        position - place * owned
    )
    key = key.astype(jnp.float32)
    target = jnp.sum(jnp.where(turned(key) < key, 1.0, 0.0), axis=0, keepdims=True)
    pick = jnp.where(down.astype(jnp.float32) == target, 1.0, 0.0).astype(jnp.bfloat16)

    proj_copy.wait()
    for view in range(views):
        moved = jnp.dot(pick, proj_buf[view], preferred_element_type=jnp.float32)
        left_buf[:, view * footprint : (view + 1) * footprint] = moved.astype(jnp.bfloat16)
    for chunk in range(chunks):
        tile_copies[chunk].wait()
        right = tile_buf[chunk].reshape(views * footprint, COLS)
        sums_buf[:, chunk * COLS : (chunk + 1) * COLS] = jnp.dot(
            left_buf[...], right, preferred_element_type=jnp.float32
        )

    packed = rows_per_owner(owned)
    half = devices // 2
    blocks = samples // LANE

    def pack(slot_index, base, out_ref):
        at = me ^ slot_mask(slot_index, devices)
        counts, _ = block_counts(owner_s, lengths_s, group, at, owned)
        for block, offset in enumerate(block_offsets(counts, blocks)):
            out_ref[pl.ds(base + offset, owned), :] = sums_buf[
                pl.ds(slot_index * owned, owned), block * LANE : (block + 1) * LANE
            ]

    if devices <= 16:
        for index in range(half):
            pack(half + index, index * packed, send_ref)
        for index in range(half):
            pack(index, index * packed, keep_ref)
    else:

        @pl.loop(0, half)
        def _(index):
            pack(half + index, index * packed, send_ref)

        @pl.loop(0, half)
        def _(index):
            pack(index, index * packed, keep_ref)


def project(proj, tiles, owner, lengths, devices):
    views, rows, footprint = proj.shape
    blocks, depth, samples = tiles.shape
    owned = rows // devices
    chunks = samples // COLS
    half_rows = devices // 2 * rows_per_owner(owned) + owned
    shape = pltpu.VMEM((half_rows, LANE), jnp.float32)
    inputs = [pltpu.with_memory_space_constraint(x, pltpu.HBM) for x in (owner, lengths, proj, tiles)]

    def kernel(*refs):
        project_kernel(devices, *refs)

    vmem = pl.BlockSpec(memory_space=pltpu.VMEM)
    hbm = pl.BlockSpec(memory_space=pltpu.HBM)
    return pl.pallas_call(
        kernel,
        out_shape=(shape, shape),
        in_specs=[hbm] * 4,
        out_specs=(vmem, vmem),
        scratch_shapes=[
            pltpu.SMEM(owner.shape, jnp.int32),
            pltpu.SMEM(lengths.shape, jnp.int32),
            pltpu.VMEM(owner.shape, jnp.int32),
            pltpu.VMEM(lengths.shape, jnp.int32),
            pltpu.VMEM(proj.shape, jnp.bfloat16),
            pltpu.VMEM((chunks, blocks, depth, COLS), jnp.bfloat16),
            pltpu.VMEM((rows, views * footprint), jnp.bfloat16),
            pltpu.VMEM((rows, samples), jnp.float32),
            pltpu.SemaphoreType.DMA((4,)),
            pltpu.SemaphoreType.DMA,
            pltpu.SemaphoreType.DMA((chunks,)),
        ],
        compiler_params=pltpu.CompilerParams(vmem_limit_bytes=40 << 20),
        cost_estimate=pl.CostEstimate(
            flops=2 * rows * views * footprint * samples,
            bytes_accessed=2 * (proj.size + tiles.size),
            transcendentals=0,
        ),
        name="project",
    )(*inputs)


def invert_kernel(devices, owner_s, lengths_s, mine_ref, other_ref, coarse_ref, fine_ref, out_ref, sum_buf, row_buf):
    owned, samples = row_buf.shape
    group = lax.axis_index("chord")
    me = lax.axis_index("view")
    packed = mine_ref.shape[0]
    sum_buf[0:packed, :] = mine_ref[...] + other_ref[...]
    counts, lengths = block_counts(owner_s, lengths_s, group, me, owned)
    offsets = block_offsets(counts, samples // LANE)
    for index in range(owned):
        rank = jnp.int32(0)
        for other in range(owned):
            if other < index:
                rank = rank + (lengths[other] >= lengths[index]).astype(jnp.int32)
            elif other > index:
                rank = rank + (lengths[other] > lengths[index]).astype(jnp.int32)
        for block, offset in enumerate(offsets):
            row_buf[index : index + 1, block * LANE : (block + 1) * LANE] = sum_buf[
                pl.ds(offset + rank, 1), :
            ]
    sub = lax.broadcasted_iota(jnp.int32, (owned, COLS), 0)
    length = jnp.zeros((owned, COLS), jnp.float32)
    for index in range(owned):
        length = jnp.where(sub == index, lengths[index].astype(jnp.float32), length)
    bins = samples // COLS
    lane = lax.broadcasted_iota(jnp.int32, (owned, COLS), 1).astype(jnp.float32) + 0.5
    weights, left = [], []
    for part in range(bins):
        spot = lane + float(part * COLS)
        inside = spot < length
        weight = jnp.sqrt(jnp.where(inside, spot * (length - spot), 1.0))
        weights.append((inside, weight))
        scaled = jnp.where(inside, weight * row_buf[:, part * COLS : (part + 1) * COLS], 0.0)
        coarse = scaled.astype(jnp.bfloat16)
        fine = (scaled - coarse.astype(jnp.float32)).astype(jnp.bfloat16)
        left.append(jnp.concatenate([coarse, fine], axis=0))
    image = [None] * bins
    for shift in range(1 - bins, bins):
        first, last = max(0, -shift), min(bins, bins - shift)
        stack = jnp.concatenate(left[first:last], axis=0)
        product = jnp.dot(
            stack, coarse_ref[shift + bins - 1], preferred_element_type=jnp.float32
        ) + jnp.dot(stack, fine_ref[shift + bins - 1], preferred_element_type=jnp.float32)
        for place, part in enumerate(range(first, last)):
            base = place * 2 * owned
            term = product[base : base + owned] + product[base + owned : base + 2 * owned]
            to = part + shift
            image[to] = term if image[to] is None else image[to] + term
    for part in range(bins):
        inside, weight = weights[part]
        out_ref[0, :, part * COLS : (part + 1) * COLS] = jnp.where(
            inside, image[part] / (math.pi * weight), 0.0
        )


def invert(mine, other, table, owner, lengths, devices, owned, samples):
    def kernel(*refs):
        invert_kernel(devices, *refs)

    smem = pl.BlockSpec(memory_space=pltpu.SMEM)
    vmem = pl.BlockSpec(memory_space=pltpu.VMEM)
    return pl.pallas_call(
        kernel,
        out_shape=jax.ShapeDtypeStruct((1, owned, samples), jnp.float32),
        in_specs=[smem, smem, vmem, vmem, vmem, vmem],
        out_specs=vmem,
        scratch_shapes=[
            pltpu.VMEM((mine.shape[0] + 3 * owned, LANE), jnp.float32),
            pltpu.VMEM((owned, samples), jnp.float32),
        ],
        compiler_params=pltpu.CompilerParams(vmem_limit_bytes=32 << 20),
        name="invert",
    )(owner, lengths, mine, other, *table)


def hilbert_table(bins):
    shape = (2 * bins - 1, COLS, COLS)
    shift = (lax.broadcasted_iota(jnp.int32, shape, 0) - (bins - 1)) * COLS
    gap = shift + lax.broadcasted_iota(jnp.int32, shape, 2) - lax.broadcasted_iota(jnp.int32, shape, 1)
    exact = 1.0 / (gap.astype(jnp.float32) + 0.5)
    coarse = lax.reduce_precision(exact, 8, 7)
    return coarse.astype(jnp.bfloat16), (exact - coarse).astype(jnp.bfloat16)


def per_device(proj, tiles, owner, lengths):
    devices = lax.axis_size("view")
    rows = proj.shape[1]
    samples = tiles.shape[2]
    owned = rows // devices
    packed = rows_per_owner(owned)
    keep, send = project(proj, tiles, owner, lengths, devices)
    table = hilbert_table(samples // COLS)
    held = devices // 2
    for mask in exchange_masks(devices)[:-1]:
        pairs = [(device, device ^ mask) for device in range(devices)]
        total = keep + lax.ppermute(send, "view", pairs)
        held //= 2
        keep, send = total[: held * packed], total[held * packed : 2 * held * packed]
    mask = exchange_masks(devices)[-1]
    pairs = [(device, device ^ mask) for device in range(devices)]
    other = lax.ppermute(send, "view", pairs)
    return invert(keep, other, table, owner, lengths, devices, owned, samples)


def solution(mesh):
    placed = (P("view", "chord", None), P("view", None, None), P(), P())
    return jax.shard_map(
        per_device, mesh=mesh, in_specs=placed, out_specs=P("chord", "view", None), check_vma=False
    )
```

```python
import math

import jax
import jax.numpy as jnp
from jax import lax
from jax.experimental import pallas as pl
from jax.experimental.pallas import tpu as pltpu
from jax.sharding import PartitionSpec as P

LANE = 128
OWNED_SAMPLES = 4608
COLS = 256


def exchange_masks(devices):
    steps = devices.bit_length() - 1
    return [1] + [(1 << step) | 1 for step in range(1, steps)]


def slot_mask(slot, devices):
    masks = exchange_masks(devices)
    steps = len(masks)
    distance = 0
    for step, mask in enumerate(masks):
        bit = (slot >> (steps - 1 - step)) & 1
        distance = distance ^ (bit * mask)
    return distance


def slot_of(distance, devices):
    steps = devices.bit_length() - 1
    slot = jnp.zeros_like(distance)
    parity = jnp.zeros_like(distance)
    for step in range(1, steps):
        bit = (distance >> step) & 1
        slot = slot | (bit << (steps - 1 - step))
        parity = parity ^ bit
    first = (distance & 1) ^ parity
    return slot | (first << (steps - 1))


def rows_per_owner(owned):
    rows = (OWNED_SAMPLES + owned * (LANE - 1)) // LANE
    return -(-rows // 4) * 4


def block_counts(lengths):
    total = jnp.int32(0)
    for length in lengths:
        blocks = (length + (LANE - 1)) >> 7
        total = total + lax.shift_right_logical(jnp.int32(0x11111111), 32 - 4 * blocks)
    return total


def offset_words(counts):
    even = counts & 0x0F0F0F0F
    odd = lax.shift_right_logical(counts, 4) & 0x0F0F0F0F
    before = ((even + odd) * 0x01010101) << 8
    return before, before + even


def row_of(words, block):
    return lax.shift_right_logical(words[block % 2], 8 * (block // 2)) & 255


def owned_lengths(owner_ref, lengths_ref, group, place, owned):
    return [lengths_ref[group, owner_ref[group, place * owned + index]] for index in range(owned)]


def column_chunks(samples):
    return [(0, samples // 2), (samples // 2, samples // 2)]


def project_kernel(
    devices, owner_hbm, lengths_hbm, proj_hbm, tiles_hbm, keep_ref, send_ref,
    owner_v, lengths_v, offset_v, offset_s, proj_buf, tile_buf, left_buf, sums_buf,
    small_sem, offset_sem, proj_sem, tile_sem,
):
    views, rows, footprint = proj_buf.shape
    samples = tile_buf.shape[2]
    chunks = column_chunks(samples)
    owned = rows // devices
    group = lax.axis_index("chord")
    me = lax.axis_index("view")
    small = [
        pltpu.make_async_copy(source, kept, small_sem.at[index])
        for index, (source, kept) in enumerate(
            [(owner_hbm, owner_v), (lengths_hbm, lengths_v)]
        )
    ]
    for copy in small:
        copy.start()
    proj_copy = pltpu.make_async_copy(proj_hbm, proj_buf, proj_sem)
    proj_copy.start()
    tile_copies = []
    for index, (start, width) in enumerate(chunks):
        columns = pl.ds(start, width)
        copy = pltpu.make_async_copy(
            tiles_hbm.at[:, :, columns], tile_buf.at[:, :, columns], tile_sem.at[index]
        )
        copy.start()
        tile_copies.append(copy)

    keep_ref[...] = jnp.zeros_like(keep_ref)
    send_ref[...] = jnp.zeros_like(send_ref)
    for copy in small:
        copy.wait()
    down = lax.broadcasted_iota(jnp.int32, (rows, rows), 0)
    across = lax.broadcasted_iota(jnp.int32, (rows, rows), 1)
    diagonal = down == across

    def turned(row):
        spread = jnp.broadcast_to(row.astype(jnp.float32), (rows, rows))
        return jnp.sum(jnp.where(diagonal, spread, 0.0), axis=1, keepdims=True)

    lengths = lengths_v[pl.ds(group, 1), :]
    order = turned(owner_v[pl.ds(group, 1), :])
    hit = order == across.astype(jnp.float32)
    position = jnp.sum(jnp.where(hit, down.astype(jnp.float32), 0.0), axis=0, keepdims=True)
    position = position.astype(jnp.int32)
    place = position // owned
    slot = slot_of(place ^ me, devices)

    reach = turned((lengths + (LANE - 1)) // LANE)
    block_index = lax.broadcasted_iota(jnp.int32, (rows, LANE), 1).astype(jnp.float32)
    before = jnp.where(block_index < samples // LANE, jnp.minimum(block_index, reach), 0.0)
    member = lax.broadcasted_iota(jnp.int32, (devices, rows), 0) == slot
    offset_v[...] = jnp.dot(
        jnp.where(member, 1.0, 0.0).astype(jnp.bfloat16),
        before.astype(jnp.bfloat16),
        preferred_element_type=jnp.float32,
    ).astype(jnp.int32)
    offset_copy = pltpu.make_async_copy(offset_v, offset_s, offset_sem)
    offset_copy.start()

    key = (slot * (samples + 1) + (samples - lengths)) * owned + (
        position - place * owned
    )
    key = key.astype(jnp.float32)
    target = jnp.sum(jnp.where(turned(key) < key, 1.0, 0.0), axis=0, keepdims=True)
    pick = jnp.where(down.astype(jnp.float32) == target, 1.0, 0.0).astype(jnp.bfloat16)

    def each_slot(body):
        if devices <= 16:
            for index in range(devices):
                body(index)
        else:
            pl.loop(0, devices)(body)

    proj_copy.wait()
    for view in range(views):
        moved = jnp.dot(pick, proj_buf[view], preferred_element_type=jnp.float32)
        left_buf[:, view * footprint : (view + 1) * footprint] = moved.astype(jnp.bfloat16)

    packed = rows_per_owner(owned)
    half = devices // 2

    def put(slot_index, offset, value):
        def to(out_ref, base):
            out_ref[pl.ds(base + offset, owned), :] = value

        if isinstance(slot_index, int):
            if slot_index < half:
                to(keep_ref, slot_index * packed)
            else:
                to(send_ref, (slot_index - half) * packed)
        else:
            pl.when(slot_index < half)(lambda: to(keep_ref, slot_index * packed))
            pl.when(slot_index >= half)(lambda: to(send_ref, (slot_index - half) * packed))

    def pack(first, last):
        def one(slot_index):
            for block in range(first, last):
                value = sums_buf[pl.ds(slot_index * owned, owned), block * LANE : (block + 1) * LANE]
                put(slot_index, offset_s[slot_index, block] if block else 0, value)

        each_slot(one)

    ready = 1
    for index, (start, width) in enumerate(chunks):
        tile_copies[index].wait()
        right = tile_buf[:, :, start : start + width].reshape(views * footprint, width)
        sums_buf[:, start : start + width] = jnp.dot(
            left_buf[...], right, preferred_element_type=jnp.float32
        )
        if index == 1:
            offset_copy.wait()
        if index:
            pack(ready, start // LANE)
            ready = max(ready, start // LANE)
    pack(ready, samples // LANE)
    pack(0, 1)


def project(proj, tiles, owner, lengths, devices):
    views, rows, footprint = proj.shape
    blocks, depth, samples = tiles.shape
    owned = rows // devices
    chunks = column_chunks(samples)
    half_rows = devices // 2 * rows_per_owner(owned) + owned
    shape = pltpu.VMEM((half_rows, LANE), jnp.float32)
    inputs = [pltpu.with_memory_space_constraint(x, pltpu.HBM) for x in (owner, lengths, proj, tiles)]

    def kernel(*refs):
        project_kernel(devices, *refs)

    vmem = pl.BlockSpec(memory_space=pltpu.VMEM)
    hbm = pl.BlockSpec(memory_space=pltpu.HBM)
    return pl.pallas_call(
        kernel,
        out_shape=(shape, shape),
        in_specs=[hbm] * 4,
        out_specs=(vmem, vmem),
        scratch_shapes=[
            pltpu.VMEM(owner.shape, jnp.int32),
            pltpu.VMEM(lengths.shape, jnp.int32),
            pltpu.VMEM((devices, LANE), jnp.int32),
            pltpu.SMEM((devices, LANE), jnp.int32),
            pltpu.VMEM(proj.shape, jnp.bfloat16),
            pltpu.VMEM(tiles.shape, jnp.bfloat16),
            pltpu.VMEM((rows, views * footprint), jnp.bfloat16),
            pltpu.VMEM((rows, samples), jnp.float32),
            pltpu.SemaphoreType.DMA((2,)),
            pltpu.SemaphoreType.DMA,
            pltpu.SemaphoreType.DMA,
            pltpu.SemaphoreType.DMA((len(chunks),)),
        ],
        compiler_params=pltpu.CompilerParams(vmem_limit_bytes=40 << 20),
        cost_estimate=pl.CostEstimate(
            flops=2 * rows * views * footprint * samples,
            bytes_accessed=2 * (proj.size + tiles.size),
            transcendentals=0,
        ),
        name="project",
    )(*inputs)


def invert_kernel(devices, owner_s, lengths_s, mine_ref, other_ref, coarse_ref, fine_ref, out_ref, sum_buf, row_buf):
    owned, samples = row_buf.shape
    group = lax.axis_index("chord")
    me = lax.axis_index("view")
    packed = mine_ref.shape[0]
    sum_buf[0:packed, :] = mine_ref[...] + other_ref[...]
    lengths = owned_lengths(owner_s, lengths_s, group, me, owned)
    words = offset_words(block_counts(lengths))
    offsets = [row_of(words, block) for block in range(samples // LANE)]
    for index in range(owned):
        rank = jnp.int32(0)
        for other in range(owned):
            if other < index:
                rank = rank + (lengths[other] >= lengths[index]).astype(jnp.int32)
            elif other > index:
                rank = rank + (lengths[other] > lengths[index]).astype(jnp.int32)
        for block, offset in enumerate(offsets):
            row_buf[index : index + 1, block * LANE : (block + 1) * LANE] = sum_buf[
                pl.ds(offset + rank, 1), :
            ]
    sub = lax.broadcasted_iota(jnp.int32, (owned, COLS), 0)
    length = jnp.zeros((owned, COLS), jnp.float32)
    for index in range(owned):
        length = jnp.where(sub == index, lengths[index].astype(jnp.float32), length)
    bins = samples // COLS
    lane = lax.broadcasted_iota(jnp.int32, (owned, COLS), 1).astype(jnp.float32) + 0.5
    weights, left = [], []
    for part in range(bins):
        spot = lane + float(part * COLS)
        inside = spot < length
        weight = jnp.sqrt(jnp.where(inside, spot * (length - spot), 1.0))
        weights.append((inside, weight))
        scaled = jnp.where(inside, weight * row_buf[:, part * COLS : (part + 1) * COLS], 0.0)
        coarse = scaled.astype(jnp.bfloat16)
        fine = (scaled - coarse.astype(jnp.float32)).astype(jnp.bfloat16)
        left.append(jnp.concatenate([coarse, fine], axis=0))
    image = [None] * bins
    for shift in range(1 - bins, bins):
        first, last = max(0, -shift), min(bins, bins - shift)
        stack = jnp.concatenate(left[first:last], axis=0)
        product = jnp.dot(
            stack, coarse_ref[shift + bins - 1], preferred_element_type=jnp.float32
        ) + jnp.dot(stack, fine_ref[shift + bins - 1], preferred_element_type=jnp.float32)
        for place, part in enumerate(range(first, last)):
            base = place * 2 * owned
            term = product[base : base + owned] + product[base + owned : base + 2 * owned]
            to = part + shift
            image[to] = term if image[to] is None else image[to] + term
    for part in range(bins):
        inside, weight = weights[part]
        out_ref[0, :, part * COLS : (part + 1) * COLS] = jnp.where(
            inside, image[part] / (math.pi * weight), 0.0
        )


def invert(mine, other, table, owner, lengths, devices, owned, samples):
    def kernel(*refs):
        invert_kernel(devices, *refs)

    smem = pl.BlockSpec(memory_space=pltpu.SMEM)
    vmem = pl.BlockSpec(memory_space=pltpu.VMEM)
    return pl.pallas_call(
        kernel,
        out_shape=jax.ShapeDtypeStruct((1, owned, samples), jnp.float32),
        in_specs=[smem, smem, vmem, vmem, vmem, vmem],
        out_specs=vmem,
        scratch_shapes=[
            pltpu.VMEM((mine.shape[0] + 3 * owned, LANE), jnp.float32),
            pltpu.VMEM((owned, samples), jnp.float32),
        ],
        compiler_params=pltpu.CompilerParams(vmem_limit_bytes=32 << 20),
        name="invert",
    )(owner, lengths, mine, other, *table)


def hilbert_table(bins):
    shape = (2 * bins - 1, COLS, COLS)
    shift = (lax.broadcasted_iota(jnp.int32, shape, 0) - (bins - 1)) * COLS
    gap = shift + lax.broadcasted_iota(jnp.int32, shape, 2) - lax.broadcasted_iota(jnp.int32, shape, 1)
    exact = 1.0 / (gap.astype(jnp.float32) + 0.5)
    coarse = lax.reduce_precision(exact, 8, 7)
    return coarse.astype(jnp.bfloat16), (exact - coarse).astype(jnp.bfloat16)


def per_device(proj, tiles, owner, lengths):
    devices = lax.axis_size("view")
    rows = proj.shape[1]
    samples = tiles.shape[2]
    owned = rows // devices
    packed = rows_per_owner(owned)
    keep, send = project(proj, tiles, owner, lengths, devices)
    table = hilbert_table(samples // COLS)
    held = devices // 2
    for mask in exchange_masks(devices)[:-1]:
        pairs = [(device, device ^ mask) for device in range(devices)]
        total = keep + lax.ppermute(send, "view", pairs)
        held //= 2
        keep, send = total[: held * packed], total[held * packed : 2 * held * packed]
    mask = exchange_masks(devices)[-1]
    pairs = [(device, device ^ mask) for device in range(devices)]
    other = lax.ppermute(send, "view", pairs)
    return invert(keep, other, table, owner, lengths, devices, owned, samples)


def solution(mesh):
    placed = (P("view", "chord", None), P("view", None, None), P(), P())
    return jax.shard_map(
        per_device, mesh=mesh, in_specs=placed, out_specs=P("chord", "view", None), check_vma=False
    )
```

```python
import math

import jax
import jax.numpy as jnp
from jax import lax
from jax.experimental import pallas as pl
from jax.experimental.pallas import tpu as pltpu
from jax.sharding import PartitionSpec as P

LANE = 128
OWNED_SAMPLES = 4608
COLS = 256


def exchange_masks(devices):
    steps = devices.bit_length() - 1
    return [1] + [(1 << step) | 1 for step in range(1, steps)]


def slot_mask(slot, devices):
    masks = exchange_masks(devices)
    steps = len(masks)
    distance = 0
    for step, mask in enumerate(masks):
        bit = (slot >> (steps - 1 - step)) & 1
        distance = distance ^ (bit * mask)
    return distance


def slot_of(distance, devices):
    steps = devices.bit_length() - 1
    slot = jnp.zeros_like(distance)
    parity = jnp.zeros_like(distance)
    for step in range(1, steps):
        bit = (distance >> step) & 1
        slot = slot | (bit << (steps - 1 - step))
        parity = parity ^ bit
    first = (distance & 1) ^ parity
    return slot | (first << (steps - 1))


def rows_per_owner(owned):
    rows = (OWNED_SAMPLES + owned * (LANE - 1)) // LANE
    return -(-rows // 4) * 4


def column_chunks(samples):
    return [(0, samples // 2), (samples // 2, samples // 2)]


def project_kernel(
    devices, owner_hbm, lengths_hbm, proj_hbm, tiles_hbm, keep_ref, send_ref,
    owner_v, lengths_v, offset_v, offset_s, proj_buf, tile_buf, left_buf, sums_buf,
    small_sem, offset_sem, proj_sem, tile_sem,
):
    views, rows, footprint = proj_buf.shape
    samples = tile_buf.shape[2]
    chunks = column_chunks(samples)
    owned = rows // devices
    group = lax.axis_index("chord")
    me = lax.axis_index("view")
    small = [
        pltpu.make_async_copy(source, kept, small_sem.at[index])
        for index, (source, kept) in enumerate(
            [(owner_hbm, owner_v), (lengths_hbm, lengths_v)]
        )
    ]
    for copy in small:
        copy.start()
    proj_copy = pltpu.make_async_copy(proj_hbm, proj_buf, proj_sem)
    proj_copy.start()
    tile_copies = []
    for index, (start, width) in enumerate(chunks):
        columns = pl.ds(start, width)
        copy = pltpu.make_async_copy(
            tiles_hbm.at[:, :, columns], tile_buf.at[:, :, columns], tile_sem.at[index]
        )
        copy.start()
        tile_copies.append(copy)

    keep_ref[...] = jnp.zeros_like(keep_ref)
    send_ref[...] = jnp.zeros_like(send_ref)
    for copy in small:
        copy.wait()
    down = lax.broadcasted_iota(jnp.int32, (rows, rows), 0)
    across = lax.broadcasted_iota(jnp.int32, (rows, rows), 1)
    diagonal = down == across

    def turned(row):
        spread = jnp.broadcast_to(row.astype(jnp.float32), (rows, rows))
        return jnp.sum(jnp.where(diagonal, spread, 0.0), axis=1, keepdims=True)

    lengths = lengths_v[pl.ds(group, 1), :]
    order = turned(owner_v[pl.ds(group, 1), :])
    hit = order == across.astype(jnp.float32)
    position = jnp.sum(jnp.where(hit, down.astype(jnp.float32), 0.0), axis=0, keepdims=True)
    position = position.astype(jnp.int32)
    place = position // owned
    slot = slot_of(place ^ me, devices)

    reach = turned((lengths + (LANE - 1)) // LANE)
    block_index = lax.broadcasted_iota(jnp.int32, (rows, LANE), 1).astype(jnp.float32)
    before = jnp.where(block_index < samples // LANE, jnp.minimum(block_index, reach), 0.0)
    member = lax.broadcasted_iota(jnp.int32, (devices, rows), 0) == slot
    offset_v[...] = jnp.dot(
        jnp.where(member, 1.0, 0.0).astype(jnp.bfloat16),
        before.astype(jnp.bfloat16),
        preferred_element_type=jnp.float32,
    ).astype(jnp.int32)
    offset_copy = pltpu.make_async_copy(offset_v, offset_s, offset_sem)
    offset_copy.start()

    key = (slot * (samples + 1) + (samples - lengths)) * owned + (
        position - place * owned
    )
    key = key.astype(jnp.float32)
    target = jnp.sum(jnp.where(turned(key) < key, 1.0, 0.0), axis=0, keepdims=True)
    pick = jnp.where(down.astype(jnp.float32) == target, 1.0, 0.0).astype(jnp.bfloat16)

    def each_slot(body):
        if devices <= 16:
            for index in range(devices):
                body(index)
        else:
            pl.loop(0, devices)(body)

    proj_copy.wait()
    for view in range(views):
        moved = jnp.dot(pick, proj_buf[view], preferred_element_type=jnp.float32)
        left_buf[:, view * footprint : (view + 1) * footprint] = moved.astype(jnp.bfloat16)

    packed = rows_per_owner(owned)
    half = devices // 2

    def put(slot_index, offset, value):
        def to(out_ref, base):
            out_ref[pl.ds(base + offset, owned), :] = value

        if isinstance(slot_index, int):
            if slot_index < half:
                to(keep_ref, slot_index * packed)
            else:
                to(send_ref, (slot_index - half) * packed)
        else:
            pl.when(slot_index < half)(lambda: to(keep_ref, slot_index * packed))
            pl.when(slot_index >= half)(lambda: to(send_ref, (slot_index - half) * packed))

    def pack(first, last):
        def one(slot_index):
            for block in range(first, last):
                value = sums_buf[pl.ds(slot_index * owned, owned), block * LANE : (block + 1) * LANE]
                put(slot_index, offset_s[slot_index, block] if block else 0, value)

        each_slot(one)

    ready = 1
    for index, (start, width) in enumerate(chunks):
        tile_copies[index].wait()
        right = tile_buf[:, :, start : start + width].reshape(views * footprint, width)
        sums_buf[:, start : start + width] = jnp.dot(
            left_buf[...], right, preferred_element_type=jnp.float32
        )
        if index == 1:
            offset_copy.wait()
        if index:
            pack(ready, start // LANE)
            ready = max(ready, start // LANE)
    pack(ready, samples // LANE)
    pack(0, 1)


def project(proj, tiles, owner, lengths, devices):
    views, rows, footprint = proj.shape
    blocks, depth, samples = tiles.shape
    owned = rows // devices
    chunks = column_chunks(samples)
    half_rows = devices // 2 * rows_per_owner(owned) + owned
    shape = pltpu.VMEM((half_rows, LANE), jnp.float32)
    inputs = [pltpu.with_memory_space_constraint(x, pltpu.HBM) for x in (owner, lengths, proj, tiles)]

    def kernel(*refs):
        project_kernel(devices, *refs)

    vmem = pl.BlockSpec(memory_space=pltpu.VMEM)
    hbm = pl.BlockSpec(memory_space=pltpu.HBM)
    return pl.pallas_call(
        kernel,
        out_shape=(shape, shape),
        in_specs=[hbm] * 4,
        out_specs=(vmem, vmem),
        scratch_shapes=[
            pltpu.VMEM(owner.shape, jnp.int32),
            pltpu.VMEM(lengths.shape, jnp.int32),
            pltpu.VMEM((devices, LANE), jnp.int32),
            pltpu.SMEM((devices, LANE), jnp.int32),
            pltpu.VMEM(proj.shape, jnp.bfloat16),
            pltpu.VMEM(tiles.shape, jnp.bfloat16),
            pltpu.VMEM((rows, views * footprint), jnp.bfloat16),
            pltpu.VMEM((rows, samples), jnp.float32),
            pltpu.SemaphoreType.DMA((2,)),
            pltpu.SemaphoreType.DMA,
            pltpu.SemaphoreType.DMA,
            pltpu.SemaphoreType.DMA((len(chunks),)),
        ],
        compiler_params=pltpu.CompilerParams(vmem_limit_bytes=40 << 20),
        cost_estimate=pl.CostEstimate(
            flops=2 * rows * views * footprint * samples,
            bytes_accessed=2 * (proj.size + tiles.size),
            transcendentals=0,
        ),
        name="project",
    )(*inputs)


def prepare_kernel(
    devices, owner_hbm, lengths_hbm, unpick_ref, inner_ref, outer_ref, coarse_ref, fine_ref,
    owner_s, lengths_s, sem,
):
    owned, samples = inner_ref.shape
    blocks = samples // LANE
    packed = unpick_ref.shape[1]
    distances = coarse_ref.shape[0]
    group = lax.axis_index("chord")
    me = lax.axis_index("view")
    copies = [
        pltpu.make_async_copy(owner_hbm, owner_s, sem.at[0]),
        pltpu.make_async_copy(lengths_hbm, lengths_s, sem.at[1]),
    ]
    for copy in copies:
        copy.start()
    across = lax.broadcasted_iota(jnp.int32, (COLS, COLS), 1)
    gap = (across - lax.broadcasted_iota(jnp.int32, (COLS, COLS), 0)).astype(jnp.float32) + 0.5
    for index in range(distances):
        exact = 1.0 / (gap + float((index - distances // 2) * COLS))
        coarse = exact.astype(jnp.bfloat16)
        coarse_ref[index] = coarse
        fine_ref[index] = (exact - coarse.astype(jnp.float32)).astype(jnp.bfloat16)
    for copy in copies:
        copy.wait()
    lengths = [lengths_s[group, owner_s[group, me * owned + index]] for index in range(owned)]

    sub = lax.broadcasted_iota(jnp.int32, (owned, LANE), 0)
    lane = lax.broadcasted_iota(jnp.int32, (owned, LANE), 1)
    length = jnp.zeros((owned, LANE), jnp.int32)
    for index in range(owned):
        length = jnp.where(sub == index, lengths[index], length)
    rank = jnp.zeros((owned, LANE), jnp.int32)
    for index in range(owned):
        ahead = (lengths[index] > length) | ((lengths[index] == length) & (index < sub))
        rank = rank + jnp.where(ahead, 1, 0)
    reach = (length + (LANE - 1)) >> 7
    rows = []
    for block in range(blocks):
        offset = jnp.int32(0)
        for index in range(owned):
            offset = offset + jnp.minimum((lengths[index] + (LANE - 1)) >> 7, block)
        hit = (lane == rank + offset) & (reach > block)
        rows.append(jnp.where(hit, 1.0, 0.0))
    unpick_ref[...] = jnp.concatenate(rows, axis=0)[:, :packed].astype(jnp.bfloat16)

    long = length.astype(jnp.float32)
    for block in range(blocks):
        spot = (lane + block * LANE).astype(jnp.float32) + 0.5
        inside = spot < long
        weight = jnp.sqrt(jnp.where(inside, spot * (long - spot), 1.0))
        columns = slice(block * LANE, (block + 1) * LANE)
        inner_ref[:, columns] = jnp.where(inside, weight, 0.0)
        outer_ref[:, columns] = jnp.where(inside, 1.0 / (math.pi * weight), 0.0)


def prepare(owner, lengths, devices, owned, samples, packed):
    distances = 2 * (samples // COLS) - 1
    inputs = [pltpu.with_memory_space_constraint(x, pltpu.HBM) for x in (owner, lengths)]
    vmem = pl.BlockSpec(memory_space=pltpu.VMEM)

    def kernel(*refs):
        prepare_kernel(devices, *refs)

    return pl.pallas_call(
        kernel,
        out_shape=(
            pltpu.VMEM((owned * samples // LANE, packed), jnp.bfloat16),
            pltpu.VMEM((owned, samples), jnp.float32),
            pltpu.VMEM((owned, samples), jnp.float32),
            pltpu.VMEM((distances, COLS, COLS), jnp.bfloat16),
            pltpu.VMEM((distances, COLS, COLS), jnp.bfloat16),
        ),
        in_specs=[pl.BlockSpec(memory_space=pltpu.HBM)] * 2,
        out_specs=(vmem,) * 5,
        scratch_shapes=[
            pltpu.SMEM(owner.shape, jnp.int32),
            pltpu.SMEM(lengths.shape, jnp.int32),
            pltpu.SemaphoreType.DMA((2,)),
        ],
        compiler_params=pltpu.CompilerParams(vmem_limit_bytes=32 << 20),
        cost_estimate=pl.CostEstimate(flops=1 << 22, bytes_accessed=1 << 21, transcendentals=1 << 19),
        name="prepare",
    )(*inputs)


def invert_kernel(mine_ref, other_ref, unpick_ref, inner_ref, outer_ref, coarse_ref, fine_ref, out_ref):
    owned, samples = inner_ref.shape
    bins = samples // COLS
    per_bin = COLS // LANE

    def halves(value):
        coarse = value.astype(jnp.bfloat16)
        return coarse, (value - coarse.astype(jnp.float32)).astype(jnp.bfloat16)

    both = jnp.concatenate(halves(mine_ref[...] + other_ref[...]), axis=1)
    spread = jnp.dot(unpick_ref[...], both, preferred_element_type=jnp.float32)
    spread = spread[:, :LANE] + spread[:, LANE:]
    left = []
    for part in range(bins):
        sums = jnp.concatenate(
            [spread[block * owned : (block + 1) * owned] for block in range(part * per_bin, (part + 1) * per_bin)],
            axis=1,
        )
        scaled = inner_ref[:, part * COLS : (part + 1) * COLS] * sums
        left.append(jnp.concatenate(halves(scaled), axis=0))
    image = [None] * bins
    for shift in range(1 - bins, bins):
        first, last = max(0, -shift), min(bins, bins - shift)
        stack = jnp.concatenate(left[first:last], axis=0)
        product = jnp.dot(
            stack, coarse_ref[shift + bins - 1], preferred_element_type=jnp.float32
        ) + jnp.dot(stack, fine_ref[shift + bins - 1], preferred_element_type=jnp.float32)
        for place, part in enumerate(range(first, last)):
            base = place * 2 * owned
            term = product[base : base + owned] + product[base + owned : base + 2 * owned]
            to = part + shift
            image[to] = term if image[to] is None else image[to] + term
    for part in range(bins):
        columns = slice(part * COLS, (part + 1) * COLS)
        out_ref[0, :, columns] = image[part] * outer_ref[:, columns]


def invert(mine, other, prepared, owned, samples):
    vmem = pl.BlockSpec(memory_space=pltpu.VMEM)
    return pl.pallas_call(
        invert_kernel,
        out_shape=jax.ShapeDtypeStruct((1, owned, samples), jnp.float32),
        in_specs=[vmem] * 7,
        out_specs=vmem,
        compiler_params=pltpu.CompilerParams(vmem_limit_bytes=32 << 20),
        name="invert",
    )(mine, other, *prepared)


def per_device(proj, tiles, owner, lengths):
    devices = lax.axis_size("view")
    rows = proj.shape[1]
    samples = tiles.shape[2]
    owned = rows // devices
    packed = rows_per_owner(owned)
    keep, send = project(proj, tiles, owner, lengths, devices)
    prepared = prepare(owner, lengths, devices, owned, samples, packed)
    held = devices // 2
    for mask in exchange_masks(devices)[:-1]:
        pairs = [(device, device ^ mask) for device in range(devices)]
        total = keep + lax.ppermute(send, "view", pairs)
        held //= 2
        keep, send = total[: held * packed], total[held * packed : 2 * held * packed]
    mask = exchange_masks(devices)[-1]
    pairs = [(device, device ^ mask) for device in range(devices)]
    other = lax.ppermute(send, "view", pairs)
    return invert(keep, other, prepared, owned, samples)


def solution(mesh):
    placed = (P("view", "chord", None), P("view", None, None), P(), P())
    return jax.shard_map(
        per_device, mesh=mesh, in_specs=placed, out_specs=P("chord", "view", None), check_vma=False
    )
```

```python
import math

import jax
import jax.numpy as jnp
from jax import lax
from jax.experimental import pallas as pl
from jax.experimental.pallas import tpu as pltpu
from jax.sharding import PartitionSpec as P

LANE = 128
OWNED_SAMPLES = 4608
COLS = 256


def side(place):
    return (place ^ (place >> 1) ^ (place >> 2)) & 1


def exchange_pairs(devices):
    steps = [[place ^ 1 for place in range(devices)]]
    for first, second in ((3, 5), (5, 3)):
        steps.append([place ^ (second if side(place) else first) for place in range(devices)])
    step = 8
    while step < devices:
        steps.append([place ^ (step | 1) for place in range(devices)])
        step *= 2
    return [list(enumerate(partners)) for partners in steps]


def slot_of(place, me, devices):
    distance = place ^ me
    steps = devices.bit_length() - 1
    first = distance & 1
    slot = jnp.zeros_like(distance)
    for step in range(1, steps):
        bit = (distance >> step) & 1
        first = first ^ bit
        if step > 2:
            slot = slot | (bit << (steps - 1 - step))
    near, far = (distance >> 1) & 1, (distance >> 2) & 1
    swap = side(me) ^ first
    early = jnp.where(swap == 1, far, near)
    late = jnp.where(swap == 1, near, far)
    return slot | (first << (steps - 1)) | (early << (steps - 2)) | (late << (steps - 3))


def rows_per_owner(owned):
    rows = (OWNED_SAMPLES + owned * (LANE - 1)) // LANE
    return -(-rows // 4) * 4


def column_chunks(samples):
    return [(0, samples // 2), (samples // 2, samples // 2)]


def project_kernel(
    devices, owner_hbm, lengths_hbm, proj_hbm, tiles_hbm, keep_ref, send_ref,
    owner_v, lengths_v, offset_v, offset_s, proj_buf, tile_buf, left_buf, sums_buf,
    small_sem, offset_sem, proj_sem, tile_sem,
):
    views, rows, footprint = proj_buf.shape
    samples = tile_buf.shape[2]
    chunks = column_chunks(samples)
    owned = rows // devices
    group = lax.axis_index("chord")
    me = lax.axis_index("view")
    small = [
        pltpu.make_async_copy(source, kept, small_sem.at[index])
        for index, (source, kept) in enumerate(
            [(owner_hbm, owner_v), (lengths_hbm, lengths_v)]
        )
    ]
    for copy in small:
        copy.start()
    proj_copy = pltpu.make_async_copy(proj_hbm, proj_buf, proj_sem)
    proj_copy.start()
    tile_copies = []
    for index, (start, width) in enumerate(chunks):
        columns = pl.ds(start, width)
        copy = pltpu.make_async_copy(
            tiles_hbm.at[:, :, columns], tile_buf.at[:, :, columns], tile_sem.at[index]
        )
        copy.start()
        tile_copies.append(copy)

    keep_ref[...] = jnp.zeros_like(keep_ref)
    send_ref[...] = jnp.zeros_like(send_ref)
    for copy in small:
        copy.wait()
    down = lax.broadcasted_iota(jnp.int32, (rows, rows), 0)
    across = lax.broadcasted_iota(jnp.int32, (rows, rows), 1)
    diagonal = down == across

    def turned(row):
        spread = jnp.broadcast_to(row.astype(jnp.float32), (rows, rows))
        return jnp.sum(jnp.where(diagonal, spread, 0.0), axis=1, keepdims=True)

    lengths = lengths_v[pl.ds(group, 1), :]
    order = turned(owner_v[pl.ds(group, 1), :])
    hit = order == across.astype(jnp.float32)
    position = jnp.sum(jnp.where(hit, down.astype(jnp.float32), 0.0), axis=0, keepdims=True)
    position = position.astype(jnp.int32)
    place = position // owned
    slot = slot_of(place, me, devices)

    reach = turned((lengths + (LANE - 1)) // LANE)
    block_index = lax.broadcasted_iota(jnp.int32, (rows, LANE), 1).astype(jnp.float32)
    before = jnp.where(block_index < samples // LANE, jnp.minimum(block_index, reach), 0.0)
    member = lax.broadcasted_iota(jnp.int32, (devices, rows), 0) == slot
    offset_v[...] = jnp.dot(
        jnp.where(member, 1.0, 0.0).astype(jnp.bfloat16),
        before.astype(jnp.bfloat16),
        preferred_element_type=jnp.float32,
    ).astype(jnp.int32)
    offset_copy = pltpu.make_async_copy(offset_v, offset_s, offset_sem)
    offset_copy.start()

    key = (slot * (samples + 1) + (samples - lengths)) * owned + (
        position - place * owned
    )
    key = key.astype(jnp.float32)
    target = jnp.sum(jnp.where(turned(key) < key, 1.0, 0.0), axis=0, keepdims=True)
    pick = jnp.where(down.astype(jnp.float32) == target, 1.0, 0.0).astype(jnp.bfloat16)

    def each_slot(body):
        if devices <= 16:
            for index in range(devices):
                body(index)
        else:
            pl.loop(0, devices)(body)

    proj_copy.wait()
    for view in range(views):
        moved = jnp.dot(pick, proj_buf[view], preferred_element_type=jnp.float32)
        left_buf[:, view * footprint : (view + 1) * footprint] = moved.astype(jnp.bfloat16)

    packed = rows_per_owner(owned)
    half = devices // 2

    def put(slot_index, offset, value):
        def to(out_ref, base):
            out_ref[pl.ds(base + offset, owned), :] = value

        if isinstance(slot_index, int):
            if slot_index < half:
                to(keep_ref, slot_index * packed)
            else:
                to(send_ref, (slot_index - half) * packed)
        else:
            pl.when(slot_index < half)(lambda: to(keep_ref, slot_index * packed))
            pl.when(slot_index >= half)(lambda: to(send_ref, (slot_index - half) * packed))

    def pack(first, last):
        def one(slot_index):
            for block in range(first, last):
                value = sums_buf[pl.ds(slot_index * owned, owned), block * LANE : (block + 1) * LANE]
                put(slot_index, offset_s[slot_index, block] if block else 0, value)

        each_slot(one)

    ready = 1
    for index, (start, width) in enumerate(chunks):
        tile_copies[index].wait()
        right = tile_buf[:, :, start : start + width].reshape(views * footprint, width)
        sums_buf[:, start : start + width] = jnp.dot(
            left_buf[...], right, preferred_element_type=jnp.float32
        )
        if index == 1:
            offset_copy.wait()
        if index:
            pack(ready, start // LANE)
            ready = max(ready, start // LANE)
    pack(ready, samples // LANE)
    pack(0, 1)


def project(proj, tiles, owner, lengths, devices):
    views, rows, footprint = proj.shape
    blocks, depth, samples = tiles.shape
    owned = rows // devices
    chunks = column_chunks(samples)
    half_rows = devices // 2 * rows_per_owner(owned) + owned
    shape = pltpu.VMEM((half_rows, LANE), jnp.float32)
    inputs = [pltpu.with_memory_space_constraint(x, pltpu.HBM) for x in (owner, lengths, proj, tiles)]

    def kernel(*refs):
        project_kernel(devices, *refs)

    vmem = pl.BlockSpec(memory_space=pltpu.VMEM)
    hbm = pl.BlockSpec(memory_space=pltpu.HBM)
    return pl.pallas_call(
        kernel,
        out_shape=(shape, shape),
        in_specs=[hbm] * 4,
        out_specs=(vmem, vmem),
        scratch_shapes=[
            pltpu.VMEM(owner.shape, jnp.int32),
            pltpu.VMEM(lengths.shape, jnp.int32),
            pltpu.VMEM((devices, LANE), jnp.int32),
            pltpu.SMEM((devices, LANE), jnp.int32),
            pltpu.VMEM(proj.shape, jnp.bfloat16),
            pltpu.VMEM(tiles.shape, jnp.bfloat16),
            pltpu.VMEM((rows, views * footprint), jnp.bfloat16),
            pltpu.VMEM((rows, samples), jnp.float32),
            pltpu.SemaphoreType.DMA((2,)),
            pltpu.SemaphoreType.DMA,
            pltpu.SemaphoreType.DMA,
            pltpu.SemaphoreType.DMA((len(chunks),)),
        ],
        compiler_params=pltpu.CompilerParams(vmem_limit_bytes=40 << 20),
        cost_estimate=pl.CostEstimate(
            flops=2 * rows * views * footprint * samples,
            bytes_accessed=2 * (proj.size + tiles.size),
            transcendentals=0,
        ),
        name="project",
    )(*inputs)


def prepare_kernel(
    devices, owner_hbm, lengths_hbm, unpick_ref, inner_ref, outer_ref, coarse_ref, fine_ref,
    owner_s, lengths_s, sem,
):
    owned, samples = inner_ref.shape
    blocks = samples // LANE
    packed = unpick_ref.shape[1]
    distances = coarse_ref.shape[0]
    group = lax.axis_index("chord")
    me = lax.axis_index("view")
    copies = [
        pltpu.make_async_copy(owner_hbm, owner_s, sem.at[0]),
        pltpu.make_async_copy(lengths_hbm, lengths_s, sem.at[1]),
    ]
    for copy in copies:
        copy.start()
    across = lax.broadcasted_iota(jnp.int32, (COLS, COLS), 1)
    gap = (across - lax.broadcasted_iota(jnp.int32, (COLS, COLS), 0)).astype(jnp.float32) + 0.5
    for index in range(distances):
        exact = 1.0 / (gap + float((index - distances // 2) * COLS))
        coarse = exact.astype(jnp.bfloat16)
        coarse_ref[index] = coarse
        fine_ref[index] = (exact - coarse.astype(jnp.float32)).astype(jnp.bfloat16)
    for copy in copies:
        copy.wait()
    lengths = [lengths_s[group, owner_s[group, me * owned + index]] for index in range(owned)]

    sub = lax.broadcasted_iota(jnp.int32, (owned, LANE), 0)
    lane = lax.broadcasted_iota(jnp.int32, (owned, LANE), 1)
    length = jnp.zeros((owned, LANE), jnp.int32)
    for index in range(owned):
        length = jnp.where(sub == index, lengths[index], length)
    rank = jnp.zeros((owned, LANE), jnp.int32)
    for index in range(owned):
        ahead = (lengths[index] > length) | ((lengths[index] == length) & (index < sub))
        rank = rank + jnp.where(ahead, 1, 0)
    reach = (length + (LANE - 1)) >> 7
    rows = []
    for block in range(blocks):
        offset = jnp.int32(0)
        for index in range(owned):
            offset = offset + jnp.minimum((lengths[index] + (LANE - 1)) >> 7, block)
        hit = (lane == rank + offset) & (reach > block)
        rows.append(jnp.where(hit, 1.0, 0.0))
    unpick_ref[...] = jnp.concatenate(rows, axis=0)[:, :packed].astype(jnp.bfloat16)

    long = length.astype(jnp.float32)
    for block in range(blocks):
        spot = (lane + block * LANE).astype(jnp.float32) + 0.5
        inside = spot < long
        weight = jnp.sqrt(jnp.where(inside, spot * (long - spot), 1.0))
        columns = slice(block * LANE, (block + 1) * LANE)
        inner_ref[:, columns] = jnp.where(inside, weight, 0.0)
        outer_ref[:, columns] = jnp.where(inside, 1.0 / (math.pi * weight), 0.0)


def prepare(owner, lengths, devices, owned, samples, packed):
    distances = 2 * (samples // COLS) - 1
    inputs = [pltpu.with_memory_space_constraint(x, pltpu.HBM) for x in (owner, lengths)]
    vmem = pl.BlockSpec(memory_space=pltpu.VMEM)

    def kernel(*refs):
        prepare_kernel(devices, *refs)

    return pl.pallas_call(
        kernel,
        out_shape=(
            pltpu.VMEM((owned * samples // LANE, packed), jnp.bfloat16),
            pltpu.VMEM((owned, samples), jnp.float32),
            pltpu.VMEM((owned, samples), jnp.float32),
            pltpu.VMEM((distances, COLS, COLS), jnp.bfloat16),
            pltpu.VMEM((distances, COLS, COLS), jnp.bfloat16),
        ),
        in_specs=[pl.BlockSpec(memory_space=pltpu.HBM)] * 2,
        out_specs=(vmem,) * 5,
        scratch_shapes=[
            pltpu.SMEM(owner.shape, jnp.int32),
            pltpu.SMEM(lengths.shape, jnp.int32),
            pltpu.SemaphoreType.DMA((2,)),
        ],
        compiler_params=pltpu.CompilerParams(vmem_limit_bytes=32 << 20),
        cost_estimate=pl.CostEstimate(flops=1 << 22, bytes_accessed=1 << 21, transcendentals=1 << 19),
        name="prepare",
    )(*inputs)


def invert_kernel(mine_ref, other_ref, unpick_ref, inner_ref, outer_ref, coarse_ref, fine_ref, out_ref):
    owned, samples = inner_ref.shape
    bins = samples // COLS
    per_bin = COLS // LANE

    def halves(value):
        coarse = value.astype(jnp.bfloat16)
        return coarse, (value - coarse.astype(jnp.float32)).astype(jnp.bfloat16)

    both = jnp.concatenate(halves(mine_ref[...] + other_ref[...]), axis=1)
    spread = jnp.dot(unpick_ref[...], both, preferred_element_type=jnp.float32)
    spread = spread[:, :LANE] + spread[:, LANE:]
    left = []
    for part in range(bins):
        sums = jnp.concatenate(
            [spread[block * owned : (block + 1) * owned] for block in range(part * per_bin, (part + 1) * per_bin)],
            axis=1,
        )
        scaled = inner_ref[:, part * COLS : (part + 1) * COLS] * sums
        left.append(jnp.concatenate(halves(scaled), axis=0))
    image = [None] * bins
    for shift in range(1 - bins, bins):
        first, last = max(0, -shift), min(bins, bins - shift)
        stack = jnp.concatenate(left[first:last], axis=0)
        product = jnp.dot(
            stack, coarse_ref[shift + bins - 1], preferred_element_type=jnp.float32
        ) + jnp.dot(stack, fine_ref[shift + bins - 1], preferred_element_type=jnp.float32)
        for place, part in enumerate(range(first, last)):
            base = place * 2 * owned
            term = product[base : base + owned] + product[base + owned : base + 2 * owned]
            to = part + shift
            image[to] = term if image[to] is None else image[to] + term
    for part in range(bins):
        columns = slice(part * COLS, (part + 1) * COLS)
        out_ref[0, :, columns] = image[part] * outer_ref[:, columns]


def invert(mine, other, prepared, owned, samples):
    vmem = pl.BlockSpec(memory_space=pltpu.VMEM)
    return pl.pallas_call(
        invert_kernel,
        out_shape=jax.ShapeDtypeStruct((1, owned, samples), jnp.float32),
        in_specs=[vmem] * 7,
        out_specs=vmem,
        compiler_params=pltpu.CompilerParams(vmem_limit_bytes=32 << 20),
        name="invert",
    )(mine, other, *prepared)


def per_device(proj, tiles, owner, lengths):
    devices = lax.axis_size("view")
    rows = proj.shape[1]
    samples = tiles.shape[2]
    owned = rows // devices
    packed = rows_per_owner(owned)
    keep, send = project(proj, tiles, owner, lengths, devices)
    prepared = prepare(owner, lengths, devices, owned, samples, packed)
    held = devices // 2
    steps = exchange_pairs(devices)
    for pairs in steps[:-1]:
        total = keep + lax.ppermute(send, "view", pairs)
        held //= 2
        keep, send = total[: held * packed], total[held * packed : 2 * held * packed]
    other = lax.ppermute(send, "view", steps[-1])
    return invert(keep, other, prepared, owned, samples)


def solution(mesh):
    placed = (P("view", "chord", None), P("view", None, None), P(), P())
    return jax.shard_map(
        per_device, mesh=mesh, in_specs=placed, out_specs=P("chord", "view", None), check_vma=False
    )
```

```python
import math

import jax
import jax.numpy as jnp
from jax import lax
from jax.experimental import pallas as pl
from jax.experimental.pallas import tpu as pltpu
from jax.sharding import PartitionSpec as P

LANE = 128
OWNED_SAMPLES = 4608
COLS = 256


def side(place):
    return (place ^ (place >> 1) ^ (place >> 2)) & 1


def exchange_pairs(devices):
    steps = [[place ^ 1 for place in range(devices)]]
    for first, second in ((3, 5), (5, 3)):
        steps.append([place ^ (second if side(place) else first) for place in range(devices)])
    step = 8
    while step < devices:
        steps.append([place ^ (step | 1) for place in range(devices)])
        step *= 2
    return [list(enumerate(partners)) for partners in steps]


def slot_of(place, me, devices):
    distance = place ^ me
    steps = devices.bit_length() - 1
    first = distance & 1
    slot = jnp.zeros_like(distance)
    for step in range(1, steps):
        bit = (distance >> step) & 1
        first = first ^ bit
        if step > 2:
            slot = slot | (bit << (steps - 1 - step))
    near, far = (distance >> 1) & 1, (distance >> 2) & 1
    swap = side(me) ^ first
    early = jnp.where(swap == 1, far, near)
    late = jnp.where(swap == 1, near, far)
    return slot | (first << (steps - 1)) | (early << (steps - 2)) | (late << (steps - 3))


def rows_per_owner(owned):
    rows = (OWNED_SAMPLES + owned * (LANE - 1)) // LANE
    return -(-rows // 4) * 4


def column_chunks(samples):
    return [(0, samples // 2), (samples // 2, samples // 2)]


def project_kernel(
    devices, owner_hbm, lengths_hbm, proj_hbm, tiles_hbm, keep_ref, send_ref,
    owner_v, lengths_v, offset_v, offset_s, proj_buf, tile_buf, left_buf, sums_buf,
    small_sem, offset_sem, proj_sem, tile_sem,
):
    views, rows, footprint = proj_buf.shape
    samples = tile_buf.shape[2]
    chunks = column_chunks(samples)
    owned = rows // devices
    group = lax.axis_index("chord")
    me = lax.axis_index("view")
    small = [
        pltpu.make_async_copy(source, kept, small_sem.at[index])
        for index, (source, kept) in enumerate(
            [(owner_hbm, owner_v), (lengths_hbm, lengths_v)]
        )
    ]
    for copy in small:
        copy.start()
    proj_copy = pltpu.make_async_copy(proj_hbm, proj_buf, proj_sem)
    proj_copy.start()
    tile_copies = []
    for index, (start, width) in enumerate(chunks):
        columns = pl.ds(start, width)
        copy = pltpu.make_async_copy(
            tiles_hbm.at[:, :, columns], tile_buf.at[:, :, columns], tile_sem.at[index]
        )
        copy.start()
        tile_copies.append(copy)

    keep_ref[...] = jnp.zeros_like(keep_ref)
    send_ref[...] = jnp.zeros_like(send_ref)
    for copy in small:
        copy.wait()
    down = lax.broadcasted_iota(jnp.int32, (rows, rows), 0)
    across = lax.broadcasted_iota(jnp.int32, (rows, rows), 1)
    diagonal = down == across

    def turned(row):
        spread = jnp.broadcast_to(row.astype(jnp.float32), (rows, rows))
        return jnp.sum(jnp.where(diagonal, spread, 0.0), axis=1, keepdims=True)

    lengths = lengths_v[pl.ds(group, 1), :]
    order = turned(owner_v[pl.ds(group, 1), :])
    hit = order == across.astype(jnp.float32)
    position = jnp.sum(jnp.where(hit, down.astype(jnp.float32), 0.0), axis=0, keepdims=True)
    position = position.astype(jnp.int32)
    place = position // owned
    slot = slot_of(place, me, devices)

    reach = turned((lengths + (LANE - 1)) // LANE)
    block_index = lax.broadcasted_iota(jnp.int32, (rows, LANE), 1).astype(jnp.float32)
    before = jnp.where(block_index < samples // LANE, jnp.minimum(block_index, reach), 0.0)
    member = lax.broadcasted_iota(jnp.int32, (devices, rows), 0) == slot
    offset_v[...] = jnp.dot(
        jnp.where(member, 1.0, 0.0).astype(jnp.bfloat16),
        before.astype(jnp.bfloat16),
        preferred_element_type=jnp.float32,
    ).astype(jnp.int32)
    offset_copy = pltpu.make_async_copy(offset_v, offset_s, offset_sem)
    offset_copy.start()

    key = (slot * (samples + 1) + (samples - lengths)) * owned + (
        position - place * owned
    )
    key = key.astype(jnp.float32)
    target = jnp.sum(jnp.where(turned(key) < key, 1.0, 0.0), axis=0, keepdims=True)
    pick = jnp.where(down.astype(jnp.float32) == target, 1.0, 0.0).astype(jnp.bfloat16)

    def each_slot(body):
        if devices <= 16:
            for index in range(devices):
                body(index)
        else:
            pl.loop(0, devices)(body)

    proj_copy.wait()
    for view in range(views):
        moved = jnp.dot(pick, proj_buf[view], preferred_element_type=jnp.float32)
        left_buf[:, view * footprint : (view + 1) * footprint] = moved.astype(jnp.bfloat16)

    packed = rows_per_owner(owned)
    half = devices // 2

    def put(slot_index, offset, value):
        def to(out_ref, base):
            out_ref[pl.ds(base + offset, owned), :] = value

        if isinstance(slot_index, int):
            if slot_index < half:
                to(keep_ref, slot_index * packed)
            else:
                to(send_ref, (slot_index - half) * packed)
        else:
            pl.when(slot_index < half)(lambda: to(keep_ref, slot_index * packed))
            pl.when(slot_index >= half)(lambda: to(send_ref, (slot_index - half) * packed))

    def pack(first, last):
        def one(slot_index):
            for block in range(first, last):
                value = sums_buf[pl.ds(slot_index * owned, owned), block * LANE : (block + 1) * LANE]
                put(slot_index, offset_s[slot_index, block] if block else 0, value)

        each_slot(one)

    ready = 1
    for index, (start, width) in enumerate(chunks):
        tile_copies[index].wait()
        right = tile_buf[:, :, start : start + width].reshape(views * footprint, width)
        sums_buf[:, start : start + width] = jnp.dot(
            left_buf[...], right, preferred_element_type=jnp.float32
        )
        if index == 1:
            offset_copy.wait()
        if index:
            pack(ready, start // LANE)
            ready = max(ready, start // LANE)
    pack(ready, samples // LANE)
    pack(0, 1)


def project(proj, tiles, owner, lengths, devices):
    views, rows, footprint = proj.shape
    blocks, depth, samples = tiles.shape
    owned = rows // devices
    chunks = column_chunks(samples)
    half_rows = devices // 2 * rows_per_owner(owned) + owned
    shape = pltpu.VMEM((half_rows, LANE), jnp.float32)
    inputs = [pltpu.with_memory_space_constraint(x, pltpu.HBM) for x in (owner, lengths, proj, tiles)]

    def kernel(*refs):
        project_kernel(devices, *refs)

    vmem = pl.BlockSpec(memory_space=pltpu.VMEM)
    hbm = pl.BlockSpec(memory_space=pltpu.HBM)
    return pl.pallas_call(
        kernel,
        out_shape=(shape, shape),
        in_specs=[hbm] * 4,
        out_specs=(vmem, vmem),
        scratch_shapes=[
            pltpu.VMEM(owner.shape, jnp.int32),
            pltpu.VMEM(lengths.shape, jnp.int32),
            pltpu.VMEM((devices, LANE), jnp.int32),
            pltpu.SMEM((devices, LANE), jnp.int32),
            pltpu.VMEM(proj.shape, jnp.bfloat16),
            pltpu.VMEM(tiles.shape, jnp.bfloat16),
            pltpu.VMEM((rows, views * footprint), jnp.bfloat16),
            pltpu.VMEM((rows, samples), jnp.float32),
            pltpu.SemaphoreType.DMA((2,)),
            pltpu.SemaphoreType.DMA,
            pltpu.SemaphoreType.DMA,
            pltpu.SemaphoreType.DMA((len(chunks),)),
        ],
        compiler_params=pltpu.CompilerParams(vmem_limit_bytes=40 << 20),
        cost_estimate=pl.CostEstimate(
            flops=2 * rows * views * footprint * samples,
            bytes_accessed=2 * (proj.size + tiles.size),
            transcendentals=0,
        ),
        name="project",
    )(*inputs)


def prepare_kernel(
    devices, owner_hbm, lengths_hbm, offset_ref, rank_ref, inner_ref, outer_ref, coarse_ref, fine_ref,
    owner_s, lengths_s, sem,
):
    owned, samples = inner_ref.shape
    blocks = samples // LANE
    distances = coarse_ref.shape[0]
    group = lax.axis_index("chord")
    me = lax.axis_index("view")
    copies = [
        pltpu.make_async_copy(owner_hbm, owner_s, sem.at[0]),
        pltpu.make_async_copy(lengths_hbm, lengths_s, sem.at[1]),
    ]
    for copy in copies:
        copy.start()
    across = lax.broadcasted_iota(jnp.int32, (COLS, COLS), 1)
    gap = (across - lax.broadcasted_iota(jnp.int32, (COLS, COLS), 0)).astype(jnp.float32) + 0.5
    for index in range(distances):
        exact = 1.0 / (gap + float((index - distances // 2) * COLS))
        coarse = exact.astype(jnp.bfloat16)
        coarse_ref[index] = coarse
        fine_ref[index] = (exact - coarse.astype(jnp.float32)).astype(jnp.bfloat16)
    for copy in copies:
        copy.wait()
    lengths = [lengths_s[group, owner_s[group, me * owned + index]] for index in range(owned)]

    sub = lax.broadcasted_iota(jnp.int32, (owned, LANE), 0)
    lane = lax.broadcasted_iota(jnp.int32, (owned, LANE), 1)
    length = jnp.zeros((owned, LANE), jnp.int32)
    for index in range(owned):
        length = jnp.where(sub == index, lengths[index], length)
    rank = jnp.zeros((owned, LANE), jnp.int32)
    for index in range(owned):
        ahead = (lengths[index] > length) | ((lengths[index] == length) & (index < sub))
        rank = rank + jnp.where(ahead, 1, 0)
    rank_ref[...] = rank
    for block in range(blocks):
        offset = jnp.int32(0)
        for index in range(owned):
            offset = offset + jnp.minimum((lengths[index] + (LANE - 1)) >> 7, block)
        offset_ref[0, block] = offset

    long = length.astype(jnp.float32)
    for block in range(blocks):
        spot = (lane + block * LANE).astype(jnp.float32) + 0.5
        inside = spot < long
        weight = jnp.sqrt(jnp.where(inside, spot * (long - spot), 1.0))
        columns = slice(block * LANE, (block + 1) * LANE)
        inner_ref[:, columns] = jnp.where(inside, weight, 0.0)
        outer_ref[:, columns] = jnp.where(inside, 1.0 / (math.pi * weight), 0.0)


def prepare(owner, lengths, devices, owned, samples):
    distances = 2 * (samples // COLS) - 1
    inputs = [pltpu.with_memory_space_constraint(x, pltpu.HBM) for x in (owner, lengths)]
    vmem = pl.BlockSpec(memory_space=pltpu.VMEM)

    def kernel(*refs):
        prepare_kernel(devices, *refs)

    return pl.pallas_call(
        kernel,
        out_shape=(
            pltpu.SMEM((1, samples // LANE), jnp.int32),
            pltpu.VMEM((owned, LANE), jnp.int32),
            pltpu.VMEM((owned, samples), jnp.float32),
            pltpu.VMEM((owned, samples), jnp.float32),
            pltpu.VMEM((distances, COLS, COLS), jnp.bfloat16),
            pltpu.VMEM((distances, COLS, COLS), jnp.bfloat16),
        ),
        in_specs=[pl.BlockSpec(memory_space=pltpu.HBM)] * 2,
        out_specs=(pl.BlockSpec(memory_space=pltpu.SMEM),) + (vmem,) * 5,
        scratch_shapes=[
            pltpu.SMEM(owner.shape, jnp.int32),
            pltpu.SMEM(lengths.shape, jnp.int32),
            pltpu.SemaphoreType.DMA((2,)),
        ],
        compiler_params=pltpu.CompilerParams(vmem_limit_bytes=32 << 20),
        cost_estimate=pl.CostEstimate(flops=1 << 22, bytes_accessed=1 << 21, transcendentals=1 << 19),
        name="prepare",
    )(*inputs)


def invert_kernel(
    mine_ref, other_ref, offset_ref, rank_ref, inner_ref, outer_ref, coarse_ref, fine_ref, out_ref, sum_buf
):
    owned, samples = inner_ref.shape
    bins = samples // COLS
    per_bin = COLS // LANE

    def halves(value):
        coarse = value.astype(jnp.bfloat16)
        return coarse, (value - coarse.astype(jnp.float32)).astype(jnp.bfloat16)

    packed = mine_ref.shape[0]
    sum_buf[0:packed, :] = mine_ref[...] + other_ref[...]
    rank = rank_ref[...]

    def chord_rows(block):
        ordered = sum_buf[pl.ds(offset_ref[0, block], owned), :]
        return jnp.take_along_axis(ordered, rank, axis=0)

    left = []
    for part in range(bins):
        sums = jnp.concatenate(
            [chord_rows(block) for block in range(part * per_bin, (part + 1) * per_bin)], axis=1
        )
        weight = inner_ref[:, part * COLS : (part + 1) * COLS]
        scaled = jnp.where(weight > 0.0, weight * sums, 0.0)
        left.append(jnp.concatenate(halves(scaled), axis=0))
    image = [None] * bins
    for shift in range(1 - bins, bins):
        first, last = max(0, -shift), min(bins, bins - shift)
        stack = jnp.concatenate(left[first:last], axis=0)
        product = jnp.dot(
            stack, coarse_ref[shift + bins - 1], preferred_element_type=jnp.float32
        ) + jnp.dot(stack, fine_ref[shift + bins - 1], preferred_element_type=jnp.float32)
        for place, part in enumerate(range(first, last)):
            base = place * 2 * owned
            term = product[base : base + owned] + product[base + owned : base + 2 * owned]
            to = part + shift
            image[to] = term if image[to] is None else image[to] + term
    for part in range(bins):
        columns = slice(part * COLS, (part + 1) * COLS)
        out_ref[0, :, columns] = image[part] * outer_ref[:, columns]


def invert(mine, other, prepared, owned, samples):
    vmem = pl.BlockSpec(memory_space=pltpu.VMEM)
    return pl.pallas_call(
        invert_kernel,
        out_shape=jax.ShapeDtypeStruct((1, owned, samples), jnp.float32),
        in_specs=[vmem, vmem, pl.BlockSpec(memory_space=pltpu.SMEM)] + [vmem] * 5,
        out_specs=vmem,
        scratch_shapes=[pltpu.VMEM((mine.shape[0] + owned, LANE), jnp.float32)],
        compiler_params=pltpu.CompilerParams(vmem_limit_bytes=32 << 20),
        name="invert",
    )(mine, other, *prepared)


def per_device(proj, tiles, owner, lengths):
    devices = lax.axis_size("view")
    rows = proj.shape[1]
    samples = tiles.shape[2]
    owned = rows // devices
    packed = rows_per_owner(owned)
    keep, send = project(proj, tiles, owner, lengths, devices)
    prepared = prepare(owner, lengths, devices, owned, samples)
    held = devices // 2
    steps = exchange_pairs(devices)
    for pairs in steps[:-1]:
        other = lax.ppermute(send, "view", pairs)
        held //= 2
        middle = held * packed
        keep, send = keep[:middle] + other[:middle], keep[middle : 2 * middle] + other[middle : 2 * middle]
    other = lax.ppermute(send, "view", steps[-1])
    return invert(keep, other, prepared, owned, samples)


def solution(mesh):
    placed = (P("view", "chord", None), P("view", None, None), P(), P())
    return jax.shard_map(
        per_device, mesh=mesh, in_specs=placed, out_specs=P("chord", "view", None), check_vma=False
    )
```

```python
import math

import jax
import jax.numpy as jnp
from jax import lax
from jax.experimental import pallas as pl
from jax.experimental.pallas import tpu as pltpu
from jax.sharding import PartitionSpec as P

LANE = 128
OWNED_SAMPLES = 4608
COLS = 256


def side(place):
    return (place ^ (place >> 1) ^ (place >> 2)) & 1


def exchange_pairs(devices):
    steps = [[place ^ 1 for place in range(devices)]]
    for first, second in ((3, 5), (5, 3)):
        steps.append([place ^ (second if side(place) else first) for place in range(devices)])
    step = 8
    while step < devices:
        steps.append([place ^ (step | 1) for place in range(devices)])
        step *= 2
    return [list(enumerate(partners)) for partners in steps]


def slot_of(place, me, devices):
    distance = place ^ me
    steps = devices.bit_length() - 1
    first = distance & 1
    slot = jnp.zeros_like(distance)
    for step in range(1, steps):
        bit = (distance >> step) & 1
        first = first ^ bit
        if step > 2:
            slot = slot | (bit << (steps - 1 - step))
    near, far = (distance >> 1) & 1, (distance >> 2) & 1
    swap = side(me) ^ first
    early = jnp.where(swap == 1, far, near)
    late = jnp.where(swap == 1, near, far)
    return slot | (first << (steps - 1)) | (early << (steps - 2)) | (late << (steps - 3))


def rows_per_owner(owned):
    rows = (OWNED_SAMPLES + owned * (LANE - 1)) // LANE
    return -(-rows // 4) * 4


def column_chunks(samples):
    return [(0, samples // 2), (samples // 2, samples // 2)]


def project_kernel(
    devices, owner_hbm, lengths_hbm, proj_hbm, tiles_hbm, keep_late_ref, keep_ref, send_late_ref, send_ref,
    owner_v, lengths_v, offset_v, offset_s, proj_buf, tile_buf, left_buf, sums_buf,
    small_sem, offset_sem, proj_sem, tile_sem,
):
    views, rows, footprint = proj_buf.shape
    samples = tile_buf.shape[2]
    chunks = column_chunks(samples)
    owned = rows // devices
    group = lax.axis_index("chord")
    me = lax.axis_index("view")
    small = [
        pltpu.make_async_copy(source, kept, small_sem.at[index])
        for index, (source, kept) in enumerate(
            [(owner_hbm, owner_v), (lengths_hbm, lengths_v)]
        )
    ]
    for copy in small:
        copy.start()
    proj_copy = pltpu.make_async_copy(proj_hbm, proj_buf, proj_sem)
    proj_copy.start()
    tile_copies = []
    for index, (start, width) in enumerate(chunks):
        columns = pl.ds(start, width)
        copy = pltpu.make_async_copy(
            tiles_hbm.at[:, :, columns], tile_buf.at[:, :, columns], tile_sem.at[index]
        )
        copy.start()
        tile_copies.append(copy)

    quarters = [keep_late_ref, keep_ref, send_late_ref, send_ref]
    for ref in quarters:
        ref[...] = jnp.zeros_like(ref)
    for copy in small:
        copy.wait()
    down = lax.broadcasted_iota(jnp.int32, (rows, rows), 0)
    across = lax.broadcasted_iota(jnp.int32, (rows, rows), 1)
    diagonal = down == across

    def turned(row):
        spread = jnp.broadcast_to(row.astype(jnp.float32), (rows, rows))
        return jnp.sum(jnp.where(diagonal, spread, 0.0), axis=1, keepdims=True)

    lengths = lengths_v[pl.ds(group, 1), :]
    order = turned(owner_v[pl.ds(group, 1), :])
    hit = order == across.astype(jnp.float32)
    position = jnp.sum(jnp.where(hit, down.astype(jnp.float32), 0.0), axis=0, keepdims=True)
    position = position.astype(jnp.int32)
    place = position // owned
    slot = slot_of(place, me, devices)

    reach = turned((lengths + (LANE - 1)) // LANE)
    block_index = lax.broadcasted_iota(jnp.int32, (rows, LANE), 1).astype(jnp.float32)
    before = jnp.where(block_index < samples // LANE, jnp.minimum(block_index, reach), 0.0)
    member = lax.broadcasted_iota(jnp.int32, (devices, rows), 0) == slot
    offset_v[...] = jnp.dot(
        jnp.where(member, 1.0, 0.0).astype(jnp.bfloat16),
        before.astype(jnp.bfloat16),
        preferred_element_type=jnp.float32,
    ).astype(jnp.int32)
    offset_copy = pltpu.make_async_copy(offset_v, offset_s, offset_sem)
    offset_copy.start()

    key = (slot * (samples + 1) + (samples - lengths)) * owned + (
        position - place * owned
    )
    key = key.astype(jnp.float32)
    target = jnp.sum(jnp.where(turned(key) < key, 1.0, 0.0), axis=0, keepdims=True)
    pick = jnp.where(down.astype(jnp.float32) == target, 1.0, 0.0).astype(jnp.bfloat16)

    def each_slot(body):
        if devices <= 16:
            for index in range(devices):
                body(index)
        else:
            pl.loop(0, devices)(body)

    proj_copy.wait()
    for view in range(views):
        moved = jnp.dot(pick, proj_buf[view], preferred_element_type=jnp.float32)
        left_buf[:, view * footprint : (view + 1) * footprint] = moved.astype(jnp.bfloat16)

    packed = rows_per_owner(owned)
    quarter = devices // 4

    def put(slot_index, offset, value):
        def to(out_ref, index):
            out_ref[pl.ds(index * packed + offset, owned), :] = value

        if isinstance(slot_index, int):
            to(quarters[slot_index // quarter], slot_index % quarter)
        else:
            for number, ref in enumerate(quarters):
                here = slot_index // quarter == number
                pl.when(here)(lambda ref=ref, number=number: to(ref, slot_index - number * quarter))

    def pack(first, last):
        def one(slot_index):
            for block in range(first, last):
                value = sums_buf[pl.ds(slot_index * owned, owned), block * LANE : (block + 1) * LANE]
                put(slot_index, offset_s[slot_index, block] if block else 0, value)

        each_slot(one)

    ready = 1
    for index, (start, width) in enumerate(chunks):
        tile_copies[index].wait()
        right = tile_buf[:, :, start : start + width].reshape(views * footprint, width)
        sums_buf[:, start : start + width] = jnp.dot(
            left_buf[...], right, preferred_element_type=jnp.float32
        )
        if index == 1:
            offset_copy.wait()
        if index:
            pack(ready, start // LANE)
            ready = max(ready, start // LANE)
    pack(ready, samples // LANE)
    pack(0, 1)


def project(proj, tiles, owner, lengths, devices):
    views, rows, footprint = proj.shape
    blocks, depth, samples = tiles.shape
    owned = rows // devices
    chunks = column_chunks(samples)
    quarter_rows = devices // 4 * rows_per_owner(owned) + owned
    shape = pltpu.VMEM((quarter_rows, LANE), jnp.float32)
    inputs = [pltpu.with_memory_space_constraint(x, pltpu.HBM) for x in (owner, lengths, proj, tiles)]

    def kernel(*refs):
        project_kernel(devices, *refs)

    vmem = pl.BlockSpec(memory_space=pltpu.VMEM)
    hbm = pl.BlockSpec(memory_space=pltpu.HBM)
    return pl.pallas_call(
        kernel,
        out_shape=(shape,) * 4,
        in_specs=[hbm] * 4,
        out_specs=(vmem,) * 4,
        scratch_shapes=[
            pltpu.VMEM(owner.shape, jnp.int32),
            pltpu.VMEM(lengths.shape, jnp.int32),
            pltpu.VMEM((devices, LANE), jnp.int32),
            pltpu.SMEM((devices, LANE), jnp.int32),
            pltpu.VMEM(proj.shape, jnp.bfloat16),
            pltpu.VMEM(tiles.shape, jnp.bfloat16),
            pltpu.VMEM((rows, views * footprint), jnp.bfloat16),
            pltpu.VMEM((rows, samples), jnp.float32),
            pltpu.SemaphoreType.DMA((2,)),
            pltpu.SemaphoreType.DMA,
            pltpu.SemaphoreType.DMA,
            pltpu.SemaphoreType.DMA((len(chunks),)),
        ],
        compiler_params=pltpu.CompilerParams(vmem_limit_bytes=40 << 20),
        cost_estimate=pl.CostEstimate(
            flops=2 * rows * views * footprint * samples,
            bytes_accessed=2 * (proj.size + tiles.size),
            transcendentals=0,
        ),
        name="project",
    )(*inputs)


def prepare_kernel(
    devices, owner_hbm, lengths_hbm, offset_ref, rank_ref, inner_ref, outer_ref, coarse_ref, fine_ref,
    owner_s, lengths_s, sem,
):
    owned, samples = inner_ref.shape
    blocks = samples // LANE
    distances = coarse_ref.shape[0]
    group = lax.axis_index("chord")
    me = lax.axis_index("view")
    copies = [
        pltpu.make_async_copy(owner_hbm, owner_s, sem.at[0]),
        pltpu.make_async_copy(lengths_hbm, lengths_s, sem.at[1]),
    ]
    for copy in copies:
        copy.start()
    across = lax.broadcasted_iota(jnp.int32, (COLS, COLS), 1)
    gap = (across - lax.broadcasted_iota(jnp.int32, (COLS, COLS), 0)).astype(jnp.float32) + 0.5
    for index in range(distances):
        exact = 1.0 / (gap + float((index - distances // 2) * COLS))
        coarse = exact.astype(jnp.bfloat16)
        coarse_ref[index] = coarse
        fine_ref[index] = (exact - coarse.astype(jnp.float32)).astype(jnp.bfloat16)
    for copy in copies:
        copy.wait()
    lengths = [lengths_s[group, owner_s[group, me * owned + index]] for index in range(owned)]

    sub = lax.broadcasted_iota(jnp.int32, (owned, LANE), 0)
    lane = lax.broadcasted_iota(jnp.int32, (owned, LANE), 1)
    length = jnp.zeros((owned, LANE), jnp.int32)
    for index in range(owned):
        length = jnp.where(sub == index, lengths[index], length)
    rank = jnp.zeros((owned, LANE), jnp.int32)
    for index in range(owned):
        ahead = (lengths[index] > length) | ((lengths[index] == length) & (index < sub))
        rank = rank + jnp.where(ahead, 1, 0)
    rank_ref[...] = rank
    for block in range(blocks):
        offset = jnp.int32(0)
        for index in range(owned):
            offset = offset + jnp.minimum((lengths[index] + (LANE - 1)) >> 7, block)
        offset_ref[0, block] = offset

    long = length.astype(jnp.float32)
    for block in range(blocks):
        spot = (lane + block * LANE).astype(jnp.float32) + 0.5
        inside = spot < long
        weight = jnp.sqrt(jnp.where(inside, spot * (long - spot), 1.0))
        columns = slice(block * LANE, (block + 1) * LANE)
        inner_ref[:, columns] = jnp.where(inside, weight, 0.0)
        outer_ref[:, columns] = jnp.where(inside, 1.0 / (math.pi * weight), 0.0)


def prepare(owner, lengths, devices, owned, samples):
    distances = 2 * (samples // COLS) - 1
    inputs = [pltpu.with_memory_space_constraint(x, pltpu.HBM) for x in (owner, lengths)]
    vmem = pl.BlockSpec(memory_space=pltpu.VMEM)

    def kernel(*refs):
        prepare_kernel(devices, *refs)

    return pl.pallas_call(
        kernel,
        out_shape=(
            pltpu.SMEM((1, samples // LANE), jnp.int32),
            pltpu.VMEM((owned, LANE), jnp.int32),
            pltpu.VMEM((owned, samples), jnp.float32),
            pltpu.VMEM((owned, samples), jnp.float32),
            pltpu.VMEM((distances, COLS, COLS), jnp.bfloat16),
            pltpu.VMEM((distances, COLS, COLS), jnp.bfloat16),
        ),
        in_specs=[pl.BlockSpec(memory_space=pltpu.HBM)] * 2,
        out_specs=(pl.BlockSpec(memory_space=pltpu.SMEM),) + (vmem,) * 5,
        scratch_shapes=[
            pltpu.SMEM(owner.shape, jnp.int32),
            pltpu.SMEM(lengths.shape, jnp.int32),
            pltpu.SemaphoreType.DMA((2,)),
        ],
        compiler_params=pltpu.CompilerParams(vmem_limit_bytes=32 << 20),
        cost_estimate=pl.CostEstimate(flops=1 << 22, bytes_accessed=1 << 21, transcendentals=1 << 19),
        name="prepare",
    )(*inputs)


def invert_kernel(
    mine_ref, other_ref, offset_ref, rank_ref, inner_ref, outer_ref, coarse_ref, fine_ref, out_ref, sum_buf
):
    owned, samples = inner_ref.shape
    bins = samples // COLS
    per_bin = COLS // LANE

    def halves(value):
        coarse = value.astype(jnp.bfloat16)
        return coarse, (value - coarse.astype(jnp.float32)).astype(jnp.bfloat16)

    packed = mine_ref.shape[0]
    sum_buf[0:packed, :] = mine_ref[...] + other_ref[...]
    rank = rank_ref[...]

    def chord_rows(block):
        ordered = sum_buf[pl.ds(offset_ref[0, block], owned), :]
        return jnp.take_along_axis(ordered, rank, axis=0)

    left = []
    for part in range(bins):
        sums = jnp.concatenate(
            [chord_rows(block) for block in range(part * per_bin, (part + 1) * per_bin)], axis=1
        )
        weight = inner_ref[:, part * COLS : (part + 1) * COLS]
        scaled = jnp.where(weight > 0.0, weight * sums, 0.0)
        left.append(jnp.concatenate(halves(scaled), axis=0))
    image = [None] * bins
    for shift in range(1 - bins, bins):
        first, last = max(0, -shift), min(bins, bins - shift)
        stack = jnp.concatenate(left[first:last], axis=0)
        product = jnp.dot(
            stack, coarse_ref[shift + bins - 1], preferred_element_type=jnp.float32
        ) + jnp.dot(stack, fine_ref[shift + bins - 1], preferred_element_type=jnp.float32)
        for place, part in enumerate(range(first, last)):
            base = place * 2 * owned
            term = product[base : base + owned] + product[base + owned : base + 2 * owned]
            to = part + shift
            image[to] = term if image[to] is None else image[to] + term
    for part in range(bins):
        columns = slice(part * COLS, (part + 1) * COLS)
        out_ref[0, :, columns] = image[part] * outer_ref[:, columns]


def invert(mine, other, prepared, owned, samples):
    vmem = pl.BlockSpec(memory_space=pltpu.VMEM)
    return pl.pallas_call(
        invert_kernel,
        out_shape=jax.ShapeDtypeStruct((1, owned, samples), jnp.float32),
        in_specs=[vmem, vmem, pl.BlockSpec(memory_space=pltpu.SMEM)] + [vmem] * 5,
        out_specs=vmem,
        scratch_shapes=[pltpu.VMEM((mine.shape[0] + owned, LANE), jnp.float32)],
        compiler_params=pltpu.CompilerParams(vmem_limit_bytes=32 << 20),
        name="invert",
    )(mine, other, *prepared)


def per_device(proj, tiles, owner, lengths):
    devices = lax.axis_size("view")
    rows = proj.shape[1]
    samples = tiles.shape[2]
    owned = rows // devices
    packed = rows_per_owner(owned)
    keep_late, keep, send_late, send = project(proj, tiles, owner, lengths, devices)
    prepared = prepare(owner, lengths, devices, owned, samples)
    *steps, last_step = exchange_pairs(devices)

    def total(terms, place, count):
        first, *rest = [array[base + place * packed : base + (place + count) * packed] for array, base in terms]
        for value in rest:
            first = first + value
        return first

    held = devices // 4
    kept, kept_late = [(keep, 0)], [(keep_late, 0)]
    for pairs in steps:
        other, other_late = lax.ppermute(send, "view", pairs), lax.ppermute(send_late, "view", pairs)
        kept.append((other, 0))
        if held == 1:
            break
        held //= 2
        send = total(kept, held, held)
        send, *arrays = lax.optimization_barrier((send, *[array for array, _ in kept]))
        send_late = total([(array, base) for array, (_, base) in zip(arrays, kept)], 0, held)
        kept_late.append((other_late, 0))
        kept = [(array, base + held * packed) for array, base in kept_late]
    other = lax.ppermute(total(kept, 0, 1), "view", last_step)
    other_late, other = lax.optimization_barrier((other_late, other))
    keep = total(kept_late + [(other_late, 0)], 0, 1)
    return invert(keep, other, prepared, owned, samples)


def solution(mesh):
    placed = (P("view", "chord", None), P("view", None, None), P(), P())
    return jax.shard_map(
        per_device, mesh=mesh, in_specs=placed, out_specs=P("chord", "view", None), check_vma=False
    )
```

```python
import math

import jax
import jax.numpy as jnp
from jax import lax
from jax.experimental import pallas as pl
from jax.experimental.pallas import tpu as pltpu
from jax.sharding import PartitionSpec as P

LANE = 128
OWNED_SAMPLES = 4608
COLS = 256


def side(place):
    return (place ^ (place >> 1) ^ (place >> 2)) & 1


def exchange_pairs(devices):
    steps = [[place ^ 1 for place in range(devices)]]
    for first, second in ((3, 5), (5, 3)):
        steps.append([place ^ (second if side(place) else first) for place in range(devices)])
    step = 8
    while step < devices:
        steps.append([place ^ (step | 1) for place in range(devices)])
        step *= 2
    return [list(enumerate(partners)) for partners in steps]


def slot_of(place, me, devices):
    distance = place ^ me
    steps = devices.bit_length() - 1
    first = distance & 1
    slot = jnp.zeros_like(distance)
    for step in range(1, steps):
        bit = (distance >> step) & 1
        first = first ^ bit
        if step > 2:
            slot = slot | (bit << (steps - 1 - step))
    near, far = (distance >> 1) & 1, (distance >> 2) & 1
    swap = side(me) ^ first
    early = jnp.where(swap == 1, far, near)
    late = jnp.where(swap == 1, near, far)
    return slot | (first << (steps - 1)) | (early << (steps - 2)) | (late << (steps - 3))


def rows_per_owner(owned):
    rows = (OWNED_SAMPLES + owned * (LANE - 1)) // LANE
    return -(-rows // 4) * 4


def column_chunks(samples):
    return [(0, samples // 2), (samples // 2, samples // 2)]


def project_kernel(
    devices, owner_hbm, lengths_hbm, proj_hbm, tiles_hbm, keep_ref, rest_ref, first_ref,
    owner_v, lengths_v, offset_v, offset_s, proj_buf, tile_buf, left_buf, sums_buf,
    small_sem, offset_sem, proj_sem, tile_sem,
):
    views, rows, footprint = proj_buf.shape
    samples = tile_buf.shape[2]
    chunks = column_chunks(samples)
    owned = rows // devices
    group = lax.axis_index("chord")
    me = lax.axis_index("view")
    small = [
        pltpu.make_async_copy(source, kept, small_sem.at[index])
        for index, (source, kept) in enumerate(
            [(owner_hbm, owner_v), (lengths_hbm, lengths_v)]
        )
    ]
    for copy in small:
        copy.start()
    proj_copy = pltpu.make_async_copy(proj_hbm, proj_buf, proj_sem)
    proj_copy.start()
    tile_copies = []
    for index, (start, width) in enumerate(chunks):
        columns = pl.ds(start, width)
        copy = pltpu.make_async_copy(
            tiles_hbm.at[:, :, columns], tile_buf.at[:, :, columns], tile_sem.at[index]
        )
        copy.start()
        tile_copies.append(copy)

    for ref in (keep_ref, rest_ref, first_ref):
        ref[...] = jnp.zeros_like(ref)
    for copy in small:
        copy.wait()
    down = lax.broadcasted_iota(jnp.int32, (rows, rows), 0)
    across = lax.broadcasted_iota(jnp.int32, (rows, rows), 1)
    diagonal = down == across

    def turned(row):
        spread = jnp.broadcast_to(row.astype(jnp.float32), (rows, rows))
        return jnp.sum(jnp.where(diagonal, spread, 0.0), axis=1, keepdims=True)

    lengths = lengths_v[pl.ds(group, 1), :]
    order = turned(owner_v[pl.ds(group, 1), :])
    hit = order == across.astype(jnp.float32)
    position = jnp.sum(jnp.where(hit, down.astype(jnp.float32), 0.0), axis=0, keepdims=True)
    position = position.astype(jnp.int32)
    place = position // owned
    slot = slot_of(place, me, devices)

    reach = turned((lengths + (LANE - 1)) // LANE)
    block_index = lax.broadcasted_iota(jnp.int32, (rows, LANE), 1).astype(jnp.float32)
    before = jnp.where(block_index < samples // LANE, jnp.minimum(block_index, reach), 0.0)
    member = lax.broadcasted_iota(jnp.int32, (devices, rows), 0) == slot
    offset_v[...] = jnp.dot(
        jnp.where(member, 1.0, 0.0).astype(jnp.bfloat16),
        before.astype(jnp.bfloat16),
        preferred_element_type=jnp.float32,
    ).astype(jnp.int32)
    offset_copy = pltpu.make_async_copy(offset_v, offset_s, offset_sem)
    offset_copy.start()

    key = (slot * (samples + 1) + (samples - lengths)) * owned + (
        position - place * owned
    )
    key = key.astype(jnp.float32)
    target = jnp.sum(jnp.where(turned(key) < key, 1.0, 0.0), axis=0, keepdims=True)
    pick = jnp.where(down.astype(jnp.float32) == target, 1.0, 0.0).astype(jnp.bfloat16)

    def each_slot(body):
        if devices <= 16:
            for index in range(devices):
                body(index)
        else:
            pl.loop(0, devices)(body)

    proj_copy.wait()
    for view in range(views):
        moved = jnp.dot(pick, proj_buf[view], preferred_element_type=jnp.float32)
        left_buf[:, view * footprint : (view + 1) * footprint] = moved.astype(jnp.bfloat16)

    packed = rows_per_owner(owned)
    half = devices // 2

    def put(slot_index, offset, value):
        def to(out_ref, index):
            out_ref[pl.ds(index * packed + offset, owned), :] = value

        if isinstance(slot_index, int):
            if slot_index == devices - 1:
                to(first_ref, 0)
            elif slot_index < half:
                to(keep_ref, slot_index)
            else:
                to(rest_ref, slot_index - half)
        else:
            pl.when(slot_index == devices - 1)(lambda: to(first_ref, 0))
            pl.when(slot_index < half)(lambda: to(keep_ref, slot_index))
            pl.when((slot_index >= half) & (slot_index < devices - 1))(lambda: to(rest_ref, slot_index - half))

    def pack(first, last):
        def one(slot_index):
            for block in range(first, last):
                value = sums_buf[pl.ds(slot_index * owned, owned), block * LANE : (block + 1) * LANE]
                put(slot_index, offset_s[slot_index, block] if block else 0, value)

        each_slot(one)

    ready = 1
    for index, (start, width) in enumerate(chunks):
        tile_copies[index].wait()
        right = tile_buf[:, :, start : start + width].reshape(views * footprint, width)
        sums_buf[:, start : start + width] = jnp.dot(
            left_buf[...], right, preferred_element_type=jnp.float32
        )
        if index == 1:
            offset_copy.wait()
        if index:
            pack(ready, start // LANE)
            ready = max(ready, start // LANE)
    pack(ready, samples // LANE)
    pack(0, 1)


def project(proj, tiles, owner, lengths, devices):
    views, rows, footprint = proj.shape
    blocks, depth, samples = tiles.shape
    owned = rows // devices
    chunks = column_chunks(samples)
    half = devices // 2
    shapes = [
        pltpu.VMEM((-(-(slots * rows_per_owner(owned) + owned) // 8) * 8, LANE), jnp.float32)
        for slots in (half, half - 1, 1)
    ]
    inputs = [pltpu.with_memory_space_constraint(x, pltpu.HBM) for x in (owner, lengths, proj, tiles)]

    def kernel(*refs):
        project_kernel(devices, *refs)

    vmem = pl.BlockSpec(memory_space=pltpu.VMEM)
    hbm = pl.BlockSpec(memory_space=pltpu.HBM)
    return pl.pallas_call(
        kernel,
        out_shape=tuple(shapes),
        in_specs=[hbm] * 4,
        out_specs=(vmem,) * 3,
        scratch_shapes=[
            pltpu.VMEM(owner.shape, jnp.int32),
            pltpu.VMEM(lengths.shape, jnp.int32),
            pltpu.VMEM((devices, LANE), jnp.int32),
            pltpu.SMEM((devices, LANE), jnp.int32),
            pltpu.VMEM(proj.shape, jnp.bfloat16),
            pltpu.VMEM(tiles.shape, jnp.bfloat16),
            pltpu.VMEM((rows, views * footprint), jnp.bfloat16),
            pltpu.VMEM((rows, samples), jnp.float32),
            pltpu.SemaphoreType.DMA((2,)),
            pltpu.SemaphoreType.DMA,
            pltpu.SemaphoreType.DMA,
            pltpu.SemaphoreType.DMA((len(chunks),)),
        ],
        compiler_params=pltpu.CompilerParams(vmem_limit_bytes=40 << 20),
        cost_estimate=pl.CostEstimate(
            flops=2 * rows * views * footprint * samples,
            bytes_accessed=2 * (proj.size + tiles.size),
            transcendentals=0,
        ),
        name="project",
    )(*inputs)


def chord_rows(packed_ref, offset, rank):
    ordered = packed_ref[pl.ds(offset, rank.shape[0]), :]
    return jnp.take_along_axis(ordered, rank, axis=0)


def prepare_kernel(
    devices, owner_hbm, lengths_hbm, *refs
):
    *term_refs, offset_ref, rank_ref, kept_ref, inner_ref, outer_ref, coarse_ref, fine_ref, owner_s, lengths_s, sum_buf, sem = refs
    owned, samples = inner_ref.shape
    blocks = samples // LANE
    distances = coarse_ref.shape[0]
    group = lax.axis_index("chord")
    me = lax.axis_index("view")
    copies = [
        pltpu.make_async_copy(owner_hbm, owner_s, sem.at[0]),
        pltpu.make_async_copy(lengths_hbm, lengths_s, sem.at[1]),
    ]
    for copy in copies:
        copy.start()
    across = lax.broadcasted_iota(jnp.int32, (COLS, COLS), 1)
    gap = (across - lax.broadcasted_iota(jnp.int32, (COLS, COLS), 0)).astype(jnp.float32) + 0.5
    for index in range(distances):
        exact = 1.0 / (gap + float((index - distances // 2) * COLS))
        coarse = exact.astype(jnp.bfloat16)
        coarse_ref[index] = coarse
        fine_ref[index] = (exact - coarse.astype(jnp.float32)).astype(jnp.bfloat16)
    for copy in copies:
        copy.wait()
    lengths = [lengths_s[group, owner_s[group, me * owned + index]] for index in range(owned)]

    sub = lax.broadcasted_iota(jnp.int32, (owned, LANE), 0)
    lane = lax.broadcasted_iota(jnp.int32, (owned, LANE), 1)
    length = jnp.zeros((owned, LANE), jnp.int32)
    for index in range(owned):
        length = jnp.where(sub == index, lengths[index], length)
    rank = jnp.zeros((owned, LANE), jnp.int32)
    for index in range(owned):
        ahead = (lengths[index] > length) | ((lengths[index] == length) & (index < sub))
        rank = rank + jnp.where(ahead, 1, 0)
    rank_ref[...] = rank
    packed = rows_per_owner(owned)
    kept = term_refs[0][0:packed, :]
    for ref in term_refs[1:]:
        kept = kept + ref[0:packed, :]
    sum_buf[0:packed, :] = kept
    for block in range(blocks):
        offset = jnp.int32(0)
        for index in range(owned):
            offset = offset + jnp.minimum((lengths[index] + (LANE - 1)) >> 7, block)
        offset_ref[0, block] = offset
        kept_ref[:, block * LANE : (block + 1) * LANE] = chord_rows(sum_buf, offset, rank)

    long = length.astype(jnp.float32)
    for block in range(blocks):
        spot = (lane + block * LANE).astype(jnp.float32) + 0.5
        inside = spot < long
        weight = jnp.sqrt(jnp.where(inside, spot * (long - spot), 1.0))
        columns = slice(block * LANE, (block + 1) * LANE)
        inner_ref[:, columns] = jnp.where(inside, weight, 0.0)
        outer_ref[:, columns] = jnp.where(inside, 1.0 / (math.pi * weight), 0.0)


def prepare(owner, lengths, terms, devices, owned, samples):
    distances = 2 * (samples // COLS) - 1
    inputs = [pltpu.with_memory_space_constraint(x, pltpu.HBM) for x in (owner, lengths)]
    vmem = pl.BlockSpec(memory_space=pltpu.VMEM)

    def kernel(*refs):
        prepare_kernel(devices, *refs)

    return pl.pallas_call(
        kernel,
        out_shape=(
            pltpu.SMEM((1, samples // LANE), jnp.int32),
            pltpu.VMEM((owned, LANE), jnp.int32),
            pltpu.VMEM((owned, samples), jnp.float32),
            pltpu.VMEM((owned, samples), jnp.float32),
            pltpu.VMEM((owned, samples), jnp.float32),
            pltpu.VMEM((distances, COLS, COLS), jnp.bfloat16),
            pltpu.VMEM((distances, COLS, COLS), jnp.bfloat16),
        ),
        in_specs=[pl.BlockSpec(memory_space=pltpu.HBM)] * 2 + [vmem] * len(terms),
        out_specs=(pl.BlockSpec(memory_space=pltpu.SMEM),) + (vmem,) * 6,
        scratch_shapes=[
            pltpu.SMEM(owner.shape, jnp.int32),
            pltpu.SMEM(lengths.shape, jnp.int32),
            pltpu.VMEM((rows_per_owner(owned) + owned, LANE), jnp.float32),
            pltpu.SemaphoreType.DMA((2,)),
        ],
        compiler_params=pltpu.CompilerParams(vmem_limit_bytes=32 << 20),
        cost_estimate=pl.CostEstimate(flops=1 << 22, bytes_accessed=1 << 21, transcendentals=1 << 19),
        name="prepare",
    )(*inputs, *terms)


def invert_kernel(
    other_ref, offset_ref, rank_ref, kept_ref, inner_ref, outer_ref, coarse_ref, fine_ref, out_ref, sum_buf
):
    owned, samples = inner_ref.shape
    bins = samples // COLS
    per_bin = COLS // LANE

    def halves(value):
        coarse = value.astype(jnp.bfloat16)
        return coarse, (value - coarse.astype(jnp.float32)).astype(jnp.bfloat16)

    sum_buf[0 : other_ref.shape[0], :] = other_ref[...]
    rank = rank_ref[...]
    left = []
    for part in range(bins):
        sums = jnp.concatenate(
            [
                chord_rows(sum_buf, offset_ref[0, block], rank)
                for block in range(part * per_bin, (part + 1) * per_bin)
            ],
            axis=1,
        )
        sums = sums + kept_ref[:, part * COLS : (part + 1) * COLS]
        weight = inner_ref[:, part * COLS : (part + 1) * COLS]
        scaled = jnp.where(weight > 0.0, weight * sums, 0.0)
        left.append(jnp.concatenate(halves(scaled), axis=0))
    image = [None] * bins
    for shift in range(1 - bins, bins):
        first, last = max(0, -shift), min(bins, bins - shift)
        stack = jnp.concatenate(left[first:last], axis=0)
        product = jnp.dot(
            stack, coarse_ref[shift + bins - 1], preferred_element_type=jnp.float32
        ) + jnp.dot(stack, fine_ref[shift + bins - 1], preferred_element_type=jnp.float32)
        for place, part in enumerate(range(first, last)):
            base = place * 2 * owned
            term = product[base : base + owned] + product[base + owned : base + 2 * owned]
            to = part + shift
            image[to] = term if image[to] is None else image[to] + term
    for part in range(bins):
        columns = slice(part * COLS, (part + 1) * COLS)
        out_ref[0, :, columns] = image[part] * outer_ref[:, columns]


def invert(other, prepared, owned, samples):
    vmem = pl.BlockSpec(memory_space=pltpu.VMEM)
    return pl.pallas_call(
        invert_kernel,
        out_shape=jax.ShapeDtypeStruct((1, owned, samples), jnp.float32),
        in_specs=[vmem, pl.BlockSpec(memory_space=pltpu.SMEM)] + [vmem] * 6,
        out_specs=vmem,
        scratch_shapes=[pltpu.VMEM((other.shape[0] + owned, LANE), jnp.float32)],
        compiler_params=pltpu.CompilerParams(vmem_limit_bytes=32 << 20),
        name="invert",
    )(other, *prepared)


def add_kernel(start, *refs):
    *term_refs, out_ref = refs
    rows = pl.ds(start, out_ref.shape[0])
    value = term_refs[0][rows, :]
    for ref in term_refs[1:]:
        value = value + ref[rows, :]
    out_ref[...] = value


def add_rows(terms, start, count):
    vmem = pl.BlockSpec(memory_space=pltpu.VMEM)
    return pl.pallas_call(
        lambda *refs: add_kernel(start, *refs),
        out_shape=pltpu.VMEM((count, LANE), jnp.float32),
        in_specs=[vmem] * len(terms),
        out_specs=vmem,
        compiler_params=pltpu.CompilerParams(vmem_limit_bytes=16 << 20),
        cost_estimate=pl.CostEstimate(
            flops=count * LANE * (len(terms) - 1), bytes_accessed=4 * count * LANE * (len(terms) + 1), transcendentals=0
        ),
        name="add_rows",
    )(*terms)


def per_device(proj, tiles, owner, lengths):
    devices = lax.axis_size("view")
    rows = proj.shape[1]
    samples = tiles.shape[2]
    owned = rows // devices
    packed = rows_per_owner(owned)
    keep, rest, first = project(proj, tiles, owner, lengths, devices)
    *steps, last_step = exchange_pairs(devices)

    def total(terms, place, count=1):
        value, *others = [array[place * packed : (place + count) * packed] for array in terms]
        for other in others:
            value = value + other
        return value

    held = devices // 2
    terms = [keep]
    for pairs in steps:
        got_first, got_rest = lax.ppermute(first, "view", pairs), lax.ppermute(rest, "view", pairs)
        first = total(terms, held - 1) + got_first[:packed]
        terms = terms + [got_rest]
        held //= 2
        if held > 1:
            rest = add_rows(terms, held * packed, (held - 1) * packed)
    other = lax.ppermute(first, "view", last_step)
    prepared = prepare(owner, lengths, terms, devices, owned, samples)
    return invert(other, prepared, owned, samples)


def solution(mesh):
    placed = (P("view", "chord", None), P("view", None, None), P(), P())
    return jax.shard_map(
        per_device, mesh=mesh, in_specs=placed, out_specs=P("chord", "view", None), check_vma=False
    )
```

```python
import math

import jax
import jax.numpy as jnp
from jax import lax
from jax.experimental import pallas as pl
from jax.experimental.pallas import tpu as pltpu
from jax.sharding import PartitionSpec as P

LANE = 128
OWNED_SAMPLES = 4608
COLS = 256


def side(place):
    return (place ^ (place >> 1) ^ (place >> 2)) & 1


def exchange_pairs(devices):
    steps = [[place ^ 1 for place in range(devices)]]
    for first, second in ((3, 5), (5, 3)):
        steps.append([place ^ (second if side(place) else first) for place in range(devices)])
    step = 8
    while step < devices:
        steps.append([place ^ (step | 1) for place in range(devices)])
        step *= 2
    return [list(enumerate(partners)) for partners in steps]


def slot_of(place, me, devices):
    distance = place ^ me
    steps = devices.bit_length() - 1
    first = distance & 1
    slot = jnp.zeros_like(distance)
    for step in range(1, steps):
        bit = (distance >> step) & 1
        first = first ^ bit
        if step > 2:
            slot = slot | (bit << (steps - 1 - step))
    near, far = (distance >> 1) & 1, (distance >> 2) & 1
    swap = side(me) ^ first
    early = jnp.where(swap == 1, far, near)
    late = jnp.where(swap == 1, near, far)
    return slot | (first << (steps - 1)) | (early << (steps - 2)) | (late << (steps - 3))


def rows_per_owner(owned):
    rows = (OWNED_SAMPLES + owned * (LANE - 1)) // LANE
    return -(-rows // 4) * 4


def column_chunks(samples):
    return [(0, samples // 2), (samples // 2, samples // 2)]


def project_kernel(
    devices, owner_hbm, lengths_hbm, proj_hbm, tiles_hbm, keep_ref, rest_ref, first_ref,
    owner_v, lengths_v, offset_v, offset_s, proj_buf, tile_buf, left_buf, sums_buf,
    small_sem, offset_sem, proj_sem, tile_sem,
):
    views, rows, footprint = proj_buf.shape
    samples = tile_buf.shape[2]
    chunks = column_chunks(samples)
    owned = rows // devices
    group = lax.axis_index("chord")
    me = lax.axis_index("view")
    small = [
        pltpu.make_async_copy(source, kept, small_sem.at[index])
        for index, (source, kept) in enumerate(
            [(owner_hbm, owner_v), (lengths_hbm, lengths_v)]
        )
    ]
    for copy in small:
        copy.start()
    proj_copy = pltpu.make_async_copy(proj_hbm, proj_buf, proj_sem)
    proj_copy.start()
    tile_copies = []
    for index, (start, width) in enumerate(chunks):
        columns = pl.ds(start, width)
        copy = pltpu.make_async_copy(
            tiles_hbm.at[:, :, columns], tile_buf.at[:, :, columns], tile_sem.at[index]
        )
        copy.start()
        tile_copies.append(copy)

    for ref in (keep_ref, rest_ref, first_ref):
        ref[...] = jnp.zeros_like(ref)
    for copy in small:
        copy.wait()
    down = lax.broadcasted_iota(jnp.int32, (rows, rows), 0)
    across = lax.broadcasted_iota(jnp.int32, (rows, rows), 1)
    diagonal = down == across

    def turned(row):
        spread = jnp.broadcast_to(row.astype(jnp.float32), (rows, rows))
        return jnp.sum(jnp.where(diagonal, spread, 0.0), axis=1, keepdims=True)

    lengths = lengths_v[pl.ds(group, 1), :]
    order = turned(owner_v[pl.ds(group, 1), :])
    hit = order == across.astype(jnp.float32)
    position = jnp.sum(jnp.where(hit, down.astype(jnp.float32), 0.0), axis=0, keepdims=True)
    position = position.astype(jnp.int32)
    place = position // owned
    slot = slot_of(place, me, devices)

    reach = turned((lengths + (LANE - 1)) // LANE)
    block_index = lax.broadcasted_iota(jnp.int32, (rows, LANE), 1).astype(jnp.float32)
    before = jnp.where(block_index < samples // LANE, jnp.minimum(block_index, reach), 0.0)
    member = lax.broadcasted_iota(jnp.int32, (devices, rows), 0) == slot
    offset_v[...] = jnp.dot(
        jnp.where(member, 1.0, 0.0).astype(jnp.bfloat16),
        before.astype(jnp.bfloat16),
        preferred_element_type=jnp.float32,
    ).astype(jnp.int32)
    offset_copy = pltpu.make_async_copy(offset_v, offset_s, offset_sem)
    offset_copy.start()

    key = (slot * (samples + 1) + (samples - lengths)) * owned + (
        position - place * owned
    )
    key = key.astype(jnp.float32)
    target = jnp.sum(jnp.where(turned(key) < key, 1.0, 0.0), axis=0, keepdims=True)
    pick = jnp.where(down.astype(jnp.float32) == target, 1.0, 0.0).astype(jnp.bfloat16)

    def each_slot(body):
        if devices <= 16:
            for index in range(devices):
                body(index)
        else:
            pl.loop(0, devices)(body)

    proj_copy.wait()
    for view in range(views):
        moved = jnp.dot(pick, proj_buf[view], preferred_element_type=jnp.float32)
        left_buf[:, view * footprint : (view + 1) * footprint] = moved.astype(jnp.bfloat16)

    packed = rows_per_owner(owned)
    half = devices // 2

    def put(slot_index, offset, value):
        def to(out_ref, index):
            out_ref[pl.ds(index * packed + offset, owned), :] = value

        if isinstance(slot_index, int):
            if slot_index == devices - 1:
                to(first_ref, 0)
            elif slot_index < half:
                to(keep_ref, slot_index)
            else:
                to(rest_ref, slot_index - half)
        else:
            pl.when(slot_index == devices - 1)(lambda: to(first_ref, 0))
            pl.when(slot_index < half)(lambda: to(keep_ref, slot_index))
            pl.when((slot_index >= half) & (slot_index < devices - 1))(lambda: to(rest_ref, slot_index - half))

    def pack(first, last):
        def one(slot_index):
            for block in range(first, last):
                value = sums_buf[pl.ds(slot_index * owned, owned), block * LANE : (block + 1) * LANE]
                put(slot_index, offset_s[slot_index, block] if block else 0, value)

        each_slot(one)

    ready = 1
    for index, (start, width) in enumerate(chunks):
        tile_copies[index].wait()
        right = tile_buf[:, :, start : start + width].reshape(views * footprint, width)
        sums_buf[:, start : start + width] = jnp.dot(
            left_buf[...], right, preferred_element_type=jnp.float32
        )
        if index == 1:
            offset_copy.wait()
        if index:
            pack(ready, start // LANE)
            ready = max(ready, start // LANE)
    pack(ready, samples // LANE)
    pack(0, 1)


def project(proj, tiles, owner, lengths, devices):
    views, rows, footprint = proj.shape
    blocks, depth, samples = tiles.shape
    owned = rows // devices
    chunks = column_chunks(samples)
    half = devices // 2
    shapes = [
        pltpu.VMEM((-(-(slots * rows_per_owner(owned) + owned) // 8) * 8, LANE), jnp.float32)
        for slots in (half, half - 1, 1)
    ]
    inputs = [pltpu.with_memory_space_constraint(x, pltpu.HBM) for x in (owner, lengths, proj, tiles)]

    def kernel(*refs):
        project_kernel(devices, *refs)

    vmem = pl.BlockSpec(memory_space=pltpu.VMEM)
    hbm = pl.BlockSpec(memory_space=pltpu.HBM)
    return pl.pallas_call(
        kernel,
        out_shape=tuple(shapes),
        in_specs=[hbm] * 4,
        out_specs=(vmem,) * 3,
        scratch_shapes=[
            pltpu.VMEM(owner.shape, jnp.int32),
            pltpu.VMEM(lengths.shape, jnp.int32),
            pltpu.VMEM((devices, LANE), jnp.int32),
            pltpu.SMEM((devices, LANE), jnp.int32),
            pltpu.VMEM(proj.shape, jnp.bfloat16),
            pltpu.VMEM(tiles.shape, jnp.bfloat16),
            pltpu.VMEM((rows, views * footprint), jnp.bfloat16),
            pltpu.VMEM((rows, samples), jnp.float32),
            pltpu.SemaphoreType.DMA((2,)),
            pltpu.SemaphoreType.DMA,
            pltpu.SemaphoreType.DMA,
            pltpu.SemaphoreType.DMA((len(chunks),)),
        ],
        compiler_params=pltpu.CompilerParams(vmem_limit_bytes=40 << 20),
        cost_estimate=pl.CostEstimate(
            flops=2 * rows * views * footprint * samples,
            bytes_accessed=2 * (proj.size + tiles.size),
            transcendentals=0,
        ),
        name="project",
    )(*inputs)


def chord_rows(packed_ref, offset, rank):
    ordered = packed_ref[pl.ds(offset, rank.shape[0]), :]
    return jnp.take_along_axis(ordered, rank, axis=0)


def prepare_kernel(
    devices, owner_hbm, lengths_hbm, *refs
):
    *term_refs, offset_ref, rank_ref, kept_ref, inner_ref, outer_ref, coarse_ref, fine_ref, owner_s, lengths_s, sum_buf, sem = refs
    owned, samples = inner_ref.shape
    blocks = samples // LANE
    distances = coarse_ref.shape[0]
    group = lax.axis_index("chord")
    me = lax.axis_index("view")
    copies = [
        pltpu.make_async_copy(owner_hbm, owner_s, sem.at[0]),
        pltpu.make_async_copy(lengths_hbm, lengths_s, sem.at[1]),
    ]
    for copy in copies:
        copy.start()
    across = lax.broadcasted_iota(jnp.int32, (COLS, COLS), 1)
    gap = (across - lax.broadcasted_iota(jnp.int32, (COLS, COLS), 0)).astype(jnp.float32) + 0.5
    for index in range(distances):
        exact = 1.0 / (gap + float((index - distances // 2) * COLS))
        coarse = exact.astype(jnp.bfloat16)
        coarse_ref[index] = coarse
        fine_ref[index] = (exact - coarse.astype(jnp.float32)).astype(jnp.bfloat16)
    for copy in copies:
        copy.wait()
    lengths = [lengths_s[group, owner_s[group, me * owned + index]] for index in range(owned)]

    sub = lax.broadcasted_iota(jnp.int32, (owned, LANE), 0)
    lane = lax.broadcasted_iota(jnp.int32, (owned, LANE), 1)
    length = jnp.zeros((owned, LANE), jnp.int32)
    for index in range(owned):
        length = jnp.where(sub == index, lengths[index], length)
    rank = jnp.zeros((owned, LANE), jnp.int32)
    for index in range(owned):
        ahead = (lengths[index] > length) | ((lengths[index] == length) & (index < sub))
        rank = rank + jnp.where(ahead, 1, 0)
    rank_ref[...] = rank
    packed = rows_per_owner(owned)
    kept = term_refs[0][0:packed, :]
    for ref in term_refs[1:]:
        kept = kept + ref[0:packed, :]
    sum_buf[0:packed, :] = kept
    for block in range(blocks):
        offset = jnp.int32(0)
        for index in range(owned):
            offset = offset + jnp.minimum((lengths[index] + (LANE - 1)) >> 7, block)
        offset_ref[0, block] = offset
        kept_ref[:, block * LANE : (block + 1) * LANE] = chord_rows(sum_buf, offset, rank)

    long = length.astype(jnp.float32)
    for block in range(blocks):
        spot = (lane + block * LANE).astype(jnp.float32) + 0.5
        inside = spot < long
        weight = jnp.sqrt(jnp.where(inside, spot * (long - spot), 1.0))
        columns = slice(block * LANE, (block + 1) * LANE)
        inner_ref[:, columns] = jnp.where(inside, weight, 0.0)
        outer_ref[:, columns] = jnp.where(inside, 1.0 / (math.pi * weight), 0.0)


def prepare(owner, lengths, terms, devices, owned, samples):
    distances = 2 * (samples // COLS) - 1
    inputs = [pltpu.with_memory_space_constraint(x, pltpu.HBM) for x in (owner, lengths)]
    vmem = pl.BlockSpec(memory_space=pltpu.VMEM)

    def kernel(*refs):
        prepare_kernel(devices, *refs)

    return pl.pallas_call(
        kernel,
        out_shape=(
            pltpu.SMEM((1, samples // LANE), jnp.int32),
            pltpu.VMEM((owned, LANE), jnp.int32),
            pltpu.VMEM((owned, samples), jnp.float32),
            pltpu.VMEM((owned, samples), jnp.float32),
            pltpu.VMEM((owned, samples), jnp.float32),
            pltpu.VMEM((distances, COLS, COLS), jnp.bfloat16),
            pltpu.VMEM((distances, COLS, COLS), jnp.bfloat16),
        ),
        in_specs=[pl.BlockSpec(memory_space=pltpu.HBM)] * 2 + [vmem] * len(terms),
        out_specs=(pl.BlockSpec(memory_space=pltpu.SMEM),) + (vmem,) * 6,
        scratch_shapes=[
            pltpu.SMEM(owner.shape, jnp.int32),
            pltpu.SMEM(lengths.shape, jnp.int32),
            pltpu.VMEM((rows_per_owner(owned) + owned, LANE), jnp.float32),
            pltpu.SemaphoreType.DMA((2,)),
        ],
        compiler_params=pltpu.CompilerParams(vmem_limit_bytes=32 << 20),
        cost_estimate=pl.CostEstimate(flops=1 << 22, bytes_accessed=1 << 21, transcendentals=1 << 19),
        name="prepare",
    )(*inputs, *terms)


def invert_kernel(
    other_ref, offset_ref, rank_ref, kept_ref, inner_ref, outer_ref, coarse_ref, fine_ref, out_ref, sum_buf
):
    owned, samples = inner_ref.shape
    bins = samples // COLS
    per_bin = COLS // LANE

    def halves(value):
        coarse = value.astype(jnp.bfloat16)
        return coarse, (value - coarse.astype(jnp.float32)).astype(jnp.bfloat16)

    sum_buf[0 : other_ref.shape[0], :] = other_ref[...]
    rank = rank_ref[...]
    left = []
    for part in range(bins):
        sums = jnp.concatenate(
            [
                chord_rows(sum_buf, offset_ref[0, block], rank)
                for block in range(part * per_bin, (part + 1) * per_bin)
            ],
            axis=1,
        )
        sums = sums + kept_ref[:, part * COLS : (part + 1) * COLS]
        weight = inner_ref[:, part * COLS : (part + 1) * COLS]
        scaled = jnp.where(weight > 0.0, weight * sums, 0.0)
        left.append(jnp.concatenate(halves(scaled), axis=0))
    image = [None] * bins
    for shift in range(1 - bins, bins):
        first, last = max(0, -shift), min(bins, bins - shift)
        stack = jnp.concatenate(left[first:last], axis=0)
        product = jnp.dot(
            stack, coarse_ref[shift + bins - 1], preferred_element_type=jnp.float32
        ) + jnp.dot(stack, fine_ref[shift + bins - 1], preferred_element_type=jnp.float32)
        for place, part in enumerate(range(first, last)):
            base = place * 2 * owned
            term = product[base : base + owned] + product[base + owned : base + 2 * owned]
            to = part + shift
            image[to] = term if image[to] is None else image[to] + term
    for part in range(bins):
        columns = slice(part * COLS, (part + 1) * COLS)
        out_ref[0, :, columns] = image[part] * outer_ref[:, columns]


def invert(other, prepared, owned, samples):
    vmem = pl.BlockSpec(memory_space=pltpu.VMEM)
    return pl.pallas_call(
        invert_kernel,
        out_shape=jax.ShapeDtypeStruct((1, owned, samples), jnp.float32),
        in_specs=[vmem, pl.BlockSpec(memory_space=pltpu.SMEM)] + [vmem] * 6,
        out_specs=vmem,
        scratch_shapes=[pltpu.VMEM((other.shape[0] + owned, LANE), jnp.float32)],
        compiler_params=pltpu.CompilerParams(vmem_limit_bytes=32 << 20),
        name="invert",
    )(other, *prepared)


def add_kernel(starts, *refs):
    *term_refs, out_ref = refs
    count = out_ref.shape[0]
    values = [ref[pl.ds(start, count), :] for ref, start in zip(term_refs, starts)]
    total = values[0]
    for value in values[1:]:
        total = total + value
    out_ref[...] = total


def add_rows(terms, starts, count):
    vmem = pl.BlockSpec(memory_space=pltpu.VMEM)
    return pl.pallas_call(
        lambda *refs: add_kernel(starts, *refs),
        out_shape=pltpu.VMEM((count, LANE), jnp.float32),
        in_specs=[vmem] * len(terms),
        out_specs=vmem,
        compiler_params=pltpu.CompilerParams(vmem_limit_bytes=16 << 20),
        cost_estimate=pl.CostEstimate(
            flops=count * LANE * (len(terms) - 1), bytes_accessed=4 * count * LANE * (len(terms) + 1), transcendentals=0
        ),
        name="add_rows",
    )(*terms)


def per_device(proj, tiles, owner, lengths):
    devices = lax.axis_size("view")
    rows = proj.shape[1]
    samples = tiles.shape[2]
    owned = rows // devices
    packed = rows_per_owner(owned)
    keep, rest, first = project(proj, tiles, owner, lengths, devices)

    def total(terms, place):
        value, *others = [array[(place - base) * packed : (place - base + 1) * packed] for array, base in terms]
        for other in others:
            value = value + other
        return value

    def apart(terms, place, count):
        return add_rows([array for array, _ in terms], [(place - base) * packed for _, base in terms], count * packed)

    def give(value):
        return lax.ppermute(value, "view", pairs)

    held = devices // 2
    pairs, *steps, last_pairs = exchange_pairs(devices)
    got_first, got_rest = give(first), give(rest)
    first = total([(keep, 0)], held - 1) + got_first[:packed]
    terms = [(keep, 0), (got_rest, 0)]
    sent_next = terms
    for pairs in steps:
        held //= 2
        got_first, got_second = give(first), None
        if held > 2:
            got_second = give(apart(sent_next, held + held // 2, held // 2 - 1))
        got_third = give(apart(sent_next, held, held // 2))
        first = total(terms, held - 1) + got_first
        sent_next = terms + [(got_second, held // 2)]
        terms = terms + [(got_third, 0)]
    pairs = last_pairs
    other = give(first)
    prepared = prepare(owner, lengths, [array for array, _ in terms], devices, owned, samples)
    return invert(other, prepared, owned, samples)


def solution(mesh):
    placed = (P("view", "chord", None), P("view", None, None), P(), P())
    return jax.shard_map(
        per_device, mesh=mesh, in_specs=placed, out_specs=P("chord", "view", None), check_vma=False
    )
```

```python
import math

import jax
import jax.numpy as jnp
from jax import lax
from jax.experimental import pallas as pl
from jax.experimental.pallas import tpu as pltpu
from jax.sharding import PartitionSpec as P

LANE = 128
OWNED_SAMPLES = 4608
COLS = 256


def side(place):
    return (place ^ (place >> 1) ^ (place >> 2)) & 1


def exchange_pairs(devices):
    steps = [[place ^ 1 for place in range(devices)]]
    for first, second in ((3, 5), (5, 3)):
        steps.append([place ^ (second if side(place) else first) for place in range(devices)])
    step = 8
    while step < devices:
        steps.append([place ^ (step | 1) for place in range(devices)])
        step *= 2
    return [list(enumerate(partners)) for partners in steps]


def slot_of(place, me, devices):
    distance = place ^ me
    steps = devices.bit_length() - 1
    first = distance & 1
    slot = jnp.zeros_like(distance)
    for step in range(1, steps):
        bit = (distance >> step) & 1
        first = first ^ bit
        if step > 2:
            slot = slot | (bit << (steps - 1 - step))
    near, far = (distance >> 1) & 1, (distance >> 2) & 1
    swap = side(me) ^ first
    early = jnp.where(swap == 1, far, near)
    late = jnp.where(swap == 1, near, far)
    return slot | (first << (steps - 1)) | (early << (steps - 2)) | (late << (steps - 3))


def rows_per_owner(owned):
    rows = (OWNED_SAMPLES + owned * (LANE - 1)) // LANE
    return -(-rows // 4) * 4


def tile_pieces(blocks, samples):
    half, head = samples // 2, blocks * 2 // 3
    return [(0, half, 0, blocks), (half, half, 0, head), (half, half, head, blocks - head)]


def project_kernel(
    devices, owner_hbm, lengths_hbm, proj_hbm, tiles_hbm, keep_ref, rest_ref, first_ref,
    owner_v, lengths_v, offset_v, offset_s, proj_buf, tile_buf, left_buf, sums_buf,
    small_sem, offset_sem, proj_sem, tile_sem,
):
    views, rows, footprint = proj_buf.shape
    samples = tile_buf.shape[2]
    pieces = tile_pieces(tile_buf.shape[0], samples)
    depth = tile_buf.shape[1]
    owned = rows // devices
    group = lax.axis_index("chord")
    me = lax.axis_index("view")
    small = [
        pltpu.make_async_copy(source, kept, small_sem.at[index])
        for index, (source, kept) in enumerate(
            [(owner_hbm, owner_v), (lengths_hbm, lengths_v)]
        )
    ]
    for copy in small:
        copy.start()
    proj_copy = pltpu.make_async_copy(proj_hbm, proj_buf, proj_sem)
    proj_copy.start()
    tile_copies = []
    for index, (start, width, first, count) in enumerate(pieces):
        place = pl.ds(first, count), slice(None), pl.ds(start, width)
        copy = pltpu.make_async_copy(tiles_hbm.at[place], tile_buf.at[place], tile_sem.at[index])
        copy.start()
        tile_copies.append(copy)

    for ref in (keep_ref, rest_ref, first_ref):
        ref[...] = jnp.zeros_like(ref)
    for copy in small:
        copy.wait()
    down = lax.broadcasted_iota(jnp.int32, (rows, rows), 0)
    across = lax.broadcasted_iota(jnp.int32, (rows, rows), 1)
    diagonal = down == across

    def turned(row):
        spread = jnp.broadcast_to(row.astype(jnp.float32), (rows, rows))
        return jnp.sum(jnp.where(diagonal, spread, 0.0), axis=1, keepdims=True)

    lengths = lengths_v[pl.ds(group, 1), :]
    order = turned(owner_v[pl.ds(group, 1), :])
    hit = order == across.astype(jnp.float32)
    position = jnp.sum(jnp.where(hit, down.astype(jnp.float32), 0.0), axis=0, keepdims=True)
    position = position.astype(jnp.int32)
    place = position // owned
    slot = slot_of(place, me, devices)

    reach = turned((lengths + (LANE - 1)) // LANE)
    block_index = lax.broadcasted_iota(jnp.int32, (rows, LANE), 1).astype(jnp.float32)
    before = jnp.where(block_index < samples // LANE, jnp.minimum(block_index, reach), 0.0)
    member = lax.broadcasted_iota(jnp.int32, (devices, rows), 0) == slot
    offset_v[...] = jnp.dot(
        jnp.where(member, 1.0, 0.0).astype(jnp.bfloat16),
        before.astype(jnp.bfloat16),
        preferred_element_type=jnp.float32,
    ).astype(jnp.int32)
    offset_copy = pltpu.make_async_copy(offset_v, offset_s, offset_sem)
    offset_copy.start()

    key = (slot * (samples + 1) + (samples - lengths)) * owned + (
        position - place * owned
    )
    key = key.astype(jnp.float32)
    target = jnp.sum(jnp.where(turned(key) < key, 1.0, 0.0), axis=0, keepdims=True)
    pick = jnp.where(down.astype(jnp.float32) == target, 1.0, 0.0).astype(jnp.bfloat16)

    def each_slot(body):
        if devices <= 16:
            for index in range(devices):
                body(index)
        else:
            pl.loop(0, devices)(body)

    proj_copy.wait()
    for view in range(views):
        moved = jnp.dot(pick, proj_buf[view], preferred_element_type=jnp.float32)
        left_buf[:, view * footprint : (view + 1) * footprint] = moved.astype(jnp.bfloat16)

    packed = rows_per_owner(owned)
    half = devices // 2

    def put(slot_index, offset, value):
        def to(out_ref, index):
            out_ref[pl.ds(index * packed + offset, owned), :] = value

        if isinstance(slot_index, int):
            if slot_index == devices - 1:
                to(first_ref, 0)
            elif slot_index < half:
                to(keep_ref, slot_index)
            else:
                to(rest_ref, slot_index - half)
        else:
            pl.when(slot_index == devices - 1)(lambda: to(first_ref, 0))
            pl.when(slot_index < half)(lambda: to(keep_ref, slot_index))
            pl.when((slot_index >= half) & (slot_index < devices - 1))(lambda: to(rest_ref, slot_index - half))

    def pack(first, last):
        def one(slot_index):
            for block in range(first, last):
                value = sums_buf[pl.ds(slot_index * owned, owned), block * LANE : (block + 1) * LANE]
                put(slot_index, offset_s[slot_index, block] if block else 0, value)

        each_slot(one)

    half_blocks = samples // 2 // LANE
    for index, (start, width, first, count) in enumerate(pieces):
        tile_copies[index].wait()
        right = tile_buf[first : first + count, :, start : start + width].reshape(count * depth, width)
        left = left_buf[:, first * depth : (first + count) * depth]
        sums = jnp.dot(left, right, preferred_element_type=jnp.float32)
        if first:
            sums = sums + sums_buf[:, start : start + width]
        sums_buf[:, start : start + width] = sums
        if index == 1:
            offset_copy.wait()
            pack(1, half_blocks)
    pack(half_blocks, samples // LANE)
    pack(0, 1)


def project(proj, tiles, owner, lengths, devices):
    views, rows, footprint = proj.shape
    blocks, depth, samples = tiles.shape
    owned = rows // devices
    half = devices // 2
    shapes = [
        pltpu.VMEM((-(-(slots * rows_per_owner(owned) + owned) // 8) * 8, LANE), jnp.float32)
        for slots in (half, half - 1, 1)
    ]
    inputs = [pltpu.with_memory_space_constraint(x, pltpu.HBM) for x in (owner, lengths, proj, tiles)]

    def kernel(*refs):
        project_kernel(devices, *refs)

    vmem = pl.BlockSpec(memory_space=pltpu.VMEM)
    hbm = pl.BlockSpec(memory_space=pltpu.HBM)
    return pl.pallas_call(
        kernel,
        out_shape=tuple(shapes),
        in_specs=[hbm] * 4,
        out_specs=(vmem,) * 3,
        scratch_shapes=[
            pltpu.VMEM(owner.shape, jnp.int32),
            pltpu.VMEM(lengths.shape, jnp.int32),
            pltpu.VMEM((devices, LANE), jnp.int32),
            pltpu.SMEM((devices, LANE), jnp.int32),
            pltpu.VMEM(proj.shape, jnp.bfloat16),
            pltpu.VMEM(tiles.shape, jnp.bfloat16),
            pltpu.VMEM((rows, views * footprint), jnp.bfloat16),
            pltpu.VMEM((rows, samples), jnp.float32),
            pltpu.SemaphoreType.DMA((2,)),
            pltpu.SemaphoreType.DMA,
            pltpu.SemaphoreType.DMA,
            pltpu.SemaphoreType.DMA((len(tile_pieces(blocks, samples)),)),
        ],
        compiler_params=pltpu.CompilerParams(vmem_limit_bytes=40 << 20),
        cost_estimate=pl.CostEstimate(
            flops=2 * rows * views * footprint * samples,
            bytes_accessed=2 * (proj.size + tiles.size),
            transcendentals=0,
        ),
        name="project",
    )(*inputs)


def chord_rows(packed_ref, offset, rank):
    ordered = packed_ref[pl.ds(offset, rank.shape[0]), :]
    return jnp.take_along_axis(ordered, rank, axis=0)


def prepare_kernel(
    devices, owner_hbm, lengths_hbm, *refs
):
    *term_refs, offset_ref, rank_ref, kept_ref, inner_ref, outer_ref, coarse_ref, fine_ref, owner_s, lengths_s, sum_buf, sem = refs
    owned, samples = inner_ref.shape
    blocks = samples // LANE
    distances = coarse_ref.shape[0]
    group = lax.axis_index("chord")
    me = lax.axis_index("view")
    copies = [
        pltpu.make_async_copy(owner_hbm, owner_s, sem.at[0]),
        pltpu.make_async_copy(lengths_hbm, lengths_s, sem.at[1]),
    ]
    for copy in copies:
        copy.start()
    across = lax.broadcasted_iota(jnp.int32, (COLS, COLS), 1)
    gap = (across - lax.broadcasted_iota(jnp.int32, (COLS, COLS), 0)).astype(jnp.float32) + 0.5
    for index in range(distances):
        exact = 1.0 / (gap + float((index - distances // 2) * COLS))
        coarse = exact.astype(jnp.bfloat16)
        coarse_ref[index] = coarse
        fine_ref[index] = (exact - coarse.astype(jnp.float32)).astype(jnp.bfloat16)
    for copy in copies:
        copy.wait()
    lengths = [lengths_s[group, owner_s[group, me * owned + index]] for index in range(owned)]

    sub = lax.broadcasted_iota(jnp.int32, (owned, LANE), 0)
    lane = lax.broadcasted_iota(jnp.int32, (owned, LANE), 1)
    length = jnp.zeros((owned, LANE), jnp.int32)
    for index in range(owned):
        length = jnp.where(sub == index, lengths[index], length)
    rank = jnp.zeros((owned, LANE), jnp.int32)
    for index in range(owned):
        ahead = (lengths[index] > length) | ((lengths[index] == length) & (index < sub))
        rank = rank + jnp.where(ahead, 1, 0)
    rank_ref[...] = rank
    packed = rows_per_owner(owned)
    kept = term_refs[0][0:packed, :]
    for ref in term_refs[1:]:
        kept = kept + ref[0:packed, :]
    sum_buf[0:packed, :] = kept
    for block in range(blocks):
        offset = jnp.int32(0)
        for index in range(owned):
            offset = offset + jnp.minimum((lengths[index] + (LANE - 1)) >> 7, block)
        offset_ref[0, block] = offset
        kept_ref[:, block * LANE : (block + 1) * LANE] = chord_rows(sum_buf, offset, rank)

    long = length.astype(jnp.float32)
    for block in range(blocks):
        spot = (lane + block * LANE).astype(jnp.float32) + 0.5
        inside = spot < long
        weight = jnp.sqrt(jnp.where(inside, spot * (long - spot), 1.0))
        columns = slice(block * LANE, (block + 1) * LANE)
        inner_ref[:, columns] = jnp.where(inside, weight, 0.0)
        outer_ref[:, columns] = jnp.where(inside, 1.0 / (math.pi * weight), 0.0)


def prepare(owner, lengths, terms, devices, owned, samples):
    distances = 2 * (samples // COLS) - 1
    inputs = [pltpu.with_memory_space_constraint(x, pltpu.HBM) for x in (owner, lengths)]
    vmem = pl.BlockSpec(memory_space=pltpu.VMEM)

    def kernel(*refs):
        prepare_kernel(devices, *refs)

    return pl.pallas_call(
        kernel,
        out_shape=(
            pltpu.SMEM((1, samples // LANE), jnp.int32),
            pltpu.VMEM((owned, LANE), jnp.int32),
            pltpu.VMEM((owned, samples), jnp.float32),
            pltpu.VMEM((owned, samples), jnp.float32),
            pltpu.VMEM((owned, samples), jnp.float32),
            pltpu.VMEM((distances, COLS, COLS), jnp.bfloat16),
            pltpu.VMEM((distances, COLS, COLS), jnp.bfloat16),
        ),
        in_specs=[pl.BlockSpec(memory_space=pltpu.HBM)] * 2 + [vmem] * len(terms),
        out_specs=(pl.BlockSpec(memory_space=pltpu.SMEM),) + (vmem,) * 6,
        scratch_shapes=[
            pltpu.SMEM(owner.shape, jnp.int32),
            pltpu.SMEM(lengths.shape, jnp.int32),
            pltpu.VMEM((rows_per_owner(owned) + owned, LANE), jnp.float32),
            pltpu.SemaphoreType.DMA((2,)),
        ],
        compiler_params=pltpu.CompilerParams(vmem_limit_bytes=32 << 20),
        cost_estimate=pl.CostEstimate(flops=1 << 22, bytes_accessed=1 << 21, transcendentals=1 << 19),
        name="prepare",
    )(*inputs, *terms)


def invert_kernel(
    other_ref, offset_ref, rank_ref, kept_ref, inner_ref, outer_ref, coarse_ref, fine_ref, out_ref, sum_buf
):
    owned, samples = inner_ref.shape
    bins = samples // COLS
    per_bin = COLS // LANE

    sum_buf[0 : other_ref.shape[0], :] = other_ref[...]
    rank = rank_ref[...]
    left = []
    for part in range(bins):
        sums = jnp.concatenate(
            [
                chord_rows(sum_buf, offset_ref[0, block], rank)
                for block in range(part * per_bin, (part + 1) * per_bin)
            ],
            axis=1,
        )
        sums = sums + kept_ref[:, part * COLS : (part + 1) * COLS]
        weight = inner_ref[:, part * COLS : (part + 1) * COLS]
        scaled = jnp.where(weight > 0.0, weight * sums, 0.0)
        coarse = scaled.astype(jnp.bfloat16).astype(jnp.float32)
        left.append(jnp.concatenate([coarse, scaled - coarse], axis=0).astype(jnp.bfloat16))
    image = [None] * bins
    for shift in range(1 - bins, bins):
        first, last = max(0, -shift), min(bins, bins - shift)
        stack = jnp.concatenate(left[first:last], axis=0)
        product = jnp.dot(
            stack, coarse_ref[shift + bins - 1], preferred_element_type=jnp.float32
        ) + jnp.dot(stack, fine_ref[shift + bins - 1], preferred_element_type=jnp.float32)
        for place, part in enumerate(range(first, last)):
            base = place * 2 * owned
            term = product[base : base + owned] + product[base + owned : base + 2 * owned]
            to = part + shift
            image[to] = term if image[to] is None else image[to] + term
    for part in range(bins):
        columns = slice(part * COLS, (part + 1) * COLS)
        out_ref[0, :, columns] = image[part] * outer_ref[:, columns]


def invert(other, prepared, owned, samples):
    vmem = pl.BlockSpec(memory_space=pltpu.VMEM)
    return pl.pallas_call(
        invert_kernel,
        out_shape=jax.ShapeDtypeStruct((1, owned, samples), jnp.float32),
        in_specs=[vmem, pl.BlockSpec(memory_space=pltpu.SMEM)] + [vmem] * 6,
        out_specs=vmem,
        scratch_shapes=[pltpu.VMEM((other.shape[0] + owned, LANE), jnp.float32)],
        compiler_params=pltpu.CompilerParams(vmem_limit_bytes=32 << 20),
        name="invert",
    )(other, *prepared)


def add_kernel(starts, *refs):
    *term_refs, out_ref = refs
    count = out_ref.shape[0]
    values = [ref[pl.ds(start, count), :] for ref, start in zip(term_refs, starts)]
    total = values[0]
    for value in values[1:]:
        total = total + value
    out_ref[...] = total


def add_rows(terms, starts, count):
    vmem = pl.BlockSpec(memory_space=pltpu.VMEM)
    return pl.pallas_call(
        lambda *refs: add_kernel(starts, *refs),
        out_shape=pltpu.VMEM((count, LANE), jnp.float32),
        in_specs=[vmem] * len(terms),
        out_specs=vmem,
        compiler_params=pltpu.CompilerParams(vmem_limit_bytes=16 << 20),
        cost_estimate=pl.CostEstimate(
            flops=count * LANE * (len(terms) - 1), bytes_accessed=4 * count * LANE * (len(terms) + 1), transcendentals=0
        ),
        name="add_rows",
    )(*terms)


def per_device(proj, tiles, owner, lengths):
    devices = lax.axis_size("view")
    rows = proj.shape[1]
    samples = tiles.shape[2]
    owned = rows // devices
    packed = rows_per_owner(owned)
    keep, rest, first = project(proj, tiles, owner, lengths, devices)

    def total(terms, place):
        value, *others = [array[(place - base) * packed : (place - base + 1) * packed] for array, base in terms]
        for other in others:
            value = value + other
        return value

    def apart(terms, place, count):
        return add_rows([array for array, _ in terms], [(place - base) * packed for _, base in terms], count * packed)

    def give(value):
        return lax.ppermute(value, "view", pairs)

    held = devices // 2
    pairs, *steps, last_pairs = exchange_pairs(devices)
    got_first, got_rest = give(first), give(rest)
    first = total([(keep, 0)], held - 1) + got_first[:packed]
    terms = [(keep, 0), (got_rest, 0)]
    sent_next = terms
    for pairs in steps:
        held //= 2
        got_first, got_second = give(first), None
        if held > 2:
            got_second = give(apart(sent_next, held + held // 2, held // 2 - 1))
        got_third = give(apart(sent_next, held, held // 2))
        first = total(terms, held - 1) + got_first
        sent_next = terms + [(got_second, held // 2)]
        terms = terms + [(got_third, 0)]
    pairs = last_pairs
    other = give(first)
    prepared = prepare(owner, lengths, [array for array, _ in terms], devices, owned, samples)
    return invert(other, prepared, owned, samples)


def solution(mesh):
    placed = (P("view", "chord", None), P("view", None, None), P(), P())
    return jax.shard_map(
        per_device, mesh=mesh, in_specs=placed, out_specs=P("chord", "view", None), check_vma=False
    )
```

```python
import math

import jax
import jax.numpy as jnp
from jax import lax
from jax.experimental import pallas as pl
from jax.experimental.pallas import tpu as pltpu
from jax.sharding import PartitionSpec as P

LANE = 128
OWNED_SAMPLES = 4608
COLS = 256


def side(place):
    return (place ^ (place >> 1) ^ (place >> 2)) & 1


def exchange_pairs(devices):
    steps = [[place ^ 1 for place in range(devices)]]
    for first, second in ((3, 5), (5, 3)):
        steps.append([place ^ (second if side(place) else first) for place in range(devices)])
    step = 8
    while step < devices:
        steps.append([place ^ (step | 1) for place in range(devices)])
        step *= 2
    return [list(enumerate(partners)) for partners in steps]


def slot_of(place, me, devices):
    distance = place ^ me
    steps = devices.bit_length() - 1
    first = distance & 1
    slot = jnp.zeros_like(distance)
    for step in range(1, steps):
        bit = (distance >> step) & 1
        first = first ^ bit
        if step > 2:
            slot = slot | (bit << (steps - 1 - step))
    near, far = (distance >> 1) & 1, (distance >> 2) & 1
    swap = side(me) ^ first
    early = jnp.where(swap == 1, far, near)
    late = jnp.where(swap == 1, near, far)
    return slot | (first << (steps - 1)) | (early << (steps - 2)) | (late << (steps - 3))


def rows_per_owner(owned):
    rows = (OWNED_SAMPLES + owned * (LANE - 1)) // LANE
    return -(-rows // 4) * 4


def tile_pieces(blocks, samples):
    half, head = samples // 2, blocks * 2 // 3
    return [(0, half, 0, blocks), (half, half, 0, head), (half, half, head, blocks - head)]


def project_kernel(
    devices, owner_hbm, lengths_hbm, proj_hbm, tiles_hbm, keep_ref, third_ref, second_ref, first_ref,
    owner_v, lengths_v, offset_v, offset_s, proj_buf, tile_buf, left_buf, sums_buf,
    small_sem, offset_sem, proj_sem, tile_sem,
):
    views, rows, footprint = proj_buf.shape
    samples = tile_buf.shape[2]
    pieces = tile_pieces(tile_buf.shape[0], samples)
    depth = tile_buf.shape[1]
    owned = rows // devices
    group = lax.axis_index("chord")
    me = lax.axis_index("view")
    small = [
        pltpu.make_async_copy(source, kept, small_sem.at[index])
        for index, (source, kept) in enumerate(
            [(owner_hbm, owner_v), (lengths_hbm, lengths_v)]
        )
    ]
    for copy in small:
        copy.start()
    proj_copy = pltpu.make_async_copy(proj_hbm, proj_buf, proj_sem)
    proj_copy.start()
    tile_copies = []
    for index, (start, width, first, count) in enumerate(pieces):
        place = pl.ds(first, count), slice(None), pl.ds(start, width)
        copy = pltpu.make_async_copy(tiles_hbm.at[place], tile_buf.at[place], tile_sem.at[index])
        copy.start()
        tile_copies.append(copy)

    for ref in (keep_ref, third_ref, second_ref, first_ref):
        ref[...] = jnp.zeros_like(ref)
    for copy in small:
        copy.wait()
    down = lax.broadcasted_iota(jnp.int32, (rows, rows), 0)
    across = lax.broadcasted_iota(jnp.int32, (rows, rows), 1)
    diagonal = down == across

    def turned(row):
        spread = jnp.broadcast_to(row.astype(jnp.float32), (rows, rows))
        return jnp.sum(jnp.where(diagonal, spread, 0.0), axis=1, keepdims=True)

    lengths = lengths_v[pl.ds(group, 1), :]
    order = turned(owner_v[pl.ds(group, 1), :])
    hit = order == across.astype(jnp.float32)
    position = jnp.sum(jnp.where(hit, down.astype(jnp.float32), 0.0), axis=0, keepdims=True)
    position = position.astype(jnp.int32)
    place = position // owned
    slot = slot_of(place, me, devices)

    reach = turned((lengths + (LANE - 1)) // LANE)
    block_index = lax.broadcasted_iota(jnp.int32, (rows, LANE), 1).astype(jnp.float32)
    before = jnp.where(block_index < samples // LANE, jnp.minimum(block_index, reach), 0.0)
    member = lax.broadcasted_iota(jnp.int32, (devices, rows), 0) == slot
    offset_v[...] = jnp.dot(
        jnp.where(member, 1.0, 0.0).astype(jnp.bfloat16),
        before.astype(jnp.bfloat16),
        preferred_element_type=jnp.float32,
    ).astype(jnp.int32)
    offset_copy = pltpu.make_async_copy(offset_v, offset_s, offset_sem)
    offset_copy.start()

    key = (slot * (samples + 1) + (samples - lengths)) * owned + (
        position - place * owned
    )
    key = key.astype(jnp.float32)
    target = jnp.sum(jnp.where(turned(key) < key, 1.0, 0.0), axis=0, keepdims=True)
    pick = jnp.where(down.astype(jnp.float32) == target, 1.0, 0.0).astype(jnp.bfloat16)

    def each_slot(body):
        if devices <= 16:
            for index in range(devices):
                body(index)
        else:
            pl.loop(0, devices)(body)

    proj_copy.wait()
    for view in range(views):
        moved = jnp.dot(pick, proj_buf[view], preferred_element_type=jnp.float32)
        left_buf[:, view * footprint : (view + 1) * footprint] = moved.astype(jnp.bfloat16)

    packed = rows_per_owner(owned)
    half = devices // 2

    def put(slot_index, offset, value):
        def to(out_ref, index):
            out_ref[pl.ds(index * packed + offset, owned), :] = value

        bounds = [0, half, half + half // 2, devices - 1, devices]
        for low, high, ref in zip(bounds, bounds[1:], (keep_ref, third_ref, second_ref, first_ref)):
            if not isinstance(slot_index, int):
                here = (slot_index >= low) & (slot_index < high)
                pl.when(here)(lambda ref=ref, low=low: to(ref, slot_index - low))
            elif low <= slot_index < high:
                to(ref, slot_index - low)

    def pack(first, last):
        def one(slot_index):
            for block in range(first, last):
                value = sums_buf[pl.ds(slot_index * owned, owned), block * LANE : (block + 1) * LANE]
                put(slot_index, offset_s[slot_index, block] if block else 0, value)

        each_slot(one)

    half_blocks = samples // 2 // LANE
    for index, (start, width, first, count) in enumerate(pieces):
        tile_copies[index].wait()
        right = tile_buf[first : first + count, :, start : start + width].reshape(count * depth, width)
        left = left_buf[:, first * depth : (first + count) * depth]
        sums = jnp.dot(left, right, preferred_element_type=jnp.float32)
        if first:
            sums = sums + sums_buf[:, start : start + width]
        sums_buf[:, start : start + width] = sums
        if index == 1:
            offset_copy.wait()
            pack(1, half_blocks)
    pack(half_blocks, samples // LANE)
    pack(0, 1)


def project(proj, tiles, owner, lengths, devices):
    views, rows, footprint = proj.shape
    blocks, depth, samples = tiles.shape
    owned = rows // devices
    half = devices // 2
    shapes = [
        pltpu.VMEM((-(-(slots * rows_per_owner(owned) + owned) // 8) * 8, LANE), jnp.float32)
        for slots in (half, half // 2, half // 2 - 1, 1)
    ]
    inputs = [pltpu.with_memory_space_constraint(x, pltpu.HBM) for x in (owner, lengths, proj, tiles)]

    def kernel(*refs):
        project_kernel(devices, *refs)

    vmem = pl.BlockSpec(memory_space=pltpu.VMEM)
    hbm = pl.BlockSpec(memory_space=pltpu.HBM)
    return pl.pallas_call(
        kernel,
        out_shape=tuple(shapes),
        in_specs=[hbm] * 4,
        out_specs=(vmem,) * 4,
        scratch_shapes=[
            pltpu.VMEM(owner.shape, jnp.int32),
            pltpu.VMEM(lengths.shape, jnp.int32),
            pltpu.VMEM((devices, LANE), jnp.int32),
            pltpu.SMEM((devices, LANE), jnp.int32),
            pltpu.VMEM(proj.shape, jnp.bfloat16),
            pltpu.VMEM(tiles.shape, jnp.bfloat16),
            pltpu.VMEM((rows, views * footprint), jnp.bfloat16),
            pltpu.VMEM((rows, samples), jnp.float32),
            pltpu.SemaphoreType.DMA((2,)),
            pltpu.SemaphoreType.DMA,
            pltpu.SemaphoreType.DMA,
            pltpu.SemaphoreType.DMA((len(tile_pieces(blocks, samples)),)),
        ],
        compiler_params=pltpu.CompilerParams(vmem_limit_bytes=40 << 20),
        cost_estimate=pl.CostEstimate(
            flops=2 * rows * views * footprint * samples,
            bytes_accessed=2 * (proj.size + tiles.size),
            transcendentals=0,
        ),
        name="project",
    )(*inputs)


def chord_rows(packed_ref, offset, rank):
    ordered = packed_ref[pl.ds(offset, rank.shape[0]), :]
    return jnp.take_along_axis(ordered, rank, axis=0)


def prepare_kernel(
    devices, owner_hbm, lengths_hbm, *refs
):
    *term_refs, offset_ref, rank_ref, kept_ref, inner_ref, outer_ref, coarse_ref, fine_ref, owner_s, lengths_s, sum_buf, sem = refs
    owned, samples = inner_ref.shape
    blocks = samples // LANE
    distances = coarse_ref.shape[0]
    group = lax.axis_index("chord")
    me = lax.axis_index("view")
    copies = [
        pltpu.make_async_copy(owner_hbm, owner_s, sem.at[0]),
        pltpu.make_async_copy(lengths_hbm, lengths_s, sem.at[1]),
    ]
    for copy in copies:
        copy.start()
    across = lax.broadcasted_iota(jnp.int32, (COLS, COLS), 1)
    gap = (across - lax.broadcasted_iota(jnp.int32, (COLS, COLS), 0)).astype(jnp.float32) + 0.5
    for index in range(distances):
        exact = 1.0 / (gap + float((index - distances // 2) * COLS))
        coarse = exact.astype(jnp.bfloat16)
        coarse_ref[index] = coarse
        fine_ref[index] = (exact - coarse.astype(jnp.float32)).astype(jnp.bfloat16)
    for copy in copies:
        copy.wait()
    lengths = [lengths_s[group, owner_s[group, me * owned + index]] for index in range(owned)]

    sub = lax.broadcasted_iota(jnp.int32, (owned, LANE), 0)
    lane = lax.broadcasted_iota(jnp.int32, (owned, LANE), 1)
    length = jnp.zeros((owned, LANE), jnp.int32)
    for index in range(owned):
        length = jnp.where(sub == index, lengths[index], length)
    rank = jnp.zeros((owned, LANE), jnp.int32)
    for index in range(owned):
        ahead = (lengths[index] > length) | ((lengths[index] == length) & (index < sub))
        rank = rank + jnp.where(ahead, 1, 0)
    rank_ref[...] = rank
    packed = rows_per_owner(owned)
    kept = term_refs[0][0:packed, :]
    for ref in term_refs[1:]:
        kept = kept + ref[0:packed, :]
    sum_buf[0:packed, :] = kept
    for block in range(blocks):
        offset = jnp.int32(0)
        for index in range(owned):
            offset = offset + jnp.minimum((lengths[index] + (LANE - 1)) >> 7, block)
        offset_ref[0, block] = offset
        kept_ref[:, block * LANE : (block + 1) * LANE] = chord_rows(sum_buf, offset, rank)

    long = length.astype(jnp.float32)
    for block in range(blocks):
        spot = (lane + block * LANE).astype(jnp.float32) + 0.5
        inside = spot < long
        weight = jnp.sqrt(jnp.where(inside, spot * (long - spot), 1.0))
        columns = slice(block * LANE, (block + 1) * LANE)
        inner_ref[:, columns] = jnp.where(inside, weight, 0.0)
        outer_ref[:, columns] = jnp.where(inside, 1.0 / (math.pi * weight), 0.0)


def prepare(owner, lengths, terms, devices, owned, samples):
    distances = 2 * (samples // COLS) - 1
    inputs = [pltpu.with_memory_space_constraint(x, pltpu.HBM) for x in (owner, lengths)]
    vmem = pl.BlockSpec(memory_space=pltpu.VMEM)

    def kernel(*refs):
        prepare_kernel(devices, *refs)

    return pl.pallas_call(
        kernel,
        out_shape=(
            pltpu.SMEM((1, samples // LANE), jnp.int32),
            pltpu.VMEM((owned, LANE), jnp.int32),
            pltpu.VMEM((owned, samples), jnp.float32),
            pltpu.VMEM((owned, samples), jnp.float32),
            pltpu.VMEM((owned, samples), jnp.float32),
            pltpu.VMEM((distances, COLS, COLS), jnp.bfloat16),
            pltpu.VMEM((distances, COLS, COLS), jnp.bfloat16),
        ),
        in_specs=[pl.BlockSpec(memory_space=pltpu.HBM)] * 2 + [vmem] * len(terms),
        out_specs=(pl.BlockSpec(memory_space=pltpu.SMEM),) + (vmem,) * 6,
        scratch_shapes=[
            pltpu.SMEM(owner.shape, jnp.int32),
            pltpu.SMEM(lengths.shape, jnp.int32),
            pltpu.VMEM((rows_per_owner(owned) + owned, LANE), jnp.float32),
            pltpu.SemaphoreType.DMA((2,)),
        ],
        compiler_params=pltpu.CompilerParams(vmem_limit_bytes=32 << 20),
        cost_estimate=pl.CostEstimate(flops=1 << 22, bytes_accessed=1 << 21, transcendentals=1 << 19),
        name="prepare",
    )(*inputs, *terms)


def invert_kernel(
    other_ref, offset_ref, rank_ref, kept_ref, inner_ref, outer_ref, coarse_ref, fine_ref, out_ref, sum_buf
):
    owned, samples = inner_ref.shape
    bins = samples // COLS
    per_bin = COLS // LANE

    sum_buf[0 : other_ref.shape[0], :] = other_ref[...]
    rank = rank_ref[...]
    left = []
    for part in range(bins):
        sums = jnp.concatenate(
            [
                chord_rows(sum_buf, offset_ref[0, block], rank)
                for block in range(part * per_bin, (part + 1) * per_bin)
            ],
            axis=1,
        )
        sums = sums + kept_ref[:, part * COLS : (part + 1) * COLS]
        weight = inner_ref[:, part * COLS : (part + 1) * COLS]
        scaled = jnp.where(weight > 0.0, weight * sums, 0.0)
        coarse = scaled.astype(jnp.bfloat16).astype(jnp.float32)
        left.append(jnp.concatenate([coarse, scaled - coarse], axis=0).astype(jnp.bfloat16))
    image = [None] * bins
    for shift in range(1 - bins, bins):
        first, last = max(0, -shift), min(bins, bins - shift)
        stack = jnp.concatenate(left[first:last], axis=0)
        product = jnp.dot(
            stack, coarse_ref[shift + bins - 1], preferred_element_type=jnp.float32
        ) + jnp.dot(stack, fine_ref[shift + bins - 1], preferred_element_type=jnp.float32)
        for place, part in enumerate(range(first, last)):
            base = place * 2 * owned
            term = product[base : base + owned] + product[base + owned : base + 2 * owned]
            to = part + shift
            image[to] = term if image[to] is None else image[to] + term
    for part in range(bins):
        columns = slice(part * COLS, (part + 1) * COLS)
        out_ref[0, :, columns] = image[part] * outer_ref[:, columns]


def invert(other, prepared, owned, samples):
    vmem = pl.BlockSpec(memory_space=pltpu.VMEM)
    return pl.pallas_call(
        invert_kernel,
        out_shape=jax.ShapeDtypeStruct((1, owned, samples), jnp.float32),
        in_specs=[vmem, pl.BlockSpec(memory_space=pltpu.SMEM)] + [vmem] * 6,
        out_specs=vmem,
        scratch_shapes=[pltpu.VMEM((other.shape[0] + owned, LANE), jnp.float32)],
        compiler_params=pltpu.CompilerParams(vmem_limit_bytes=32 << 20),
        name="invert",
    )(other, *prepared)


def add_kernel(starts, *refs):
    *term_refs, out_ref = refs
    count = out_ref.shape[0]
    values = [ref[pl.ds(start, count), :] for ref, start in zip(term_refs, starts)]
    total = values[0]
    for value in values[1:]:
        total = total + value
    out_ref[...] = total


def add_rows(terms, starts, count):
    vmem = pl.BlockSpec(memory_space=pltpu.VMEM)
    return pl.pallas_call(
        lambda *refs: add_kernel(starts, *refs),
        out_shape=pltpu.VMEM((count, LANE), jnp.float32),
        in_specs=[vmem] * len(terms),
        out_specs=vmem,
        compiler_params=pltpu.CompilerParams(vmem_limit_bytes=16 << 20),
        cost_estimate=pl.CostEstimate(
            flops=count * LANE * (len(terms) - 1), bytes_accessed=4 * count * LANE * (len(terms) + 1), transcendentals=0
        ),
        name="add_rows",
    )(*terms)


def per_device(proj, tiles, owner, lengths):
    devices = lax.axis_size("view")
    rows = proj.shape[1]
    samples = tiles.shape[2]
    owned = rows // devices
    packed = rows_per_owner(owned)
    keep, third, second, first = project(proj, tiles, owner, lengths, devices)

    def total(terms, place):
        value, *others = [array[(place - base) * packed : (place - base + 1) * packed] for array, base in terms]
        for other in others:
            value = value + other
        return value

    def apart(terms, place, count):
        return add_rows([array for array, _ in terms], [(place - base) * packed for _, base in terms], count * packed)

    def give(value):
        return lax.ppermute(value, "view", pairs)

    held = devices // 2
    *steps, last_pairs = exchange_pairs(devices)
    terms = [(keep, 0)]
    for pairs in steps:
        if len(terms) > 1:
            held //= 2
            second = apart(sent_next, held + held // 2, held // 2 - 1) if held > 2 else None
            third = apart(sent_next, held, held // 2)
        got_first, got_second, got_third = give(first), None if second is None else give(second), give(third)
        first = total(terms, held - 1) + got_first[:packed]
        sent_next = terms + [(got_second, held // 2)]
        terms = terms + [(got_third, 0)]
    pairs = last_pairs
    other = give(first)
    prepared = prepare(owner, lengths, [array for array, _ in terms], devices, owned, samples)
    return invert(other, prepared, owned, samples)


def solution(mesh):
    placed = (P("view", "chord", None), P("view", None, None), P(), P())
    return jax.shard_map(
        per_device, mesh=mesh, in_specs=placed, out_specs=P("chord", "view", None), check_vma=False
    )
```

```python
import math

import jax
import jax.numpy as jnp
from jax import lax
from jax.experimental import pallas as pl
from jax.experimental.pallas import tpu as pltpu
from jax.sharding import PartitionSpec as P

LANE = 128
OWNED_SAMPLES = 4608
COLS = 256


def side(place):
    return (place ^ (place >> 1) ^ (place >> 2)) & 1


def exchange_pairs(devices):
    steps = [[place ^ 1 for place in range(devices)]]
    for first, second in ((3, 5), (5, 3)):
        steps.append([place ^ (second if side(place) else first) for place in range(devices)])
    step = 8
    while step < devices:
        steps.append([place ^ (step | 1) for place in range(devices)])
        step *= 2
    return [list(enumerate(partners)) for partners in steps]


def slot_of(place, me, devices):
    distance = place ^ me
    steps = devices.bit_length() - 1
    first = distance & 1
    slot = jnp.zeros_like(distance)
    for step in range(1, steps):
        bit = (distance >> step) & 1
        first = first ^ bit
        if step > 2:
            slot = slot | (bit << (steps - 1 - step))
    near, far = (distance >> 1) & 1, (distance >> 2) & 1
    swap = side(me) ^ first
    early = jnp.where(swap == 1, far, near)
    late = jnp.where(swap == 1, near, far)
    return slot | (first << (steps - 1)) | (early << (steps - 2)) | (late << (steps - 3))


def rows_per_owner(owned):
    rows = (OWNED_SAMPLES + owned * (LANE - 1)) // LANE
    return -(-rows // 4) * 4


def tile_pieces(blocks, samples):
    half, head = samples // 2, blocks * 2 // 3
    return [(0, half, 0, blocks), (half, half, 0, head), (half, half, head, blocks - head)]


def project_kernel(
    devices, owner_hbm, lengths_hbm, proj_hbm, tiles_hbm, keep_ref, third_ref, second_ref, first_ref,
    owner_v, lengths_v, offset_v, offset_s, proj_buf, tile_buf, left_buf, sums_buf,
    small_sem, offset_sem, proj_sem, tile_sem,
):
    views, rows, footprint = proj_buf.shape
    samples = tile_buf.shape[2]
    pieces = tile_pieces(tile_buf.shape[0], samples)
    depth = tile_buf.shape[1]
    owned = rows // devices
    group = lax.axis_index("chord")
    me = lax.axis_index("view")
    small = [
        pltpu.make_async_copy(source, kept, small_sem.at[index])
        for index, (source, kept) in enumerate(
            [(owner_hbm, owner_v), (lengths_hbm, lengths_v)]
        )
    ]
    for copy in small:
        copy.start()
    proj_copy = pltpu.make_async_copy(proj_hbm, proj_buf, proj_sem)
    proj_copy.start()
    tile_copies = []
    for index, (start, width, first, count) in enumerate(pieces):
        place = pl.ds(first, count), slice(None), pl.ds(start, width)
        copy = pltpu.make_async_copy(tiles_hbm.at[place], tile_buf.at[place], tile_sem.at[index])
        copy.start()
        tile_copies.append(copy)

    for ref in (keep_ref, third_ref, second_ref, first_ref):
        ref[...] = jnp.zeros_like(ref)
    for copy in small:
        copy.wait()
    down = lax.broadcasted_iota(jnp.int32, (rows, rows), 0)
    across = lax.broadcasted_iota(jnp.int32, (rows, rows), 1)
    diagonal = down == across

    def turned(row):
        spread = jnp.broadcast_to(row.astype(jnp.float32), (rows, rows))
        return jnp.sum(jnp.where(diagonal, spread, 0.0), axis=1, keepdims=True)

    lengths = lengths_v[pl.ds(group, 1), :]
    order = turned(owner_v[pl.ds(group, 1), :])
    hit = order == across.astype(jnp.float32)
    position = jnp.sum(jnp.where(hit, down.astype(jnp.float32), 0.0), axis=0, keepdims=True)
    position = position.astype(jnp.int32)
    place = position // owned
    slot = slot_of(place, me, devices)

    reach = turned((lengths + (LANE - 1)) // LANE)
    block_index = lax.broadcasted_iota(jnp.int32, (rows, LANE), 1).astype(jnp.float32)
    before = jnp.where(block_index < samples // LANE, jnp.minimum(block_index, reach), 0.0)
    member = lax.broadcasted_iota(jnp.int32, (devices, rows), 0) == slot
    offset_v[...] = jnp.dot(
        jnp.where(member, 1.0, 0.0).astype(jnp.bfloat16),
        before.astype(jnp.bfloat16),
        preferred_element_type=jnp.float32,
    ).astype(jnp.int32)
    offset_copy = pltpu.make_async_copy(offset_v, offset_s, offset_sem)
    offset_copy.start()

    key = (slot * (samples + 1) + (samples - lengths)) * owned + (
        position - place * owned
    )
    key = key.astype(jnp.float32)
    target = jnp.sum(jnp.where(turned(key) < key, 1.0, 0.0), axis=0, keepdims=True)
    pick = jnp.where(down.astype(jnp.float32) == target, 1.0, 0.0).astype(jnp.bfloat16)

    def each_slot(body):
        if devices <= 16:
            for index in range(devices):
                body(index)
        else:
            pl.loop(0, devices)(body)

    proj_copy.wait()
    wide = jnp.concatenate([proj_buf[view] for view in range(views)], axis=1)
    left_buf[...] = jnp.dot(pick, wide, preferred_element_type=jnp.float32).astype(jnp.bfloat16)

    packed = rows_per_owner(owned)
    half = devices // 2

    def put(slot_index, offset, value):
        def to(out_ref, index):
            out_ref[pl.ds(index * packed + offset, owned), :] = value

        bounds = [0, half, half + half // 2, devices - 1, devices]
        for low, high, ref in zip(bounds, bounds[1:], (keep_ref, third_ref, second_ref, first_ref)):
            if not isinstance(slot_index, int):
                here = (slot_index >= low) & (slot_index < high)
                pl.when(here)(lambda ref=ref, low=low: to(ref, slot_index - low))
            elif low <= slot_index < high:
                to(ref, slot_index - low)

    def pack(first, last):
        def one(slot_index):
            for block in range(first, last):
                value = sums_buf[pl.ds(slot_index * owned, owned), block * LANE : (block + 1) * LANE]
                put(slot_index, offset_s[slot_index, block] if block else 0, value)

        each_slot(one)

    half_blocks = samples // 2 // LANE
    for index, (start, width, first, count) in enumerate(pieces):
        tile_copies[index].wait()
        right = tile_buf[first : first + count, :, start : start + width].reshape(count * depth, width)
        left = left_buf[:, first * depth : (first + count) * depth]
        sums = jnp.dot(left, right, preferred_element_type=jnp.float32)
        if first:
            sums = sums + sums_buf[:, start : start + width]
        sums_buf[:, start : start + width] = sums
        if index == 1:
            offset_copy.wait()
            pack(1, half_blocks)
    pack(half_blocks, samples // LANE)
    pack(0, 1)


def project(proj, tiles, owner, lengths, devices):
    views, rows, footprint = proj.shape
    blocks, depth, samples = tiles.shape
    owned = rows // devices
    half = devices // 2
    shapes = [
        pltpu.VMEM((-(-(slots * rows_per_owner(owned) + owned) // 8) * 8, LANE), jnp.float32)
        for slots in (half, half // 2, half // 2 - 1, 1)
    ]
    inputs = [pltpu.with_memory_space_constraint(x, pltpu.HBM) for x in (owner, lengths, proj, tiles)]

    def kernel(*refs):
        project_kernel(devices, *refs)

    vmem = pl.BlockSpec(memory_space=pltpu.VMEM)
    hbm = pl.BlockSpec(memory_space=pltpu.HBM)
    return pl.pallas_call(
        kernel,
        out_shape=tuple(shapes),
        in_specs=[hbm] * 4,
        out_specs=(vmem,) * 4,
        scratch_shapes=[
            pltpu.VMEM(owner.shape, jnp.int32),
            pltpu.VMEM(lengths.shape, jnp.int32),
            pltpu.VMEM((devices, LANE), jnp.int32),
            pltpu.SMEM((devices, LANE), jnp.int32),
            pltpu.VMEM(proj.shape, jnp.bfloat16),
            pltpu.VMEM(tiles.shape, jnp.bfloat16),
            pltpu.VMEM((rows, views * footprint), jnp.bfloat16),
            pltpu.VMEM((rows, samples), jnp.float32),
            pltpu.SemaphoreType.DMA((2,)),
            pltpu.SemaphoreType.DMA,
            pltpu.SemaphoreType.DMA,
            pltpu.SemaphoreType.DMA((len(tile_pieces(blocks, samples)),)),
        ],
        compiler_params=pltpu.CompilerParams(vmem_limit_bytes=40 << 20),
        cost_estimate=pl.CostEstimate(
            flops=2 * rows * views * footprint * samples,
            bytes_accessed=2 * (proj.size + tiles.size),
            transcendentals=0,
        ),
        name="project",
    )(*inputs)


def chord_rows(packed_ref, offset, rank):
    ordered = packed_ref[pl.ds(offset, rank.shape[0]), :]
    return jnp.take_along_axis(ordered, rank, axis=0)


def prepare_kernel(
    devices, owner_hbm, lengths_hbm, *refs
):
    *term_refs, offset_ref, rank_ref, kept_ref, inner_ref, outer_ref, coarse_ref, fine_ref, owner_s, lengths_s, sum_buf, sem = refs
    owned, samples = inner_ref.shape
    blocks = samples // LANE
    distances = coarse_ref.shape[0]
    group = lax.axis_index("chord")
    me = lax.axis_index("view")
    copies = [
        pltpu.make_async_copy(owner_hbm, owner_s, sem.at[0]),
        pltpu.make_async_copy(lengths_hbm, lengths_s, sem.at[1]),
    ]
    for copy in copies:
        copy.start()
    across = lax.broadcasted_iota(jnp.int32, (COLS, COLS), 1)
    gap = (across - lax.broadcasted_iota(jnp.int32, (COLS, COLS), 0)).astype(jnp.float32) + 0.5
    for index in range(distances):
        exact = 1.0 / (gap + float((index - distances // 2) * COLS))
        coarse = exact.astype(jnp.bfloat16)
        coarse_ref[index] = coarse
        fine_ref[index] = (exact - coarse.astype(jnp.float32)).astype(jnp.bfloat16)
    for copy in copies:
        copy.wait()
    lengths = [lengths_s[group, owner_s[group, me * owned + index]] for index in range(owned)]

    sub = lax.broadcasted_iota(jnp.int32, (owned, LANE), 0)
    lane = lax.broadcasted_iota(jnp.int32, (owned, LANE), 1)
    length = jnp.zeros((owned, LANE), jnp.int32)
    for index in range(owned):
        length = jnp.where(sub == index, lengths[index], length)
    rank = jnp.zeros((owned, LANE), jnp.int32)
    for index in range(owned):
        ahead = (lengths[index] > length) | ((lengths[index] == length) & (index < sub))
        rank = rank + jnp.where(ahead, 1, 0)
    rank_ref[...] = rank
    packed = rows_per_owner(owned)
    kept = term_refs[0][0:packed, :]
    for ref in term_refs[1:]:
        kept = kept + ref[0:packed, :]
    sum_buf[0:packed, :] = kept
    for block in range(blocks):
        offset = jnp.int32(0)
        for index in range(owned):
            offset = offset + jnp.minimum((lengths[index] + (LANE - 1)) >> 7, block)
        offset_ref[0, block] = offset
        kept_ref[:, block * LANE : (block + 1) * LANE] = chord_rows(sum_buf, offset, rank)

    long = length.astype(jnp.float32)
    for block in range(blocks):
        spot = (lane + block * LANE).astype(jnp.float32) + 0.5
        inside = spot < long
        weight = jnp.sqrt(jnp.where(inside, spot * (long - spot), 1.0))
        columns = slice(block * LANE, (block + 1) * LANE)
        inner_ref[:, columns] = jnp.where(inside, weight, 0.0)
        outer_ref[:, columns] = jnp.where(inside, 1.0 / (math.pi * weight), 0.0)


def prepare(owner, lengths, terms, devices, owned, samples):
    distances = 2 * (samples // COLS) - 1
    inputs = [pltpu.with_memory_space_constraint(x, pltpu.HBM) for x in (owner, lengths)]
    vmem = pl.BlockSpec(memory_space=pltpu.VMEM)

    def kernel(*refs):
        prepare_kernel(devices, *refs)

    return pl.pallas_call(
        kernel,
        out_shape=(
            pltpu.SMEM((1, samples // LANE), jnp.int32),
            pltpu.VMEM((owned, LANE), jnp.int32),
            pltpu.VMEM((owned, samples), jnp.float32),
            pltpu.VMEM((owned, samples), jnp.float32),
            pltpu.VMEM((owned, samples), jnp.float32),
            pltpu.VMEM((distances, COLS, COLS), jnp.bfloat16),
            pltpu.VMEM((distances, COLS, COLS), jnp.bfloat16),
        ),
        in_specs=[pl.BlockSpec(memory_space=pltpu.HBM)] * 2 + [vmem] * len(terms),
        out_specs=(pl.BlockSpec(memory_space=pltpu.SMEM),) + (vmem,) * 6,
        scratch_shapes=[
            pltpu.SMEM(owner.shape, jnp.int32),
            pltpu.SMEM(lengths.shape, jnp.int32),
            pltpu.VMEM((rows_per_owner(owned) + owned, LANE), jnp.float32),
            pltpu.SemaphoreType.DMA((2,)),
        ],
        compiler_params=pltpu.CompilerParams(vmem_limit_bytes=32 << 20),
        cost_estimate=pl.CostEstimate(flops=1 << 22, bytes_accessed=1 << 21, transcendentals=1 << 19),
        name="prepare",
    )(*inputs, *terms)


def invert_kernel(
    other_ref, offset_ref, rank_ref, kept_ref, inner_ref, outer_ref, coarse_ref, fine_ref, out_ref, sum_buf
):
    owned, samples = inner_ref.shape
    bins = samples // COLS
    per_bin = COLS // LANE

    sum_buf[0 : other_ref.shape[0], :] = other_ref[...]
    rank = rank_ref[...]
    left = []
    for part in range(bins):
        sums = jnp.concatenate(
            [
                chord_rows(sum_buf, offset_ref[0, block], rank)
                for block in range(part * per_bin, (part + 1) * per_bin)
            ],
            axis=1,
        )
        sums = sums + kept_ref[:, part * COLS : (part + 1) * COLS]
        weight = inner_ref[:, part * COLS : (part + 1) * COLS]
        scaled = jnp.where(weight > 0.0, weight * sums, 0.0)
        coarse = scaled.astype(jnp.bfloat16).astype(jnp.float32)
        left.append(jnp.concatenate([coarse, scaled - coarse], axis=0).astype(jnp.bfloat16))
    image = [None] * bins
    for shift in range(1 - bins, bins):
        first, last = max(0, -shift), min(bins, bins - shift)
        stack = jnp.concatenate(left[first:last], axis=0)
        product = jnp.dot(
            stack, coarse_ref[shift + bins - 1], preferred_element_type=jnp.float32
        ) + jnp.dot(stack, fine_ref[shift + bins - 1], preferred_element_type=jnp.float32)
        for place, part in enumerate(range(first, last)):
            base = place * 2 * owned
            term = product[base : base + owned] + product[base + owned : base + 2 * owned]
            to = part + shift
            image[to] = term if image[to] is None else image[to] + term
    for part in range(bins):
        columns = slice(part * COLS, (part + 1) * COLS)
        out_ref[0, :, columns] = image[part] * outer_ref[:, columns]


def invert(other, prepared, owned, samples):
    vmem = pl.BlockSpec(memory_space=pltpu.VMEM)
    return pl.pallas_call(
        invert_kernel,
        out_shape=jax.ShapeDtypeStruct((1, owned, samples), jnp.float32),
        in_specs=[vmem, pl.BlockSpec(memory_space=pltpu.SMEM)] + [vmem] * 6,
        out_specs=vmem,
        scratch_shapes=[pltpu.VMEM((other.shape[0] + owned, LANE), jnp.float32)],
        compiler_params=pltpu.CompilerParams(vmem_limit_bytes=32 << 20),
        name="invert",
    )(other, *prepared)


def add_kernel(starts, *refs):
    *term_refs, out_ref = refs
    count = out_ref.shape[0]
    values = [ref[pl.ds(start, count), :] for ref, start in zip(term_refs, starts)]
    total = values[0]
    for value in values[1:]:
        total = total + value
    out_ref[...] = total


def add_rows(terms, starts, count):
    vmem = pl.BlockSpec(memory_space=pltpu.VMEM)
    return pl.pallas_call(
        lambda *refs: add_kernel(starts, *refs),
        out_shape=pltpu.VMEM((count, LANE), jnp.float32),
        in_specs=[vmem] * len(terms),
        out_specs=vmem,
        compiler_params=pltpu.CompilerParams(vmem_limit_bytes=16 << 20),
        cost_estimate=pl.CostEstimate(
            flops=count * LANE * (len(terms) - 1), bytes_accessed=4 * count * LANE * (len(terms) + 1), transcendentals=0
        ),
        name="add_rows",
    )(*terms)


def per_device(proj, tiles, owner, lengths):
    devices = lax.axis_size("view")
    rows = proj.shape[1]
    samples = tiles.shape[2]
    owned = rows // devices
    packed = rows_per_owner(owned)
    keep, third, second, first = project(proj, tiles, owner, lengths, devices)

    def total(terms, place):
        value, *others = [array[(place - base) * packed : (place - base + 1) * packed] for array, base in terms]
        for other in others:
            value = value + other
        return value

    def apart(terms, place, count):
        return add_rows([array for array, _ in terms], [(place - base) * packed for _, base in terms], count * packed)

    def give(value):
        return lax.ppermute(value, "view", pairs)

    held = devices // 2
    *steps, last_pairs = exchange_pairs(devices)
    terms = [(keep, 0)]
    for pairs in steps:
        if len(terms) > 1:
            held //= 2
            second = apart(sent_next, held + held // 2, held // 2 - 1) if held > 2 else None
            third = apart(sent_next, held, held // 2)
        got_first, got_second, got_third = give(first), None if second is None else give(second), give(third)
        first = total(terms, held - 1) + got_first[:packed]
        sent_next = terms + [(got_second, held // 2)]
        terms = terms + [(got_third, 0)]
    pairs = last_pairs
    other = give(first)
    prepared = prepare(owner, lengths, [array for array, _ in terms], devices, owned, samples)
    return invert(other, prepared, owned, samples)


def solution(mesh):
    placed = (P("view", "chord", None), P("view", None, None), P(), P())
    return jax.shard_map(
        per_device, mesh=mesh, in_specs=placed, out_specs=P("chord", "view", None), check_vma=False
    )
```

```python
import math

import jax
import jax.numpy as jnp
from jax import lax
from jax.experimental import pallas as pl
from jax.experimental.pallas import tpu as pltpu
from jax.sharding import PartitionSpec as P

LANE = 128
OWNED_SAMPLES = 4608
COLS = 256


def side(place):
    return (place ^ (place >> 1) ^ (place >> 2)) & 1


def exchange_pairs(devices):
    steps = [[place ^ 1 for place in range(devices)]]
    for first, second in ((3, 5), (5, 3)):
        steps.append([place ^ (second if side(place) else first) for place in range(devices)])
    step = 8
    while step < devices:
        steps.append([place ^ (step | 1) for place in range(devices)])
        step *= 2
    return [list(enumerate(partners)) for partners in steps]


def slot_of(place, me, devices):
    distance = place ^ me
    steps = devices.bit_length() - 1
    first = distance & 1
    slot = jnp.zeros_like(distance)
    for step in range(1, steps):
        bit = (distance >> step) & 1
        first = first ^ bit
        if step > 2:
            slot = slot | (bit << (steps - 1 - step))
    near, far = (distance >> 1) & 1, (distance >> 2) & 1
    swap = side(me) ^ first
    early = jnp.where(swap == 1, far, near)
    late = jnp.where(swap == 1, near, far)
    return slot | (first << (steps - 1)) | (early << (steps - 2)) | (late << (steps - 3))


def rows_per_owner(owned):
    rows = (OWNED_SAMPLES + owned * (LANE - 1)) // LANE
    return -(-rows // 4) * 4


def tile_pieces(blocks, samples):
    half, head = samples // 2, blocks * 2 // 3
    return [(0, half, 0, blocks), (half, half, 0, head), (half, half, head, blocks - head)]


def project_kernel(
    devices, owner_hbm, lengths_hbm, proj_hbm, tiles_hbm, keep_ref, third_ref, second_ref, first_ref,
    owner_v, lengths_v, offset_v, offset_s, proj_buf, tile_buf, left_buf, sums_buf,
    small_sem, offset_sem, proj_sem, tile_sem,
):
    views, rows, footprint = proj_buf.shape
    samples = tile_buf.shape[2]
    pieces = tile_pieces(tile_buf.shape[0], samples)
    depth = tile_buf.shape[1]
    owned = rows // devices
    group = lax.axis_index("chord")
    me = lax.axis_index("view")
    small = [
        pltpu.make_async_copy(source, kept, small_sem.at[index])
        for index, (source, kept) in enumerate(
            [(owner_hbm, owner_v), (lengths_hbm, lengths_v)]
        )
    ]
    for copy in small:
        copy.start()
    proj_copy = pltpu.make_async_copy(proj_hbm, proj_buf, proj_sem)
    proj_copy.start()
    tile_copies = []
    for index, (start, width, first, count) in enumerate(pieces):
        place = pl.ds(first, count), slice(None), pl.ds(start, width)
        copy = pltpu.make_async_copy(tiles_hbm.at[place], tile_buf.at[place], tile_sem.at[index])
        copy.start()
        tile_copies.append(copy)

    for copy in small:
        copy.wait()
    down = lax.broadcasted_iota(jnp.int32, (rows, rows), 0)
    across = lax.broadcasted_iota(jnp.int32, (rows, rows), 1)
    diagonal = down == across

    def turned(row):
        spread = jnp.broadcast_to(row.astype(jnp.float32), (rows, rows))
        return jnp.sum(jnp.where(diagonal, spread, 0.0), axis=1, keepdims=True)

    lengths = lengths_v[pl.ds(group, 1), :]
    order = turned(owner_v[pl.ds(group, 1), :])
    hit = order == across.astype(jnp.float32)
    position = jnp.sum(jnp.where(hit, down.astype(jnp.float32), 0.0), axis=0, keepdims=True)
    position = position.astype(jnp.int32)
    place = position // owned
    slot = slot_of(place, me, devices)

    reach = turned((lengths + (LANE - 1)) // LANE)
    block_index = lax.broadcasted_iota(jnp.int32, (rows, LANE), 1).astype(jnp.float32)
    before = jnp.where(block_index < samples // LANE, jnp.minimum(block_index, reach), 0.0)
    member = lax.broadcasted_iota(jnp.int32, (devices, rows), 0) == slot
    offset_v[...] = jnp.dot(
        jnp.where(member, 1.0, 0.0).astype(jnp.bfloat16),
        before.astype(jnp.bfloat16),
        preferred_element_type=jnp.float32,
    ).astype(jnp.int32)
    offset_copy = pltpu.make_async_copy(offset_v, offset_s, offset_sem)
    offset_copy.start()

    key = (slot * (samples + 1) + (samples - lengths)) * owned + (
        position - place * owned
    )
    key = key.astype(jnp.float32)
    target = jnp.sum(jnp.where(turned(key) < key, 1.0, 0.0), axis=0, keepdims=True)
    pick = jnp.where(down.astype(jnp.float32) == target, 1.0, 0.0).astype(jnp.bfloat16)

    def each_slot(body):
        if devices <= 16:
            for index in range(devices):
                body(index)
        else:
            pl.loop(0, devices)(body)

    proj_copy.wait()
    wide = jnp.concatenate([proj_buf[view] for view in range(views)], axis=1)
    left_buf[...] = jnp.dot(pick, wide, preferred_element_type=jnp.float32).astype(jnp.bfloat16)

    packed = rows_per_owner(owned)
    half = devices // 2

    def put(slot_index, offset, value):
        def to(out_ref, index):
            out_ref[pl.ds(index * packed + offset, owned), :] = value

        bounds = [0, half, half + half // 2, devices - 1, devices]
        for low, high, ref in zip(bounds, bounds[1:], (keep_ref, third_ref, second_ref, first_ref)):
            if not isinstance(slot_index, int):
                here = (slot_index >= low) & (slot_index < high)
                pl.when(here)(lambda ref=ref, low=low: to(ref, slot_index - low))
            elif low <= slot_index < high:
                to(ref, slot_index - low)

    def pack(first, last):
        def one(slot_index):
            for block in range(first, last):
                value = sums_buf[pl.ds(slot_index * owned, owned), block * LANE : (block + 1) * LANE]
                put(slot_index, offset_s[slot_index, block] if block else 0, value)

        each_slot(one)

    half_blocks = samples // 2 // LANE
    for index, (start, width, first, count) in enumerate(pieces):
        tile_copies[index].wait()
        right = tile_buf[first : first + count, :, start : start + width].reshape(count * depth, width)
        left = left_buf[:, first * depth : (first + count) * depth]
        sums = jnp.dot(left, right, preferred_element_type=jnp.float32)
        if first:
            sums = sums + sums_buf[:, start : start + width]
        sums_buf[:, start : start + width] = sums
        if index == 1:
            offset_copy.wait()
            pack(1, half_blocks)
    pack(half_blocks, samples // LANE)
    pack(0, 1)


def project(proj, tiles, owner, lengths, devices):
    views, rows, footprint = proj.shape
    blocks, depth, samples = tiles.shape
    owned = rows // devices
    half = devices // 2
    shapes = [
        pltpu.VMEM((-(-(slots * rows_per_owner(owned) + owned) // 8) * 8, LANE), jnp.float32)
        for slots in (half, half // 2, half // 2 - 1, 1)
    ]
    inputs = [pltpu.with_memory_space_constraint(x, pltpu.HBM) for x in (owner, lengths, proj, tiles)]

    def kernel(*refs):
        project_kernel(devices, *refs)

    vmem = pl.BlockSpec(memory_space=pltpu.VMEM)
    hbm = pl.BlockSpec(memory_space=pltpu.HBM)
    return pl.pallas_call(
        kernel,
        out_shape=tuple(shapes),
        in_specs=[hbm] * 4,
        out_specs=(vmem,) * 4,
        scratch_shapes=[
            pltpu.VMEM(owner.shape, jnp.int32),
            pltpu.VMEM(lengths.shape, jnp.int32),
            pltpu.VMEM((devices, LANE), jnp.int32),
            pltpu.SMEM((devices, LANE), jnp.int32),
            pltpu.VMEM(proj.shape, jnp.bfloat16),
            pltpu.VMEM(tiles.shape, jnp.bfloat16),
            pltpu.VMEM((rows, views * footprint), jnp.bfloat16),
            pltpu.VMEM((rows, samples), jnp.float32),
            pltpu.SemaphoreType.DMA((2,)),
            pltpu.SemaphoreType.DMA,
            pltpu.SemaphoreType.DMA,
            pltpu.SemaphoreType.DMA((len(tile_pieces(blocks, samples)),)),
        ],
        compiler_params=pltpu.CompilerParams(vmem_limit_bytes=40 << 20),
        cost_estimate=pl.CostEstimate(
            flops=2 * rows * views * footprint * samples,
            bytes_accessed=2 * (proj.size + tiles.size),
            transcendentals=0,
        ),
        name="project",
    )(*inputs)


def chord_rows(packed_ref, offset, rank):
    ordered = packed_ref[pl.ds(offset, rank.shape[0]), :]
    return jnp.take_along_axis(ordered, rank, axis=0)


def prepare_kernel(
    devices, owner_hbm, lengths_hbm, *refs
):
    *term_refs, offset_ref, rank_ref, kept_ref, inner_ref, outer_ref, coarse_ref, fine_ref, owner_s, lengths_s, sum_buf, sem = refs
    owned, samples = inner_ref.shape
    blocks = samples // LANE
    distances = coarse_ref.shape[0]
    group = lax.axis_index("chord")
    me = lax.axis_index("view")
    copies = [
        pltpu.make_async_copy(owner_hbm, owner_s, sem.at[0]),
        pltpu.make_async_copy(lengths_hbm, lengths_s, sem.at[1]),
    ]
    for copy in copies:
        copy.start()
    across = lax.broadcasted_iota(jnp.int32, (COLS, COLS), 1)
    gap = (across - lax.broadcasted_iota(jnp.int32, (COLS, COLS), 0)).astype(jnp.float32) + 0.5
    for index in range(distances):
        exact = 1.0 / (gap + float((index - distances // 2) * COLS))
        coarse = exact.astype(jnp.bfloat16)
        coarse_ref[index] = coarse
        fine_ref[index] = (exact - coarse.astype(jnp.float32)).astype(jnp.bfloat16)
    for copy in copies:
        copy.wait()
    lengths = [lengths_s[group, owner_s[group, me * owned + index]] for index in range(owned)]

    sub = lax.broadcasted_iota(jnp.int32, (owned, LANE), 0)
    lane = lax.broadcasted_iota(jnp.int32, (owned, LANE), 1)
    length = jnp.zeros((owned, LANE), jnp.int32)
    for index in range(owned):
        length = jnp.where(sub == index, lengths[index], length)
    rank = jnp.zeros((owned, LANE), jnp.int32)
    for index in range(owned):
        ahead = (lengths[index] > length) | ((lengths[index] == length) & (index < sub))
        rank = rank + jnp.where(ahead, 1, 0)
    rank_ref[...] = rank
    packed = rows_per_owner(owned)
    kept = term_refs[0][0:packed, :]
    for ref in term_refs[1:]:
        kept = kept + ref[0:packed, :]
    sum_buf[0:packed, :] = kept
    for block in range(blocks):
        offset = jnp.int32(0)
        for index in range(owned):
            offset = offset + jnp.minimum((lengths[index] + (LANE - 1)) >> 7, block)
        offset_ref[0, block] = offset
        kept_ref[:, block * LANE : (block + 1) * LANE] = chord_rows(sum_buf, offset, rank)

    long = length.astype(jnp.float32)
    for block in range(blocks):
        spot = (lane + block * LANE).astype(jnp.float32) + 0.5
        inside = spot < long
        weight = jnp.sqrt(jnp.where(inside, spot * (long - spot), 1.0))
        columns = slice(block * LANE, (block + 1) * LANE)
        inner_ref[:, columns] = jnp.where(inside, weight, 0.0)
        outer_ref[:, columns] = jnp.where(inside, 1.0 / (math.pi * weight), 0.0)


def prepare(owner, lengths, terms, devices, owned, samples):
    distances = 2 * (samples // COLS) - 1
    inputs = [pltpu.with_memory_space_constraint(x, pltpu.HBM) for x in (owner, lengths)]
    vmem = pl.BlockSpec(memory_space=pltpu.VMEM)

    def kernel(*refs):
        prepare_kernel(devices, *refs)

    return pl.pallas_call(
        kernel,
        out_shape=(
            pltpu.SMEM((1, samples // LANE), jnp.int32),
            pltpu.VMEM((owned, LANE), jnp.int32),
            pltpu.VMEM((owned, samples), jnp.float32),
            pltpu.VMEM((owned, samples), jnp.float32),
            pltpu.VMEM((owned, samples), jnp.float32),
            pltpu.VMEM((distances, COLS, COLS), jnp.bfloat16),
            pltpu.VMEM((distances, COLS, COLS), jnp.bfloat16),
        ),
        in_specs=[pl.BlockSpec(memory_space=pltpu.HBM)] * 2 + [vmem] * len(terms),
        out_specs=(pl.BlockSpec(memory_space=pltpu.SMEM),) + (vmem,) * 6,
        scratch_shapes=[
            pltpu.SMEM(owner.shape, jnp.int32),
            pltpu.SMEM(lengths.shape, jnp.int32),
            pltpu.VMEM((rows_per_owner(owned) + owned, LANE), jnp.float32),
            pltpu.SemaphoreType.DMA((2,)),
        ],
        compiler_params=pltpu.CompilerParams(vmem_limit_bytes=32 << 20),
        cost_estimate=pl.CostEstimate(flops=1 << 22, bytes_accessed=1 << 21, transcendentals=1 << 19),
        name="prepare",
    )(*inputs, *terms)


def invert_kernel(
    other_ref, offset_ref, rank_ref, kept_ref, inner_ref, outer_ref, coarse_ref, fine_ref, out_ref, sum_buf
):
    owned, samples = inner_ref.shape
    bins = samples // COLS
    per_bin = COLS // LANE

    sum_buf[0 : other_ref.shape[0], :] = other_ref[...]
    rank = rank_ref[...]
    left = []
    for part in range(bins):
        sums = jnp.concatenate(
            [
                chord_rows(sum_buf, offset_ref[0, block], rank)
                for block in range(part * per_bin, (part + 1) * per_bin)
            ],
            axis=1,
        )
        sums = sums + kept_ref[:, part * COLS : (part + 1) * COLS]
        weight = inner_ref[:, part * COLS : (part + 1) * COLS]
        scaled = jnp.where(weight > 0.0, weight * sums, 0.0)
        coarse = scaled.astype(jnp.bfloat16).astype(jnp.float32)
        left.append(jnp.concatenate([coarse, scaled - coarse], axis=0).astype(jnp.bfloat16))
    image = [None] * bins
    for shift in range(1 - bins, bins):
        first, last = max(0, -shift), min(bins, bins - shift)
        stack = jnp.concatenate(left[first:last], axis=0)
        product = jnp.dot(
            stack, coarse_ref[shift + bins - 1], preferred_element_type=jnp.float32
        ) + jnp.dot(stack, fine_ref[shift + bins - 1], preferred_element_type=jnp.float32)
        for place, part in enumerate(range(first, last)):
            base = place * 2 * owned
            term = product[base : base + owned] + product[base + owned : base + 2 * owned]
            to = part + shift
            image[to] = term if image[to] is None else image[to] + term
    for part in range(bins):
        columns = slice(part * COLS, (part + 1) * COLS)
        out_ref[0, :, columns] = image[part] * outer_ref[:, columns]


def invert(other, prepared, owned, samples):
    vmem = pl.BlockSpec(memory_space=pltpu.VMEM)
    return pl.pallas_call(
        invert_kernel,
        out_shape=jax.ShapeDtypeStruct((1, owned, samples), jnp.float32),
        in_specs=[vmem, pl.BlockSpec(memory_space=pltpu.SMEM)] + [vmem] * 6,
        out_specs=vmem,
        scratch_shapes=[pltpu.VMEM((other.shape[0] + owned, LANE), jnp.float32)],
        compiler_params=pltpu.CompilerParams(vmem_limit_bytes=32 << 20),
        name="invert",
    )(other, *prepared)


def add_kernel(starts, *refs):
    *term_refs, out_ref = refs
    count = out_ref.shape[0]
    values = [ref[pl.ds(start, count), :] for ref, start in zip(term_refs, starts)]
    total = values[0]
    for value in values[1:]:
        total = total + value
    out_ref[...] = total


def add_rows(terms, starts, count):
    vmem = pl.BlockSpec(memory_space=pltpu.VMEM)
    return pl.pallas_call(
        lambda *refs: add_kernel(starts, *refs),
        out_shape=pltpu.VMEM((count, LANE), jnp.float32),
        in_specs=[vmem] * len(terms),
        out_specs=vmem,
        compiler_params=pltpu.CompilerParams(vmem_limit_bytes=16 << 20),
        cost_estimate=pl.CostEstimate(
            flops=count * LANE * (len(terms) - 1), bytes_accessed=4 * count * LANE * (len(terms) + 1), transcendentals=0
        ),
        name="add_rows",
    )(*terms)


def per_device(proj, tiles, owner, lengths):
    devices = lax.axis_size("view")
    rows = proj.shape[1]
    samples = tiles.shape[2]
    owned = rows // devices
    packed = rows_per_owner(owned)
    keep, third, second, first = project(proj, tiles, owner, lengths, devices)

    def total(terms, place):
        value, *others = [array[(place - base) * packed : (place - base + 1) * packed] for array, base in terms]
        for other in others:
            value = value + other
        return value

    def apart(terms, place, count):
        return add_rows([array for array, _ in terms], [(place - base) * packed for _, base in terms], count * packed)

    def give(value):
        return lax.ppermute(value, "view", pairs)

    held = devices // 2
    *steps, last_pairs = exchange_pairs(devices)
    terms = [(keep, 0)]
    for pairs in steps:
        if len(terms) > 1:
            held //= 2
            second = apart(sent_next, held + held // 2, held // 2 - 1) if held > 2 else None
            third = apart(sent_next, held, held // 2)
        got_first, got_second, got_third = give(first), None if second is None else give(second), give(third)
        first = total(terms, held - 1) + got_first[:packed]
        sent_next = terms + [(got_second, held // 2)]
        terms = terms + [(got_third, 0)]
    pairs = last_pairs
    other = give(first)
    prepared = prepare(owner, lengths, [array for array, _ in terms], devices, owned, samples)
    return invert(other, prepared, owned, samples)


def solution(mesh):
    placed = (P("view", "chord", None), P("view", None, None), P(), P())
    return jax.shard_map(
        per_device, mesh=mesh, in_specs=placed, out_specs=P("chord", "view", None), check_vma=False
    )
```
